32 devices in a mesh: tm: 16 (over z, y, x), rows: 2 (over core).
Axes of the slice: x: 2, y: 2, z: 4, core: 2. Of those that a mesh axis runs over, the one named last changes fastest.
Arguments:
- frames: bfloat16 [2, 32768, 512], P('rows', 'tm'), may hold values from -6 to 6
- utt_lengths: int32 [2, 128], P('rows'), may hold values from 1 to 64, 2048 in all within a row
- w_qkv: bfloat16 [512, 1536], replicated, may hold values from -0.25 to 0.25
- w_out: bfloat16 [512, 512], replicated, may hold values from -1.5 to 1.5
- w_up: bfloat16 [512, 2048], replicated, may hold values from -0.25 to 0.25
- w_down: bfloat16 [2048, 512], replicated, may hold values from -0.125 to 0.125
- gain_attn: float32 [512], replicated, may hold values from 0.1 to 1.9
- bias_attn: float32 [512], replicated, may hold values from -2.5 to 2.5
- gain_ffn: float32 [512], replicated, may hold values from 0.1 to 1.9
- bias_ffn: float32 [512], replicated, may hold values from -2.5 to 2.5
- out_grad: bfloat16 [2, 32768, 512], P('rows', 'tm'), may hold values from -6 to 6
Outputs:
- out_frames: bfloat16 [2, 32768, 512], P('rows', 'tm')
- grad_frames: float32 [2, 32768, 512], P('rows', 'tm')
- grad_qkv: float32 [512, 1536], replicated
- grad_out_w: float32 [512, 512], replicated
- grad_up: float32 [512, 2048], replicated
- grad_down: float32 [2048, 512], replicated
- grad_gain_attn: float32 [512], replicated
- grad_bias_attn: float32 [512], replicated
- grad_gain_ffn: float32 [512], replicated
- grad_bias_ffn: float32 [512], replicated
The draws below stay inside these ranges and needn't reach their ends.
Inputs may be any that keep to these rules, and one draw needn't show every extreme that they name: `utt_lengths`: each row's lengths sum to 2048 and the largest is 64.
All inputs are finite; a program needn't handle non-finite values.
Results may differ from the reference program's by a relative error of at most 0.012.
Values may be sent and summed in bfloat16 or wider, within the bound.
A program may use at most 192 MiB of HBM per device.

```python
import math
import jax
import jax.numpy as jnp
import numpy as np
from jax import lax

D = 512
HEADS = 8
HEAD_DIM = 64
FF = 2048
SEG = 16
MOST = 64
FRAMES = 32768
BATCH = 2
NSEG_ROW = 2048
NUTT = 128


def level_of(own_key, dims, shards, low, largest):
    def one(dim, parts):
        steps = jax.random.uniform(jax.random.fold_in(jax.random.fold_in(own_key, 6), dim), (parts,), jnp.float32, low / len(shards), largest / len(shards))
        return jnp.repeat(jnp.exp(steps), dims[dim] // parts).reshape((-1,) + (1,) * (len(dims) - dim - 1))

    gain = one(*shards[0])
    for cut in shards[1:]:
        gain = gain * one(*cut)
    return gain


def profile(number_of, total, reach, skew):
    loads = [(1 << 20) // math.isqrt(standing ** skew) + 1 for standing in range(2, number_of + 1)]
    spare, holding = total - reach - (number_of - 1), [1] * (number_of - 1)
    while spare > 0:
        free = [i for i in range(number_of - 1) if holding[i] < reach]
        whole, budget = sum([loads[i] for i in free]), spare
        for i in free:
            extra = min(reach - holding[i], max(1, budget * loads[i] // whole), spare)
            holding[i] = holding[i] + extra
            spare = spare - extra
    return np.array([reach] + holding)


def ragged(stream_key, amount, total, reach, slope):
    if amount == 2:
        one = jax.random.randint(stream_key, (), max(1, total - reach), min(reach, total - 1) + 1)
        return jnp.stack([one, total - one])
    tallies = jnp.asarray(profile(amount, total, reach, slope), jnp.int32)
    couples = (amount - 1) // 2
    source_of, taker = tallies[1:1 + 2 * couples:2], tallies[2:2 + 2 * couples:2]
    margin = jnp.minimum(source_of - 1, reach - taker)
    passed = jax.random.randint(jax.random.fold_in(stream_key, 1), (couples,), 0, 1 << 20) % (margin + 1)
    tallies = tallies.at[1:1 + 2 * couples:2].set(source_of - passed).at[2:2 + 2 * couples:2].set(taker + passed)
    return tallies[jax.random.permutation(jax.random.fold_in(stream_key, 2), amount)]


def normal_values(key, extent, width, bound, pieces=(), kind=jnp.bfloat16):
    entries = jax.random.normal(key, extent, jnp.float32) * width
    if len(pieces) > 0:
        entries = level_of(key, extent, pieces, -0.22, 0.18) * entries
    return jnp.clip(entries, min=-bound, max=bound).astype(kind)


def setup_inputs(seed: int = 0) -> dict:
    seeds = jax.random.split(jax.random.key(seed), 12)
    frames = normal_values(seeds[0], (BATCH, FRAMES, D), 1.0, 6.0, ((0, 2), (1, 16)))
    utt_lengths = jax.vmap(lambda own: ragged(own, NUTT, NSEG_ROW, MOST, 2))(jax.random.split(seeds[1], BATCH)).reshape((BATCH, NUTT)).astype(jnp.int32)
    w_qkv = normal_values(seeds[2], (D, 3 * D), D ** -0.5, 0.25)
    w_out = normal_values(seeds[3], (D, D), (D // 32) ** -0.5, 1.5)
    w_up = normal_values(seeds[4], (D, FF), D ** -0.5, 0.25)
    w_down = normal_values(seeds[5], (FF, D), FF ** -0.5, 0.125)
    gain_attn = jnp.clip(1.0 + 0.18 * jax.random.normal(seeds[6], (D,), jnp.float32), 0.1, 1.9)
    bias_attn = normal_values(seeds[7], (D,), 0.5, 2.5, (), jnp.float32)
    gain_ffn = jnp.clip(1.0 + 0.18 * jax.random.normal(seeds[8], (D,), jnp.float32), 0.1, 1.9)
    bias_ffn = normal_values(seeds[9], (D,), 0.5, 2.5, (), jnp.float32)
    out_grad = normal_values(seeds[10], (BATCH, FRAMES, D), 1.0, 6.0, ((0, 2), (1, 16)))
    return dict(frames=frames, utt_lengths=utt_lengths, w_qkv=w_qkv, w_out=w_out, w_up=w_up, w_down=w_down, gain_attn=gain_attn, bias_attn=bias_attn, gain_ffn=gain_ffn, bias_ffn=bias_ffn, out_grad=out_grad)


@jax.custom_vjp
def low(v):
    return lax.optimization_barrier(v.astype(jnp.bfloat16)).astype(jnp.float32)

@jax.custom_vjp
def low_back(v):
    return v

def low_keep(v):
    return (low(v), None)

def low_pass(kept, grad):
    return (grad,)

def back_keep(v):
    return (v, None)

def back_low(kept, grad):
    return (low(grad),)
low.defvjp(low_keep, low_pass)
low_back.defvjp(back_keep, back_low)
EPS = 1e-05

def layer_norm(values, gain_vec, shift_vec):
    row_mean = lax.optimization_barrier(jnp.mean(values, axis=-1, keepdims=True))
    centred = values - row_mean
    row_var = lax.optimization_barrier(jnp.mean(centred * centred, axis=-1, keepdims=True))
    return centred * lax.rsqrt(row_var + EPS) * gain_vec + shift_vec

def gelu_exact(values):
    return jax.nn.gelu(values, approximate=False)

def matmul(first_op, second_op):
    return jnp.dot(first_op, second_op, precision=lax.Precision.HIGHEST, preferred_element_type=jnp.float32)

def attend_mask(seg_ids, groups):
    id_blocks = seg_ids.reshape(groups + 2, 4)
    query_ids = id_blocks[1:groups + 1]
    key_ids = jnp.concatenate([id_blocks[:groups], id_blocks[1:groups + 1], id_blocks[2:]], 1)[:, 2:10]
    memory_ids = jnp.concatenate([id_blocks[:groups], id_blocks[1:groups + 1]], 1)
    query_rows = jnp.repeat(query_ids, 16, axis=1)
    key_rows = jnp.repeat(key_ids, 16, axis=1)[:, :120]
    query_seg = lax.broadcasted_iota(jnp.int32, (64, 120), 0) // 16
    key_pos = lax.broadcasted_iota(jnp.int32, (64, 120), 1)
    near_ok = (key_pos >= 16 * query_seg + 2) & (key_pos < 16 * query_seg + 52)
    slot_seg = lax.broadcasted_iota(jnp.int32, (64, 8), 0) // 16
    slot_pos = lax.broadcasted_iota(jnp.int32, (64, 8), 1)
    recent_ok = (slot_pos >= slot_seg) & (slot_pos <= slot_seg + 3)
    memory_ok = recent_ok[None] & (query_rows[:, :, None] == memory_ids[:, None, :])
    frame_ok = near_ok[None] & (query_rows[:, :, None] == key_rows[:, None, :])
    return jnp.concatenate([memory_ok, frame_ok], 2)

def group_attention(part_q, part_kv, part_mem, part_ids, groups):
    frame_blocks = part_kv.reshape(groups + 1, 64, 2 * D)
    frame_window = jnp.concatenate([frame_blocks[:groups], frame_blocks[1:, :56]], 1)
    memory_blocks = part_mem.reshape(groups + 1, 4, 2 * D)
    memory_window = jnp.concatenate([memory_blocks[:groups], memory_blocks[1:]], 1)
    key_window = jnp.concatenate([memory_window, frame_window], 1)
    key_heads = key_window[:, :, :D].reshape(groups, 128, HEADS, HEAD_DIM)
    value_heads = key_window[:, :, D:].reshape(groups, 128, HEADS, HEAD_DIM)
    query_heads = part_q.reshape(groups, 64, HEADS, HEAD_DIM)
    scores = jnp.einsum('gqhe,gkhe->ghqk', query_heads, key_heads, precision=lax.Precision.HIGHEST) * HEAD_DIM ** (-0.5)
    scores = low_back(scores)
    allowed = attend_mask(part_ids, groups)
    scores = jnp.where(allowed[:, None], scores, -1e+30)
    top_score = lax.optimization_barrier(jnp.max(scores, axis=-1, keepdims=True))
    shifted = jnp.exp(scores - top_score)
    probs_all = low(shifted / lax.optimization_barrier(jnp.sum(shifted, axis=-1, keepdims=True)))
    mixed = jnp.einsum('ghqk,gkhe->gqhe', probs_all, value_heads, precision=lax.Precision.HIGHEST)
    return mixed.reshape(groups * 64, D)

def row_attention(queries, keyvals, memory_kv, seg_ids):
    frame_total = queries.shape[0]
    span_len = math.gcd(frame_total, 4096)
    groups = span_len // 64
    pad_kv = jnp.concatenate([jnp.zeros((32, 2 * D), jnp.float32), keyvals, jnp.zeros((32, 2 * D), jnp.float32)], 0)
    pad_mem = jnp.concatenate([jnp.zeros((4, 2 * D), jnp.float32), memory_kv], 0)
    minus_ones = jnp.full((4,), -1, jnp.int32)
    pad_ids = jnp.concatenate([minus_ones, seg_ids, minus_ones], 0).astype(jnp.int32)

    def one_span(span_index):
        span_start = (span_index * span_len).astype(jnp.int32)
        seg_start = (span_index * (span_len // 16)).astype(jnp.int32)
        part_q = lax.dynamic_slice_in_dim(queries, span_start, span_len, 0)
        part_kv = lax.dynamic_slice_in_dim(pad_kv, span_start, span_len + 64, 0)
        part_mem = lax.dynamic_slice_in_dim(pad_mem, seg_start, span_len // 16 + 4, 0)
        part_ids = lax.dynamic_slice_in_dim(pad_ids, seg_start, span_len // 16 + 8, 0)
        return group_attention(part_q, part_kv, part_mem, part_ids, groups)
    outputs = lax.map(jax.checkpoint(one_span), jnp.arange(frame_total // span_len, dtype=jnp.int32))
    return outputs.reshape(frame_total, D)

def utterance_ids(utt_lengths):
    starts = (jnp.cumsum(utt_lengths, axis=1) - utt_lengths).astype(jnp.int32)
    seg_numbers = lax.iota(jnp.int32, NSEG_ROW)
    hits = (starts[:, None, :] <= seg_numbers[None, :, None]).astype(jnp.int32)
    return (lax.optimization_barrier(jnp.sum(hits, axis=2)) - 1).astype(jnp.int32)

def forward(frames32, w_qkv, w_out, w_up, w_down, gain_attn, bias_attn, gain_ffn, bias_ffn, seg_ids):
    normed = low(layer_norm(frames32, gain_attn, bias_attn))
    projected = low_back(low(matmul(normed.reshape(BATCH * FRAMES, D), w_qkv))).reshape(BATCH, FRAMES, 3 * D)
    summary = low(lax.optimization_barrier(jnp.mean(normed.reshape(BATCH, NSEG_ROW, SEG, D), axis=2)))
    memory_kv = low_back(low(matmul(summary.reshape(BATCH * NSEG_ROW, D), w_qkv[:, D:]))).reshape(BATCH, NSEG_ROW, 2 * D)
    rows_out = [row_attention(projected[row_index, :, :D], projected[row_index, :, D:], memory_kv[row_index], seg_ids[row_index]) for row_index in range(BATCH)]
    attended = low_back(low(jnp.stack(rows_out, 0)))
    branch = low_back(matmul(attended.reshape(BATCH * FRAMES, D), w_out)).reshape(BATCH, FRAMES, D)
    middle = frames32 + branch
    normed_two = low(layer_norm(middle, gain_ffn, bias_ffn))
    hidden = low_back(matmul(normed_two.reshape(BATCH * FRAMES, D), w_up))
    activated = low(gelu_exact(hidden))
    ffn_out = low_back(matmul(activated, w_down)).reshape(BATCH, FRAMES, D)
    return middle + ffn_out

def reference(frames, utt_lengths, w_qkv, w_out, w_up, w_down, gain_attn, bias_attn, gain_ffn, bias_ffn, out_grad):
    seg_ids = utterance_ids(utt_lengths)
    floats = [item.astype(jnp.float32) for item in (frames, w_qkv, w_out, w_up, w_down, gain_attn, bias_attn, gain_ffn, bias_ffn)]

    def wrapped(frames32, wq, wo, wu, wd, ga, ba, gf, bf):
        return forward(frames32, wq, wo, wu, wd, ga, ba, gf, bf, seg_ids)
    result, pull_back = jax.vjp(wrapped, *floats)
    grads = pull_back(out_grad.astype(jnp.float32))
    return (result.astype(jnp.bfloat16), grads[0], grads[1], grads[2], grads[3], grads[4], grads[5], grads[6], grads[7], grads[8])
```

```python
import functools

import jax
import jax.numpy as jnp
from jax import lax
from jax.experimental import pallas as pl
from jax.experimental.pallas import tpu as pltpu
from jax.sharding import PartitionSpec as P

HEAD_DIM = 64
SEG = 16
GROUP = 64
KEYS = 128
MEMROWS = 16
FRONT = 32
EPS = 1e-05
FFC = 512
bf = jnp.bfloat16
f32 = jnp.float32
MESH = pl.DeviceIdType.MESH


def nn(a, b):
    return jnp.dot(a, b, preferred_element_type=f32)


def nt(a, b):
    return lax.dot_general(a, b, (((1,), (1,)), ((), ())), preferred_element_type=f32)


def tn(a, b):
    return lax.dot_general(a, b, (((0,), (0,)), ((), ())), preferred_element_type=f32)


def iota(shape, dim):
    return lax.broadcasted_iota(jnp.int32, shape, dim)


def standardise(x):
    mu = jnp.mean(x, axis=-1, keepdims=True)
    xc = x - mu
    rstd = lax.rsqrt(jnp.mean(xc * xc, axis=-1, keepdims=True) + EPS)
    return xc * rstd, rstd


def norm_grad(d, xhat, rstd, gain):
    g = d * gain
    return rstd * (
        g
        - jnp.mean(g, axis=-1, keepdims=True)
        - xhat * jnp.mean(g * xhat, axis=-1, keepdims=True)
    )


def rows_of(start, size, step=16):
    return pl.ds(pl.multiple_of(start, step), size)


def spread_heads(x):
    lane = iota((1, 256), 1) // HEAD_DIM
    return jnp.concatenate(
        [jnp.where(lane == h, x, jnp.zeros_like(x)) for h in range(4)], axis=0
    )


def own_columns(a):
    return jnp.where(iota((1, 128), 1) < HEAD_DIM, a[:GROUP], a[GROUP:])


def body(ntm, dims, *refs):
    T, D, FF, NU = dims
    NG = T // GROUP
    NS = T // SEG
    (
        frames_h, lens, wqkv, wo, wu, wd, ga, ba, gf, bfn, dy,
        out_h, gframes_h, units_h, small_h,
        X, Q, KV, MW, NT_, SUMM, ATTT, PR, MID, N2, N2T, DYT, OUT, D2, ACT, DH,
        MKV, SEL, KR, LO, HI, ST, EN, HX, HRL, HRR, HRM, SNL, SNR, U, UQ, SMALL, DSUM, DMK,
        lsem, osem, ssem, rsem,
    ) = refs
    TT = 256
    me = lax.axis_index("tm")
    right = lax.rem(me + 1, ntm)
    left = lax.rem(me + ntm - 1, ntm)

    load_x = pltpu.make_async_copy(frames_h, X, lsem.at[0])
    load_x.start()

    barrier = pltpu.get_barrier_semaphore()
    for other in (left, right):
        pl.semaphore_signal(barrier, inc=1, device_id={"tm": other}, device_id_type=MESH)
    pl.semaphore_wait(barrier, 2)

    def remote(k, src, dst, to):
        return pltpu.make_async_remote_copy(
            src_ref=src, dst_ref=dst, send_sem=ssem.at[k], recv_sem=rsem.at[k],
            device_id={"tm": to}, device_id_type=MESH,
        )

    to_right = remote(0, frames_h.at[T - 64 : T], HX.at[0:64], right)
    to_left = remote(1, frames_h.at[0:16], HX.at[64:80], left)
    to_right.start()
    to_left.start()

    for b in range(NU // 128):
        u = iota((128, 128), 0) + 128 * b
        first = jnp.zeros((128, 1), f32)
        last = jnp.zeros((128, 1), f32)
        for c in range(NU // 128):
            v = iota((128, 128), 1) + 128 * c
            n = lens[:, 128 * c : 128 * c + 128].astype(f32)
            first = first + jnp.sum(jnp.where(v < u, n, 0.0), axis=1, keepdims=True)
            last = last + jnp.sum(jnp.where(v <= u, n, 0.0), axis=1, keepdims=True)
        ST[128 * b : 128 * b + 128, :] = jnp.broadcast_to(first, (128, 128))
        EN[128 * b : 128 * b + 128, :] = jnp.broadcast_to(last, (128, 128))
    row = iota((KEYS, 128), 0)
    seg_q = (iota((KEYS, 128), 1) % GROUP) // SEG
    pos = row - MEMROWS
    mem_ok = (row < 8) & (seg_q <= row) & (row <= seg_q + 3)
    near_ok = (pos >= SEG * seg_q + 2) & (pos < SEG * seg_q + 52)
    rel = jnp.where(row < MEMROWS, row - 4, jnp.right_shift(pos, 4) - 2)
    KR[...] = jnp.where(
        jnp.where(row < MEMROWS, mem_ok.astype(jnp.int32), near_ok.astype(jnp.int32)) > 0,
        rel.astype(f32), -1e9,
    )

    def bounds(g, _):
        base = (me * NS + 4 * g).astype(f32)
        seg = base + ((iota((1, 128), 1) % GROUP) // SEG).astype(f32)
        st, en = ST[...], EN[...]
        lo = jnp.max(jnp.where(st <= seg, st, -1.0), axis=0, keepdims=True) - base
        hi = jnp.min(jnp.where(en > seg, en, 1e9), axis=0, keepdims=True) - base
        LO[g] = jnp.broadcast_to(lo, (8, 128))
        HI[g] = jnp.broadcast_to(hi, (8, 128))
        return 0

    lax.fori_loop(0, NG, bounds, 0)
    r512, c256 = iota((NG * 16, 256), 0), iota((NG * 16, 256), 1)
    seg = 4 * jnp.right_shift(r512, 4) - 4 + (r512 & 15)
    src = jnp.where(seg < 0, seg + 4 + NS, seg)
    SEL[...] = jnp.where(((r512 & 15) < 8) & (src == c256), 1.0, 0.0).astype(bf)

    load_x.wait()

    gain1, bias1 = ga[...], ba[...]
    mean16 = jnp.where(
        iota((16, TT), 0) == jnp.right_shift(iota((16, TT), 1), 4), 1.0 / SEG, 0.0
    ).astype(bf)

    def project(i, _):
        r = rows_of(i * TT, TT)
        xhat, _r = standardise(X[r, :].astype(f32))
        nb = (xhat * gain1 + bias1).astype(bf)
        NT_[:, rows_of(i * TT, TT, 128)] = nb.T
        SUMM[rows_of(i * 16, 16), :] = nn(mean16, nb).astype(bf)
        Q[r, :] = (nn(nb, wqkv[:, :D]) * HEAD_DIM**-0.5).astype(bf)
        KV[rows_of(i * TT + FRONT, TT), :] = nn(nb, wqkv[:, D:]).astype(bf)
        DYT[:, rows_of(i * TT, TT, 128)] = dy[r, :].T
        return 0

    lax.fori_loop(0, T // TT, project, 0)

    to_right.wait()
    to_left.wait()
    xhat, _r = standardise(HX[...].astype(f32))
    nb = (xhat * gain1 + bias1).astype(bf)
    edge = nn(nb, wqkv[:, D:]).astype(bf)
    KV[0:FRONT, :] = edge[32:64]
    KV[T + FRONT : T + FRONT + 16, :] = edge[64:80]
    SUMM[NS:256, :] = jnp.zeros((256 - NS, D), bf)
    SUMM[NS : NS + 16, :] = nn(mean16[:, :64], nb[:64]).astype(bf)
    MKV[...] = nn(SUMM[...], wqkv[:, D:]).astype(bf)
    MW[...] = nn(SEL[...], MKV[...]).astype(bf)

    gain2, bias2 = gf[...], bfn[...]

    def attend(i, _):
        r = rows_of(i * TT, TT)
        tiles = []
        for j in range(TT // GROUP):
            g = i * (TT // GROUP) + j
            win = rows_of(g * GROUP, 112)
            mem = rows_of(g * MEMROWS, MEMROWS)
            lo, hi = LO[g][0:1], HI[g][0:1]
            kr = KR[...]
            ok = (kr >= lo) & (kr < hi)
            cols = []
            for h in range(2):
                c = slice(256 * h, 256 * h + 256)
                cv = slice(D + 256 * h, D + 256 * h + 256)
                k4 = jnp.concatenate([MW[mem, c], KV[win, c]], axis=0)
                v4 = jnp.concatenate([MW[mem, cv], KV[win, cv]], axis=0)
                q4 = spread_heads(Q[rows_of(g * GROUP, GROUP), c])
                s = nt(k4, q4)
                for p in range(2):
                    cp = slice(128 * p, 128 * p + 128)
                    sp = jnp.where(ok, s[:, cp], -1e30)
                    e = jnp.exp(sp - jnp.max(sp, axis=0, keepdims=True))
                    pr = (e * (1.0 / jnp.sum(e, axis=0, keepdims=True))).astype(bf)
                    PR[rows_of(g * KEYS, KEYS), 256 * h + 128 * p : 256 * h + 128 * p + 128] = pr
                    cols.append(own_columns(tn(pr, v4[:, cp])))
            tiles.append(jnp.concatenate(cols, axis=1))
        att = jnp.concatenate(tiles, axis=0).astype(bf)
        ATTT[:, rows_of(i * TT, TT, 128)] = att.T
        mid = X[r, :].astype(f32) + nn(att, wo[...])
        MID[r, :] = mid
        xhat, _r = standardise(mid)
        n2 = (xhat * gain2 + bias2).astype(bf)
        N2[r, :] = n2
        N2T[:, rows_of(i * TT, TT, 128)] = n2.T
        return 0

    lax.fori_loop(0, T // TT, attend, 0)

    FT = 512
    for c in range(FF // FFC):
        cs = slice(c * FFC, (c + 1) * FFC)

        def ffn(i, _, c=c, cs=cs):
            r = rows_of(i * FT, FT)
            h = nn(N2[r, :], wu[:, cs])
            da = nt(dy[r, :], wd[cs, :])
            phi = 0.5 + 0.5 * lax.erf(h * 0.7071067811865476)
            slope = phi + h * (jnp.exp(h * h * -0.5) * 0.3989422804014327)
            a = (h * phi).astype(bf)
            d = (da * slope).astype(bf)
            ACT[r, :] = a
            DH[r, :] = d
            o = nn(a, wd[cs, :])
            d2 = nt(d, wu[:, cs])
            if c == 0:
                OUT[r, :] = MID[r, :] + o
                D2[r, :] = d2
            elif c < FF // FFC - 1:
                OUT[r, :] += o
                D2[r, :] += d2
            else:
                N2[r, :] = (OUT[r, :] + o).astype(bf)
                D2[r, :] += d2
            return 0

        lax.fori_loop(0, T // FT, ffn, 0)
        U[c] = nn(DYT[...], ACT[...]).astype(bf)
        U[FF // FFC + c] = nn(N2T[...], DH[...]).astype(bf)

    store_out = pltpu.make_async_copy(N2, out_h, osem.at[0])
    store_out.start()

    SMALL[...] = jnp.zeros_like(SMALL)

    def back_mid(i, _):
        r = rows_of(i * TT, TT)
        d2 = D2[r, :]
        xhat, rstd = standardise(MID[r, :])
        SMALL[2:3, :] += jnp.sum(d2 * xhat, axis=0, keepdims=True)
        SMALL[3:4, :] += jnp.sum(d2, axis=0, keepdims=True)
        dmid = dy[r, :].astype(f32) + norm_grad(d2, xhat, rstd, gain2)
        D2[r, :] = dmid
        db = dmid.astype(bf)
        ACT[r, :] = db
        DH[r, :] = nt(db, wo[...]).astype(bf)
        return 0

    lax.fori_loop(0, T // TT, back_mid, 0)
    U[2 * (FF // FFC)] = nn(ATTT[...], ACT[...]).astype(bf)

    for h in range(2):
        c = slice(256 * h, 256 * h + 256)
        cv = slice(D + 256 * h, D + 256 * h + 256)
        OUT[...] = jnp.zeros_like(OUT)

        def back_att(i, _, c=c, cv=cv):
            for j in range(4):
                g = lax.rem(i * 4 + j + NG - 1, NG)
                win = rows_of(g * GROUP, 112)
                mem = rows_of(g * MEMROWS, MEMROWS)
                qr = rows_of(g * GROUP, GROUP)
                k4 = jnp.concatenate([MW[mem, c], KV[win, c]], axis=0)
                v4 = jnp.concatenate([MW[mem, cv], KV[win, cv]], axis=0)
                q4 = spread_heads(Q[qr, c])
                o4 = spread_heads(DH[qr, c])
                pb = PR[rows_of(g * KEYS, KEYS), c]
                pf = pb.astype(f32)
                dp = nt(v4, o4)
                ds = (pf * (dp - jnp.sum(pf * dp, axis=0, keepdims=True))).astype(bf)
                dk = nn(ds, q4)
                dv = nn(pb, o4)
                dq = jnp.concatenate(
                    [
                        own_columns(tn(ds[:, 128 * p : 128 * p + 128], k4[:, 128 * p : 128 * p + 128]))
                        for p in range(2)
                    ],
                    axis=1,
                )
                Q[qr, c] = (dq * HEAD_DIM**-0.5).astype(bf)
                MW[mem, c] = dk[:MEMROWS].astype(bf)
                MW[mem, cv] = dv[:MEMROWS].astype(bf)
                OUT[win, 0:256] += dk[MEMROWS:]
                OUT[win, 256:512] += dv[MEMROWS:]
            return 0

        lax.fori_loop(0, NG // 4, back_att, 0)
        SNL[h, 0:FRONT, :] = OUT[0:FRONT, :].astype(bf)
        SNL[h, FRONT : FRONT + 16, 0:256] = MW[0:16, c]
        SNL[h, FRONT : FRONT + 16, 256:512] = MW[0:16, cv]
        SNR[h] = OUT[T + FRONT : T + FRONT + 16, :].astype(bf)
        give_left = remote(2 + 2 * h, SNL.at[h], HRL.at[h], left)
        give_right = remote(3 + 2 * h, SNR.at[h], HRR.at[h], right)
        give_left.start()
        give_right.start()
        give_left.wait()
        give_right.wait()
        live_l = jnp.where(me < ntm - 1, 1.0, 0.0).astype(f32)
        live_r = jnp.where(me > 0, 1.0, 0.0).astype(f32)
        OUT[T : T + FRONT, :] += HRL[h, 0:FRONT, :].astype(f32) * live_l
        OUT[FRONT : FRONT + 16, :] += HRR[h].astype(f32) * live_r
        pick = jnp.where(
            (iota((NS, 16), 0) == iota((NS, 16), 1) + NS - 4) & (iota((NS, 16), 1) < 4), 1.0, 0.0
        ).astype(bf)
        sel_own = SEL[:, 0:NS]
        dmw = jnp.concatenate([MW[:, c], MW[:, cv]], axis=1)
        dmk = tn(sel_own, dmw) + nn(pick, HRL[h, FRONT : FRONT + 16, :]) * live_l
        DMK[...] = dmk.astype(bf)

        def to_low(i, _, c=c, cv=cv):
            r = rows_of(i * TT + FRONT, TT)
            KV[r, c] = OUT[r, 0:256].astype(bf)
            KV[r, cv] = OUT[r, 256:512].astype(bf)
            return 0

        lax.fori_loop(0, T // TT, to_low, 0)
        own = slice(FRONT, T + FRONT)
        UQ[h, 0] = nn(NT_[...], Q[:, c]).astype(bf)
        UQ[h, 1] = (nn(NT_[...], KV[own, c]) + tn(SUMM[0:NS, :], DMK[:, 0:256])).astype(bf)
        UQ[h, 2] = (nn(NT_[...], KV[own, cv]) + tn(SUMM[0:NS, :], DMK[:, 256:512])).astype(bf)
        wk = slice(D + 256 * h, D + 256 * h + 256)
        wv = slice(2 * D + 256 * h, 2 * D + 256 * h + 256)
        dsum = (nt(DMK[:, 0:256], wqkv[:, wk]) + nt(DMK[:, 256:512], wqkv[:, wv])) * (1.0 / SEG)
        if h == 0:
            DSUM[...] = dsum
        else:
            DSUM[...] += dsum
        widen = jnp.where(
            jnp.right_shift(iota((TT, 16), 0), 4) == iota((TT, 16), 1), 1.0, 0.0
        ).astype(bf)

        def back_in(i, _, h=h, c=c, cv=cv, wk=wk, wv=wv):
            r = rows_of(i * TT, TT)
            rk = rows_of(i * TT + FRONT, TT)
            dn = nt(Q[r, c], wqkv[:, c]) + nt(KV[rk, c], wqkv[:, wk]) + nt(KV[rk, cv], wqkv[:, wv])
            if h == 0:
                MID[r, :] = dn
                return 0
            dn = dn + MID[r, :] + nn(widen, DSUM[rows_of(i * 16, 16), :].astype(bf))
            xhat, rstd = standardise(X[r, :].astype(f32))
            SMALL[0:1, :] += jnp.sum(dn * xhat, axis=0, keepdims=True)
            SMALL[1:2, :] += jnp.sum(dn, axis=0, keepdims=True)
            D2[r, :] += norm_grad(dn, xhat, rstd, gain1)
            return 0

        lax.fori_loop(0, T // TT, back_in, 0)

    store_g = pltpu.make_async_copy(D2, gframes_h, osem.at[1])
    store_g.start()
    nu = 2 * (FF // FFC) + 1
    store_u = pltpu.make_async_copy(U, units_h.at[0:nu], osem.at[2])
    store_u.start()
    store_q = [
        pltpu.make_async_copy(UQ.at[h, k], units_h.at[nu + k, :, pl.ds(256 * h, 256)], osem.at[4 + 3 * h + k])
        for h in range(2)
        for k in range(3)
    ]
    for s in store_q:
        s.start()
    store_s = pltpu.make_async_copy(SMALL, small_h, osem.at[3])
    store_s.start()
    store_out.wait()
    store_g.wait()
    store_u.wait()
    for s in store_q:
        s.wait()
    store_s.wait()


def local(frames, lens, wqkv, wo, wu, wd, ga, ba, gf, bfn, dy):
    T, D = frames.shape[1:]
    FF = wu.shape[1]
    NU = lens.shape[1]
    NG, NS = T // GROUP, T // SEG
    ntm = lax.axis_size("tm")
    nu = 2 * (FF // FFC) + 1
    V = pl.BlockSpec(memory_space=pltpu.VMEM)
    A = pl.BlockSpec(memory_space=pl.ANY)
    vm = lambda *s: pltpu.VMEM(s[:-1], s[-1])
    scratch = [
        vm(T, D, bf), vm(T, D, bf), vm(T + FRONT + 16, 2 * D, bf), vm(NG * 16, 2 * D, bf),
        vm(D, T, bf), vm(256, D, bf), vm(D, T, bf), vm(NG * KEYS, D, bf),
        vm(T, D, f32), vm(T, D, bf), vm(D, T, bf), vm(D, T, bf),
        vm(T + FRONT + 16, D, f32), vm(T, D, f32), vm(T, FFC, bf), vm(T, FFC, bf),
        vm(256, 2 * D, bf), vm(NG * 16, 256, bf), vm(KEYS, 128, f32), vm(NG, 8, 128, f32),
        vm(NG, 8, 128, f32), vm(NU, 128, f32), vm(NU, 128, f32), vm(80, D, bf),
        vm(2, 48, D, bf), vm(2, 16, D, bf), vm(2, 16, D, bf), vm(2, 48, D, bf), vm(2, 16, D, bf),
        vm(nu, D, D, bf), vm(2, 3, D, 256, bf), vm(8, D, f32), vm(NS, D, f32), vm(NS, D, bf),
        pltpu.SemaphoreType.DMA((2,)), pltpu.SemaphoreType.DMA((10,)),
        pltpu.SemaphoreType.DMA((6,)), pltpu.SemaphoreType.DMA((6,)),
    ]
    row = lambda v: v.reshape(1, D)
    out, gframes, units, small = pl.pallas_call(
        functools.partial(body, ntm, (T, D, FF, NU)),
        out_shape=[
            jax.ShapeDtypeStruct((T, D), bf),
            jax.ShapeDtypeStruct((T, D), f32),
            jax.ShapeDtypeStruct((nu + 3, D, D), bf),
            jax.ShapeDtypeStruct((8, D), f32),
        ],
        in_specs=[A] + [V] * 10,
        out_specs=[A] * 4,
        scratch_shapes=scratch,
        compiler_params=pltpu.CompilerParams(
            vmem_limit_bytes=60 * 2**20, collective_id=0, has_side_effects=True
        ),
    )(frames[0], lens, wqkv, wo, wu, wd, row(ga), row(ba), row(gf), row(bfn), dy[0])
    units = lax.psum(units, ("tm", "rows")).astype(f32)
    small = lax.psum(small, ("tm", "rows"))
    n = FF // FFC
    return (
        out[None],
        gframes[None],
        units[nu:].transpose(1, 0, 2).reshape(D, 3 * D),
        units[2 * n],
        units[n : 2 * n].transpose(1, 0, 2).reshape(D, FF),
        units[:n].transpose(0, 2, 1).reshape(FF, D),
        small[0], small[1], small[2], small[3],
    )


def solution(mesh):
    big, rep = P("rows", "tm", None), P()
    return jax.shard_map(
        local,
        mesh=mesh,
        in_specs=(big, P("rows", None)) + (rep,) * 8 + (big,),
        out_specs=(big, big) + (rep,) * 8,
        check_vma=False,
    )
```

```python
import functools

import jax
import jax.numpy as jnp
from jax import lax
from jax.experimental import pallas as pl
from jax.experimental.pallas import tpu as pltpu
from jax.sharding import PartitionSpec as P

HEAD_DIM = 64
SEG = 16
GROUP = 64
KEYS = 128
MEMROWS = 16
FRONT = 32
EPS = 1e-05
FFC = 512
TT = 512
GI = TT // GROUP
bf = jnp.bfloat16
f32 = jnp.float32
MESH = pl.DeviceIdType.MESH
ORDER = "10031110qqq"
GAPS = {
    "0": [1, 5, 4, 3, 3, 3, 3, 4, 5, 1],
    "q": [1, 5, 4, 4, 5, 1],
}


def nn(a, b):
    return jnp.dot(a, b, preferred_element_type=f32)


def nt(a, b):
    return lax.dot_general(a, b, (((1,), (1,)), ((), ())), preferred_element_type=f32)


def tn(a, b):
    return lax.dot_general(a, b, (((0,), (0,)), ((), ())), preferred_element_type=f32)


def iota(shape, dim):
    return lax.broadcasted_iota(jnp.int32, shape, dim)


def standardise(x):
    mu = jnp.mean(x, axis=-1, keepdims=True)
    xc = x - mu
    rstd = lax.rsqrt(jnp.mean(xc * xc, axis=-1, keepdims=True) + EPS)
    return xc * rstd, rstd


def norm_grad(d, xhat, rstd, gain):
    g = d * gain
    return rstd * (
        g
        - jnp.mean(g, axis=-1, keepdims=True)
        - xhat * jnp.mean(g * xhat, axis=-1, keepdims=True)
    )


def rows_of(start, size, step=16):
    return pl.ds(pl.multiple_of(start, step), size)


def spread_heads(x):
    lane = iota((1, 256), 1) // HEAD_DIM
    return jnp.concatenate(
        [jnp.where(lane == h, x, jnp.zeros_like(x)) for h in range(4)], axis=0
    )


def own_columns(a):
    return jnp.where(iota((1, 128), 1) < HEAD_DIM, a[:GROUP], a[GROUP:])


class Reduction:
    def __init__(self, stages, rows, own, got, sems, gaps, name):
        self.own, self.got, self.name = own, got, name
        self.ssem, self.rsem, self.freed = sems
        self.gaps = gaps
        self.pos, self.rest = 0, 0
        self.levels = []
        lo, size, at, sem = 0, rows, 0, 0
        for axes in stages:
            k = len(axes)
            split = size % (16 << k) == 0
            part = size >> k if split else size
            rank = sum(bit * 2**j for j, (bit, _) in enumerate(axes))
            peers = []
            for m in range(1, 1 << k):
                flip = [(m >> j) & 1 for j in range(k)]
                other = sum(
                    (1 - bit if f else bit) * 2**j for j, (f, (bit, _)) in enumerate(zip(flip, axes))
                )
                dev = {}
                for f, (bit, (axis, here, step)) in zip(flip, axes):
                    if f:
                        dev[axis] = dev.get(axis, here) + (1 - 2 * bit) * step
                peers.append((dev, other))
            mine = lo + rank * part if split else lo
            self.levels.append((peers, lo, mine, part, at, sem, split))
            lo, size = mine, part
            at += part * len(peers)
            sem += 2 * len(peers)
        self.steps = [(i, True) for i in range(len(stages))]
        self.steps += [(i, False) for i in reversed(range(len(stages))) if self.levels[i][6]]

    @staticmethod
    def landing(stages, rows):
        size, at, sem = rows, 0, 0
        for k in stages:
            size = size >> k if size % (16 << k) == 0 else size
            at += size * ((1 << k) - 1)
            sem += 2 * ((1 << k) - 1)
        return at, sem

    def copies(self, k):
        i, inward = self.steps[k]
        peers, lo, mine, part, at, sem, split = self.levels[i]
        made = []
        for q, (dev, other) in enumerate(peers):
            if inward:
                src = self.own(lo + other * part if split else lo, part)
                dst = self.got(at + q * part, part)
            else:
                src = dst = self.own(mine, part)
            z = sem + 2 * q + (0 if inward else 1)
            made.append(
                pltpu.make_async_remote_copy(
                    src_ref=src, dst_ref=dst, send_sem=self.ssem.at[z], recv_sem=self.rsem.at[z],
                    device_id=dev, device_id_type=MESH,
                )
            )
        return made

    def finish(self, k):
        for copy in self.copies(k):
            copy.wait()
        i, inward = self.steps[k]
        if inward:
            peers, _, mine, part, at, _, split = self.levels[i]
            if split:
                for dev, _other in peers:
                    pl.semaphore_signal(
                        self.freed.at[i], inc=1, device_id=dev, device_id_type=MESH
                    )
            view = self.own(mine, part)
            total = view[...]
            for q in range(len(peers)):
                total = total + self.got(at + q * part, part)[...]
            view[...] = total

    def advance(self):
        if self.pos:
            self.finish(self.pos - 1)
        if self.pos < len(self.steps):
            i, inward = self.steps[self.pos]
            if not inward:
                pl.semaphore_wait(self.freed.at[i], len(self.levels[i][0]))
            for copy in self.copies(self.pos):
                copy.start()
            self.rest = self.gaps[min(self.pos, len(self.gaps) - 1)]
        self.pos += 1
        return self.pos > len(self.steps)


def schemes(bits):
    low, high = list(range(min(2, bits))), list(range(2, bits))
    one = lambda order: [[b] for b in order]
    return {
        "0": one(low + high),
        "1": one(low[::-1] + high),
        "2": one(high + low),
        "3": one(high + low[::-1]),
        "q": [low] + [high[i : i + 2] for i in range(0, len(high), 2)],
    }


def body(ntm, dims, *refs):
    T, D, FF, NU = dims
    NG = T // GROUP
    NS = T // SEG
    NC = FF // FFC
    nu = 2 * NC + 1
    (
        frames_h, dy_h, wqkv_h, wo_h, wu_h, wd_h, lens, ga, ba, gf, bfn,
        out_h, gframes_h, units_h, uqkv_h, small_h,
        X, DY, wqkv, wo, wu, wd,
        Q, KV, MW, NT_, SUMM, ATTT, PR, MID, N2, N2T, DYT, OUT, D2, ACT, DH,
        SEL, KR, LO, HI, HX, HRL, HRR, SNL, SNR, U, UR, UQR, SMALL, SMR, DSUM, DMK,
        lsem, osem, ssem, rsem, ussem, ursem, xssem, xrsem, freed,
    ) = refs
    me, row_id = lax.axis_index("tm"), lax.axis_index("rows")
    right = lax.rem(me + 1, ntm)
    left = lax.rem(me + ntm - 1, ntm)

    loads = [
        pltpu.make_async_copy(src, dst, lsem.at[k])
        for k, (src, dst) in enumerate(
            [(frames_h, X), (wqkv_h, wqkv), (dy_h, DY), (wo_h, wo), (wu_h, wu), (wd_h, wd)]
        )
    ]
    for load in loads:
        load.start()

    bits = ntm.bit_length() - 1
    axes = [(row_id, ("rows", row_id, 1))]
    for b in range(bits):
        axes.append((lax.rem(lax.div(me, 2**b), 2), ("tm", me, 2**b)))

    def flipped(which):
        dev = {}
        for bit, (axis, here, step) in which:
            dev[axis] = dev.get(axis, here) + (1 - 2 * bit) * step
        return dev

    barrier = pltpu.get_barrier_semaphore()
    others = [{"tm": left}, {"tm": right}] + [flipped([a]) for a in axes]
    low = axes[1:3]
    others += [flipped(low)] if len(low) == 2 else []
    others += [flipped(axes[i : i + 2]) for i in range(3, bits, 2)]
    for other in others:
        pl.semaphore_signal(barrier, inc=1, device_id=other, device_id_type=MESH)

    def remote(k, src, dst, to):
        return pltpu.make_async_remote_copy(
            src_ref=src, dst_ref=dst, send_sem=ssem.at[k], recv_sem=rsem.at[k],
            device_id={"tm": to}, device_id_type=MESH,
        )

    kinds = schemes(bits)
    active = []

    def reduction(k, kind, rows, own, got):
        stages = [[axes[0]]] + [[axes[1 + b] for b in stage] for stage in kinds[kind]]
        gaps = GAPS[kind] if kind in GAPS else GAPS["0"]
        active.append(Reduction(stages, rows, own, got, (ussem.at[k], ursem.at[k], freed.at[k]), gaps, k))

    def slot(every=False):
        for red in list(active):
            red.rest -= 1
            if (red.rest <= 0 or every) and red.advance():
                active.remove(red)

    def slots(i, count):
        for k in range(count):
            if active:

                @pl.when(i == k)
                def _():
                    slot()

    def reduce_unit(k, kind):
        reduction(
            k, kind, D,
            lambda lo, n: U.at[k, rows_of(lo, n)],
            lambda lo, n: UR.at[k, lo : lo + n],
        )

    for load in loads[:3]:
        load.wait()
    gain1, bias1 = ga[...], ba[...]
    NM = TT // SEG
    mean16 = jnp.where(
        iota((NM, TT), 0) == jnp.right_shift(iota((NM, TT), 1), 4), 1.0 / SEG, 0.0
    ).astype(bf)

    def project(i, _):
        r = rows_of(i * TT, TT)
        xhat, _r = standardise(X[r, :].astype(f32))
        nb = (xhat * gain1 + bias1).astype(bf)
        NT_[:, rows_of(i * TT, TT, 128)] = nb.T
        SUMM[rows_of(i * NM, NM), :] = nn(mean16, nb).astype(bf)
        Q[r, :] = (nn(nb, wqkv[:, :D]) * HEAD_DIM**-0.5).astype(bf)
        KV[rows_of(i * TT + FRONT, TT), :] = nn(nb, wqkv[:, D:]).astype(bf)
        DYT[:, rows_of(i * TT, TT, 128)] = DY[r, :].T
        return 0

    lax.fori_loop(0, T // TT, project, 0)

    pl.semaphore_wait(barrier, len(others))
    to_right = remote(0, frames_h.at[T - 64 : T], HX.at[0:64], right)
    to_left = remote(1, frames_h.at[0:16], HX.at[64:80], left)
    to_right.start()
    to_left.start()

    for b in range(NU // 128):
        u = iota((128, 128), 0) + 128 * b
        first = jnp.zeros((128, 1), f32)
        last = jnp.zeros((128, 1), f32)
        for c in range(NU // 128):
            v = iota((128, 128), 1) + 128 * c
            n = lens[:, 128 * c : 128 * c + 128].astype(f32)
            first = first + jnp.sum(jnp.where(v < u, n, 0.0), axis=1, keepdims=True)
            last = last + jnp.sum(jnp.where(v <= u, n, 0.0), axis=1, keepdims=True)
        MID[128 * b : 128 * b + 128, 0:128] = jnp.broadcast_to(first, (128, 128))
        MID[128 * b : 128 * b + 128, 128:256] = jnp.broadcast_to(last, (128, 128))
    row = iota((KEYS, 128), 0)
    seg_q = (iota((KEYS, 128), 1) % GROUP) // SEG
    pos = row - MEMROWS
    mem_ok = (row < 8) & (seg_q <= row) & (row <= seg_q + 3)
    near_ok = (pos >= SEG * seg_q + 2) & (pos < SEG * seg_q + 52)
    rel = jnp.where(row < MEMROWS, row - 4, jnp.right_shift(pos, 4) - 2)
    KR[...] = jnp.where(
        jnp.where(row < MEMROWS, mem_ok.astype(jnp.int32), near_ok.astype(jnp.int32)) > 0,
        rel.astype(f32), -1e9,
    )

    def bounds(g, _):
        base = (me * NS + 4 * g).astype(f32)
        seg = base + ((iota((1, 128), 1) % GROUP) // SEG).astype(f32)
        st, en = MID[0:NU, 0:128], MID[0:NU, 128:256]
        lo = jnp.max(jnp.where(st <= seg, st, -1.0), axis=0, keepdims=True) - base
        hi = jnp.min(jnp.where(en > seg, en, 1e9), axis=0, keepdims=True) - base
        LO[g] = jnp.broadcast_to(lo, (8, 128))
        HI[g] = jnp.broadcast_to(hi, (8, 128))
        return 0

    lax.fori_loop(0, NG, bounds, 0)
    r512, c256 = iota((NG * 16, 256), 0), iota((NG * 16, 256), 1)
    seg = 4 * jnp.right_shift(r512, 4) - 4 + (r512 & 15)
    src = jnp.where(seg < 0, seg + 4 + NS, seg)
    SEL[...] = jnp.where(((r512 & 15) < 8) & (src == c256), 1.0, 0.0).astype(bf)
    SMALL[...] = jnp.zeros_like(SMALL)

    to_right.wait()
    to_left.wait()
    xhat, _r = standardise(HX[...].astype(f32))
    nb = (xhat * gain1 + bias1).astype(bf)
    edge = nn(nb, wqkv[:, D:]).astype(bf)
    KV[0:FRONT, :] = edge[32:64]
    KV[T + FRONT : T + FRONT + 16, :] = edge[64:80]
    SUMM[NS:256, :] = jnp.zeros((256 - NS, D), bf)
    SUMM[NS : NS + 16, :] = nn(mean16[:16, :64], nb[:64]).astype(bf)
    MW[...] = nn(SEL[...], nn(SUMM[...], wqkv[:, D:]).astype(bf)).astype(bf)

    loads[3].wait()
    gain2, bias2 = gf[...], bfn[...]

    def window(g, c):
        win = rows_of(g * GROUP, 112)
        mem = rows_of(g * MEMROWS, MEMROWS)
        return jnp.concatenate([MW[mem, c], KV[win, c]], axis=0)

    def attend(i, _):
        r = rows_of(i * TT, TT)
        gs = [i * GI + j for j in range(GI)]
        for j, g in enumerate(gs):
            for h in range(2):
                c = slice(256 * h, 256 * h + 256)
                q4 = spread_heads(Q[rows_of(g * GROUP, GROUP), c])
                OUT[KEYS * j : KEYS * j + KEYS, c] = nt(window(g, c), q4)
        for j, g in enumerate(gs):
            lo, hi = LO[g][0:1], HI[g][0:1]
            kr = KR[...]
            ok = (kr >= lo) & (kr < hi)
            for p in range(D // 128):
                cp = slice(128 * p, 128 * p + 128)
                s = jnp.where(ok, OUT[KEYS * j : KEYS * j + KEYS, cp], -1e30)
                e = jnp.exp(s - jnp.max(s, axis=0, keepdims=True))
                pr = e * (1.0 / jnp.sum(e, axis=0, keepdims=True))
                PR[rows_of(g * KEYS, KEYS), cp] = pr.astype(bf)
        tiles = []
        for g in gs:
            cols = []
            for p in range(D // 128):
                cp = slice(128 * p, 128 * p + 128)
                v2 = window(g, slice(D + 128 * p, D + 128 * p + 128))
                cols.append(own_columns(tn(PR[rows_of(g * KEYS, KEYS), cp], v2)))
            tiles.append(jnp.concatenate(cols, axis=1))
        att = jnp.concatenate(tiles, axis=0).astype(bf)
        ATTT[:, rows_of(i * TT, TT, 128)] = att.T
        mid = X[r, :].astype(f32) + nn(att, wo[...])
        MID[r, :] = mid
        xhat, _r = standardise(mid)
        n2 = (xhat * gain2 + bias2).astype(bf)
        N2[r, :] = n2
        N2T[:, rows_of(i * TT, TT, 128)] = n2.T
        return 0

    lax.fori_loop(0, T // TT, attend, 0)

    loads[4].wait()
    loads[5].wait()
    for c in range(NC):
        cs = slice(c * FFC, (c + 1) * FFC)

        def ffn(i, _, c=c, cs=cs):
            slots(i, T // TT)

            r = rows_of(i * TT, TT)
            h = nn(N2[r, :], wu[:, cs])
            da = nt(DY[r, :], wd[cs, :])
            phi = 0.5 + 0.5 * lax.erf(h * 0.7071067811865476)
            slope = phi + h * (jnp.exp(h * h * -0.5) * 0.3989422804014327)
            a = (h * phi).astype(bf)
            d = (da * slope).astype(bf)
            ACT[r, :] = a
            DH[r, :] = d
            o = nn(a, wd[cs, :])
            d2 = nt(d, wu[:, cs])
            if c == 0:
                OUT[r, :] = MID[r, :] + o
                D2[r, :] = d2
            elif c < NC - 1:
                OUT[r, :] += o
                D2[r, :] += d2
            else:
                N2[r, :] = (OUT[r, :] + o).astype(bf)
                D2[r, :] += d2
            return 0

        lax.fori_loop(0, T // TT, ffn, 0)
        U[c] = nn(DYT[...], ACT[...]).astype(bf)
        reduce_unit(c, ORDER[2 * c])
        slot()
        U[NC + c] = nn(N2T[...], DH[...]).astype(bf)
        reduce_unit(NC + c, ORDER[2 * c + 1])
        slot()

    store_out = pltpu.make_async_copy(N2, out_h, osem.at[0])
    store_out.start()

    def back_mid(i, _):
        slots(i, T // TT)

        r = rows_of(i * TT, TT)
        d2 = D2[r, :]
        xhat, rstd = standardise(MID[r, :])
        SMALL[2:3, :] += jnp.sum(d2 * xhat, axis=0, keepdims=True)
        SMALL[3:4, :] += jnp.sum(d2, axis=0, keepdims=True)
        dmid = DY[r, :].astype(f32) + norm_grad(d2, xhat, rstd, gain2)
        D2[r, :] = dmid
        db = dmid.astype(bf)
        ACT[r, :] = db
        DH[r, :] = nt(db, wo[...]).astype(bf)
        return 0

    lax.fori_loop(0, T // TT, back_mid, 0)
    U[2 * NC] = nn(ATTT[...], ACT[...]).astype(bf)
    reduce_unit(2 * NC, ORDER[2 * NC])

    for h in range(2):
        c = slice(256 * h, 256 * h + 256)
        cv = slice(D + 256 * h, D + 256 * h + 256)
        OUT[...] = jnp.zeros_like(OUT)
        give_left = remote(2 + 2 * h, SNL.at[h], HRL.at[h], left)
        give_right = remote(3 + 2 * h, SNR.at[h], HRR.at[h], right)

        def back_att(i, _, h=h, c=c, cv=cv, give_left=give_left, give_right=give_right):
            slots(i, NG // GI)

            gs = [lax.rem(i * GI + j + NG - 1, NG) for j in range(GI)]
            half = slice(0, 256)
            for j, g in enumerate(gs):
                o4 = spread_heads(DH[rows_of(g * GROUP, GROUP), c])
                MID[GI * KEYS + KEYS * j : GI * KEYS + KEYS * j + KEYS, half] = nt(window(g, cv), o4)
            for j, g in enumerate(gs):
                for p in range(2):
                    cp = slice(128 * p, 128 * p + 128)
                    cg = slice(256 * h + 128 * p, 256 * h + 128 * p + 128)
                    pf = PR[rows_of(g * KEYS, KEYS), cg].astype(f32)
                    t = pf * MID[GI * KEYS + KEYS * j : GI * KEYS + KEYS * j + KEYS, cp]
                    ds = t - pf * jnp.sum(t, axis=0, keepdims=True)
                    ACT[KEYS * j : KEYS * j + KEYS, cp] = ds.astype(bf)
            for j, g in enumerate(gs):
                k4 = window(g, c)
                for p in range(2):
                    cp = slice(128 * p, 128 * p + 128)
                    dq = own_columns(tn(ACT[KEYS * j : KEYS * j + KEYS, cp], k4[:, cp]))
                    ACT[GROUP * j : GROUP * j + GROUP, 256 + 128 * p : 384 + 128 * p] = (
                        dq * HEAD_DIM**-0.5
                    ).astype(bf)
            for j, g in enumerate(gs):
                qr = rows_of(g * GROUP, GROUP)
                MID[KEYS * j : KEYS * j + KEYS, 0:256] = nn(
                    ACT[KEYS * j : KEYS * j + KEYS, half], spread_heads(Q[qr, c])
                )
                MID[KEYS * j : KEYS * j + KEYS, 256:512] = nn(
                    PR[rows_of(g * KEYS, KEYS), c], spread_heads(DH[qr, c])
                )
            for j, g in enumerate(gs):
                win = rows_of(g * GROUP, 112)
                mem = rows_of(g * MEMROWS, MEMROWS)
                Q[rows_of(g * GROUP, GROUP), c] = ACT[GROUP * j : GROUP * j + GROUP, 256:512]
                MW[mem, c] = MID[KEYS * j : KEYS * j + MEMROWS, 0:256].astype(bf)
                MW[mem, cv] = MID[KEYS * j : KEYS * j + MEMROWS, 256:512].astype(bf)
                OUT[win, :] += MID[KEYS * j + MEMROWS : KEYS * j + KEYS, :]

            @pl.when(i == 0)
            def _():
                SNL[h, 0:FRONT, :] = OUT[0:FRONT, :].astype(bf)
                SNL[h, FRONT : FRONT + 16, 0:256] = MW[0:16, c]
                SNL[h, FRONT : FRONT + 16, 256:512] = MW[0:16, cv]
                SNR[h] = OUT[T + FRONT : T + FRONT + 16, :].astype(bf)
                give_left.start()
                give_right.start()

            return 0

        lax.fori_loop(0, NG // GI, back_att, 0)
        give_left.wait()
        give_right.wait()
        live_l = jnp.where(me < ntm - 1, 1.0, 0.0).astype(f32)
        live_r = jnp.where(me > 0, 1.0, 0.0).astype(f32)
        OUT[T : T + FRONT, :] += HRL[h, 0:FRONT, :].astype(f32) * live_l
        OUT[FRONT : FRONT + 16, :] += HRR[h].astype(f32) * live_r
        pick = jnp.where(
            (iota((NS, 16), 0) == iota((NS, 16), 1) + NS - 4) & (iota((NS, 16), 1) < 4), 1.0, 0.0
        ).astype(bf)
        dmw = jnp.concatenate([MW[:, c], MW[:, cv]], axis=1)
        dmk = tn(SEL[:, 0:NS], dmw) + nn(pick, HRL[h, FRONT : FRONT + 16, :]) * live_l
        DMK[:, 512 * h : 512 * h + 512] = dmk.astype(bf)

        def to_low(i, _, c=c, cv=cv):
            r = rows_of(i * TT + FRONT, TT)
            KV[r, c] = OUT[r, 0:256].astype(bf)
            KV[r, cv] = OUT[r, 256:512].astype(bf)
            return 0

        lax.fori_loop(0, T // TT, to_low, 0)
        own = slice(FRONT, T + FRONT)
        at = 768 * h
        N2T[:, at : at + 256] = nn(NT_[...], Q[:, c]).astype(bf)
        N2T[:, at + 256 : at + 512] = (
            nn(NT_[...], KV[own, c]) + tn(SUMM[0:NS, :], DMK[:, 512 * h : 512 * h + 256])
        ).astype(bf)
        N2T[:, at + 512 : at + 768] = (
            nn(NT_[...], KV[own, cv]) + tn(SUMM[0:NS, :], DMK[:, 512 * h + 256 : 512 * h + 512])
        ).astype(bf)
        reduction(
            nu + h, ORDER[2 * NC + 1 + h], D,
            lambda lo, n, at=at: N2T.at[rows_of(lo, n), at : at + 768],
            lambda lo, n, h=h: UQR.at[h, lo : lo + n],
        )
        slot()

    dsum = jnp.zeros((NS, D), f32)
    for h in range(2):
        for k in range(2):
            lo = D * (1 + k) + 256 * h
            dsum += nt(DMK[:, 512 * h + 256 * k : 512 * h + 256 * k + 256], wqkv[:, lo : lo + 256])
    DSUM[...] = (dsum * (1.0 / SEG)).astype(bf)
    widen = jnp.where(
        jnp.right_shift(iota((TT, NM), 0), 4) == iota((TT, NM), 1), 1.0, 0.0
    ).astype(bf)

    def back_in(i, _):
        slots(i, T // TT)

        r = rows_of(i * TT, TT)
        rk = rows_of(i * TT + FRONT, TT)
        dn = nt(Q[r, :], wqkv[:, :D]) + nt(KV[rk, :], wqkv[:, D:])
        dn = dn + nn(widen, DSUM[rows_of(i * NM, NM), :])
        xhat, rstd = standardise(X[r, :].astype(f32))
        SMALL[0:1, :] += jnp.sum(dn * xhat, axis=0, keepdims=True)
        SMALL[1:2, :] += jnp.sum(dn, axis=0, keepdims=True)
        D2[r, :] += norm_grad(dn, xhat, rstd, gain1)
        return 0

    lax.fori_loop(0, T // TT, back_in, 0)
    store_g = pltpu.make_async_copy(D2, gframes_h, osem.at[1])
    store_g.start()

    def small_copy(k):
        return pltpu.make_async_remote_copy(
            src_ref=SMALL, dst_ref=SMR.at[k], send_sem=xssem.at[k], recv_sem=xrsem.at[k],
            device_id=flipped([axes[k]]), device_id_type=MESH,
        )

    for k in range(bits + 1):
        small_copy(k).start()
        slot(True)
        small_copy(k).wait()
        SMALL[...] += SMR[k]
    while active:
        slot(True)
    store_u = pltpu.make_async_copy(U, units_h, osem.at[2])
    store_q = pltpu.make_async_copy(N2T.at[:, 0 : 3 * D], uqkv_h, osem.at[3])
    store_s = pltpu.make_async_copy(SMALL, small_h, osem.at[4])
    for store in (store_u, store_q, store_s):
        store.start()
    for store in (store_out, store_g, store_u, store_q, store_s):
        store.wait()


def finish(gd, gu, go, gq, out, gframes, small, gd_o, gu_o, go_o, gq_o, out_o, gframes_o, *vectors):
    for k, vector in enumerate(vectors):
        vector[...] = small[k : k + 1, :]
    gd_o[...] = gd[0].astype(f32).T
    gu_o[...] = gu[0].astype(f32)
    go_o[...] = go[0].astype(f32)
    for h in range(2):
        for p in range(3):
            gq_o[:, 512 * p + 256 * h : 512 * p + 256 * h + 256] = gq[
                :, 768 * h + 256 * p : 768 * h + 256 * p + 256
            ].astype(f32)
    out_o[...] = out[...]
    gframes_o[...] = gframes[...]


def local(frames, lens, wqkv, wo, wu, wd, ga, ba, gf, bfn, dy):
    T, D = frames.shape[1:]
    FF = wu.shape[1]
    NU = lens.shape[1]
    NG, NS = T // GROUP, T // SEG
    NC = FF // FFC
    ntm = lax.axis_size("tm")
    levels = ntm.bit_length()
    nu = 2 * NC + 1
    V = pl.BlockSpec(memory_space=pltpu.VMEM)
    A = pl.BlockSpec(memory_space=pl.ANY)
    vm = lambda *s: pltpu.VMEM(s[:-1], s[-1])
    dma = lambda *s: pltpu.SemaphoreType.DMA(s)
    land, sems = 0, 0
    for kind in schemes(levels - 1).values():
        need = Reduction.landing([1] + [len(stage) for stage in kind], D)
        land, sems = max(land, need[0]), max(sems, need[1])
    scratch = [
        vm(T, D, bf), vm(T, D, bf), vm(D, 3 * D, bf), vm(D, D, bf), vm(D, FF, bf), vm(FF, D, bf),
        vm(T, D, bf), vm(T + FRONT + 16, 2 * D, bf), vm(NG * 16, 2 * D, bf),
        vm(D, T, bf), vm(256, D, bf), vm(D, T, bf), vm(NG * KEYS, D, bf),
        vm(T, D, f32), vm(T, D, bf), vm(D, T, bf), vm(D, T, bf),
        vm(T + FRONT + 16, D, f32), vm(T, D, f32), vm(T, FFC, bf), vm(T, FFC, bf),
        vm(NG * 16, 256, bf), vm(KEYS, 128, f32), vm(NG, 8, 128, f32),
        vm(NG, 8, 128, f32), vm(80, D, bf),
        vm(2, 48, D, bf), vm(2, 16, D, bf), vm(2, 48, D, bf), vm(2, 16, D, bf),
        vm(nu, D, D, bf), vm(nu, land, D, bf), vm(2, land, 768, bf),
        vm(8, D, f32), vm(levels, 8, D, f32), vm(NS, D, bf), vm(NS, 2 * D, bf),
        dma(6), dma(5), dma(6), dma(6),
        dma(nu + 2, sems), dma(nu + 2, sems), dma(levels), dma(levels),
        pltpu.SemaphoreType.REGULAR((nu + 2, levels)),
    ]
    row = lambda v: v.reshape(1, D)
    out, gframes, units, uqkv, small = pl.pallas_call(
        functools.partial(body, ntm, (T, D, FF, NU)),
        out_shape=[
            jax.ShapeDtypeStruct((T, D), bf),
            jax.ShapeDtypeStruct((T, D), f32),
            jax.ShapeDtypeStruct((nu, D, D), bf),
            jax.ShapeDtypeStruct((D, 3 * D), bf),
            jax.ShapeDtypeStruct((8, D), f32),
        ],
        in_specs=[A] * 6 + [V] * 5,
        out_specs=[A] * 5,
        scratch_shapes=scratch,
        compiler_params=pltpu.CompilerParams(
            vmem_limit_bytes=63 * 2**20, collective_id=0, has_side_effects=True
        ),
    )(frames[0], dy[0], wqkv, wo, wu, wd, lens, row(ga), row(ba), row(gf), row(bfn))
    parts = FFC // 256
    steps = NC * parts
    part, tile = D // steps, T // steps
    spec = lambda shape, index: pl.BlockSpec(shape, index)
    down, up, gout, gqkv, out, gframes, *vectors = pl.pallas_call(
        finish,
        grid=(steps,),
        out_shape=[
            jax.ShapeDtypeStruct((FF, D), f32),
            jax.ShapeDtypeStruct((D, FF), f32),
            jax.ShapeDtypeStruct((D, D), f32),
            jax.ShapeDtypeStruct((D, 3 * D), f32),
            jax.ShapeDtypeStruct((T, D), bf),
            jax.ShapeDtypeStruct((T, D), f32),
        ]
        + [jax.ShapeDtypeStruct((1, D), f32)] * 4,
        in_specs=[
            spec((1, D, 256), lambda k: (k // parts, 0, k % parts)),
            spec((1, D, 256), lambda k: (NC + k // parts, 0, k % parts)),
            spec((1, part, D), lambda k: (2 * NC, k, 0)),
            spec((part, 3 * D), lambda k: (k, 0)),
            spec((tile, D), lambda k: (k, 0)),
            spec((tile, D), lambda k: (k, 0)),
            spec((8, D), lambda k: (0, 0)),
        ],
        out_specs=[
            spec((256, D), lambda k: (k, 0)),
            spec((D, 256), lambda k: (0, k)),
            spec((part, D), lambda k: (k, 0)),
            spec((part, 3 * D), lambda k: (k, 0)),
            spec((tile, D), lambda k: (k, 0)),
            spec((tile, D), lambda k: (k, 0)),
        ]
        + [spec((1, D), lambda k: (0, 0))] * 4,
        compiler_params=pltpu.CompilerParams(vmem_limit_bytes=62 * 2**20),
    )(units, units, units, uqkv, out, gframes, small)
    return (
        out[None], gframes[None], gqkv, gout, up, down,
        *[v.reshape(D) for v in vectors],
    )


def solution(mesh):
    big, rep = P("rows", "tm", None), P()
    return jax.shard_map(
        local,
        mesh=mesh,
        in_specs=(big, P("rows", None)) + (rep,) * 8 + (big,),
        out_specs=(big, big) + (rep,) * 8,
        check_vma=False,
    )
```

```python
import functools

import jax
import jax.numpy as jnp
from jax import lax
from jax.experimental import pallas as pl
from jax.experimental.pallas import tpu as pltpu
from jax.sharding import PartitionSpec as P

HEAD_DIM = 64
SEG = 16
GROUP = 64
KEYS = 128
MEMROWS = 16
FRONT = 32
EPS = 1e-05
FFC = 512
TT = 512
GI = TT // GROUP
bf = jnp.bfloat16
f32 = jnp.float32
MESH = pl.DeviceIdType.MESH
ORDER = ["01"] * 9 + ["q", "q"]
GAPS = {
    "0": [1, 4, 3, 3, 4, 3, 3, 4, 1],
    "p": [1, 5, 3, 3, 3, 5, 1],
    "q": [1, 4, 3, 3, 4, 1],
}


def nn(a, b):
    return jnp.dot(a, b, preferred_element_type=f32)


def nt(a, b):
    return lax.dot_general(a, b, (((1,), (1,)), ((), ())), preferred_element_type=f32)


def tn(a, b):
    return lax.dot_general(a, b, (((0,), (0,)), ((), ())), preferred_element_type=f32)


def iota(shape, dim):
    return lax.broadcasted_iota(jnp.int32, shape, dim)


def standardise(x):
    mu = jnp.mean(x, axis=-1, keepdims=True)
    xc = x - mu
    rstd = lax.rsqrt(jnp.mean(xc * xc, axis=-1, keepdims=True) + EPS)
    return xc * rstd, rstd


def norm_grad(d, xhat, rstd, gain):
    g = d * gain
    return rstd * (
        g
        - jnp.mean(g, axis=-1, keepdims=True)
        - xhat * jnp.mean(g * xhat, axis=-1, keepdims=True)
    )


def rows_of(start, size, step=16):
    return pl.ds(pl.multiple_of(start, step), size)


def spread_heads(x):
    lane = iota((1, 256), 1) // HEAD_DIM
    return jnp.concatenate(
        [jnp.where(lane == h, x, jnp.zeros_like(x)) for h in range(4)], axis=0
    )


def own_columns(a):
    return jnp.where(iota((1, 128), 1) < HEAD_DIM, a[:GROUP], a[GROUP:])


class Reduction:
    def __init__(self, stages, rows, own, got, sems, gaps, name):
        self.own, self.got, self.name = own, got, name
        self.ssem, self.rsem, self.freed = sems
        self.gaps = gaps
        self.pos, self.rest = 0, 0
        self.levels = []
        lo, size, at, sem = 0, rows, 0, 0
        for n, axes in enumerate(stages):
            k = len(axes)
            split = size % (16 << k) == 0 and (k > 1 or n < len(stages) - 1)
            part = size >> k if split else size
            rank = sum(bit * 2**j for j, (bit, _) in enumerate(axes))
            peers = []
            for m in range(1, 1 << k):
                flip = [(m >> j) & 1 for j in range(k)]
                other = sum(
                    (1 - bit if f else bit) * 2**j for j, (f, (bit, _)) in enumerate(zip(flip, axes))
                )
                dev = {}
                for f, (bit, (axis, here, step)) in zip(flip, axes):
                    if f:
                        dev[axis] = dev.get(axis, here) + (1 - 2 * bit) * step
                peers.append((dev, other))
            mine = lo + rank * part if split else lo
            self.levels.append((peers, lo, mine, part, at, sem, split))
            lo, size = mine, part
            at += part * len(peers)
            sem += 2 * len(peers)
        self.steps = [(i, True) for i in range(len(stages))]
        self.steps += [(i, False) for i in reversed(range(len(stages))) if self.levels[i][6]]

    @staticmethod
    def landing(stages, rows):
        size, at, sem = rows, 0, 0
        for n, k in enumerate(stages):
            split = size % (16 << k) == 0 and (k > 1 or n < len(stages) - 1)
            size = size >> k if split else size
            at += size * ((1 << k) - 1)
            sem += 2 * ((1 << k) - 1)
        return at, sem

    def copies(self, k):
        i, inward = self.steps[k]
        peers, lo, mine, part, at, sem, split = self.levels[i]
        made = []
        for q, (dev, other) in enumerate(peers):
            if inward:
                src = self.own(lo + other * part if split else lo, part)
                dst = self.got(at + q * part, part)
            else:
                src = dst = self.own(mine, part)
            z = sem + 2 * q + (0 if inward else 1)
            made.append(
                pltpu.make_async_remote_copy(
                    src_ref=src, dst_ref=dst, send_sem=self.ssem.at[z], recv_sem=self.rsem.at[z],
                    device_id=dev, device_id_type=MESH,
                )
            )
        return made

    def finish(self, k):
        for copy in self.copies(k):
            copy.wait()
        i, inward = self.steps[k]
        if inward:
            peers, _, mine, part, at, _, split = self.levels[i]
            if split:
                for dev, _other in peers:
                    pl.semaphore_signal(
                        self.freed.at[i], inc=1, device_id=dev, device_id_type=MESH
                    )
            view = self.own(mine, part)
            total = view[...]
            for q in range(len(peers)):
                total = total + self.got(at + q * part, part)[...]
            view[...] = total

    def advance(self):
        if self.pos:
            self.finish(self.pos - 1)
        if self.pos < len(self.steps):
            i, inward = self.steps[self.pos]
            if not inward:
                pl.semaphore_wait(self.freed.at[i], len(self.levels[i][0]))
            for copy in self.copies(self.pos):
                copy.start()
            self.rest = self.gaps[min(self.pos, len(self.gaps) - 1)]
        self.pos += 1
        return self.pos > len(self.steps)


def schemes(bits):
    low, high = list(range(min(2, bits))), list(range(2, bits))
    one = lambda order: [[b] for b in order]
    return {
        "0": one(low + high),
        "1": one(low[::-1] + high),
        "2": one(high + low),
        "3": one(high + low[::-1]),
        "p": [low] + one(high),
        "q": [low] + [high[i : i + 2] for i in range(0, len(high), 2)],
    }


def body(ntm, dims, *refs):
    T, D, FF, NU = dims
    NG = T // GROUP
    NS = T // SEG
    NC = FF // FFC
    nu = 2 * NC + 1
    (
        frames_h, dy_h, wqkv_h, wo_h, wu_h, wd_h, lens, ga, ba, gf, bfn,
        out_h, gframes_h, units_h, uqkv_h, small_h, acts_h, mid_h,
        X, DY, wqkv, wo, wu, wd,
        Q, KV, MW, NT_, SUMM, ATTT, PR, MID, N2, N2T, DYT, OUT, D2, ACT, DH,
        SEL, KR, LOHI, HX, HRL, HRR, SNL, SNR, U, UR, UQR, SMALL, SMR,
        lsem, osem, ssem, rsem, ussem, ursem, xssem, xrsem, freed, asem, bsem,
    ) = refs
    me, row_id = lax.axis_index("tm"), lax.axis_index("rows")
    right = lax.rem(me + 1, ntm)
    left = lax.rem(me + ntm - 1, ntm)

    loads = [
        pltpu.make_async_copy(src, dst, lsem.at[k])
        for k, (src, dst) in enumerate(
            [(frames_h, X), (wqkv_h, wqkv), (dy_h, DY), (wo_h, wo), (wu_h, wu), (wd_h, wd)]
        )
    ]
    for load in loads[:2]:
        load.start()

    bits = ntm.bit_length() - 1
    axes = [(row_id, ("rows", row_id, 1))]
    for b in range(bits):
        axes.append((lax.rem(lax.div(me, 2**b), 2), ("tm", me, 2**b)))

    def flipped(which):
        dev = {}
        for bit, (axis, here, step) in which:
            dev[axis] = dev.get(axis, here) + (1 - 2 * bit) * step
        return dev

    barrier = pltpu.get_barrier_semaphore()
    others = [{"tm": left}, {"tm": right}] + [flipped([a]) for a in axes]
    low = axes[1:3]
    others += [flipped(low)] if len(low) == 2 else []
    others += [flipped(axes[i : i + 2]) for i in range(3, bits, 2)]
    for other in others:
        pl.semaphore_signal(barrier, inc=1, device_id=other, device_id_type=MESH)

    def remote(k, src, dst, to):
        return pltpu.make_async_remote_copy(
            src_ref=src, dst_ref=dst, send_sem=ssem.at[k], recv_sem=rsem.at[k],
            device_id={"tm": to}, device_id_type=MESH,
        )

    kinds = schemes(bits)
    active = []

    def reduction(k, kind, rows, own, got):
        stages = [[axes[0]]] + [[axes[1 + b] for b in stage] for stage in kinds[kind]]
        gaps = GAPS[kind] if kind in GAPS else GAPS["0"]
        active.append(Reduction(stages, rows, own, got, (ussem.at[k], ursem.at[k], freed.at[k]), gaps, k))

    def slot(every=False):
        for red in list(active):
            red.rest -= 1
            if (red.rest <= 0 or every) and red.advance():
                active.remove(red)

    def slots(i, count):
        for k in range(count):
            if active:

                @pl.when(i == k)
                def _():
                    slot()

    def reduce_block(k, kind, own, got, width):
        for part, order in enumerate(kind):
            cols = pl.ds(part * (width // len(kind)), width // len(kind))
            reduction(
                2 * k + part, order, D,
                lambda lo, n, cols=cols: own(rows_of(lo, n), cols),
                lambda lo, n, cols=cols: got(pl.ds(lo, n), cols),
            )

    def reduce_unit(k, kind):
        reduce_block(
            k, kind, lambda r, c: U.at[k, r, c], lambda r, c: UR.at[k, r, c], D
        )

    for load in loads[:2]:
        load.wait()
    for load in loads[2:]:
        load.start()
    gain1, bias1 = ga[...], ba[...]
    NM = TT // SEG
    mean16 = jnp.where(
        iota((NM, TT), 0) == jnp.right_shift(iota((NM, TT), 1), 4), 1.0 / SEG, 0.0
    ).astype(bf)

    def project(i, _):
        r = rows_of(i * TT, TT)
        xhat, _r = standardise(X[r, :].astype(f32))
        nb = (xhat * gain1 + bias1).astype(bf)
        NT_[:, rows_of(i * TT, TT, 128)] = nb.T
        SUMM[rows_of(i * NM, NM), :] = nn(mean16, nb).astype(bf)
        Q[r, :] = (nn(nb, wqkv[:, :D]) * HEAD_DIM**-0.5).astype(bf)
        KV[rows_of(i * TT + FRONT, TT), :] = nn(nb, wqkv[:, D:]).astype(bf)
        return 0

    lax.fori_loop(0, T // TT, project, 0)

    pl.semaphore_wait(barrier, len(others))
    to_right = remote(0, frames_h.at[T - 64 : T], HX.at[0:64], right)
    to_left = remote(1, frames_h.at[0:16], HX.at[64:80], left)
    to_right.start()
    to_left.start()

    for b in range(NU // 128):
        u = iota((128, 128), 0) + 128 * b
        first = jnp.zeros((128, 1), f32)
        last = jnp.zeros((128, 1), f32)
        for c in range(NU // 128):
            v = iota((128, 128), 1) + 128 * c
            n = lens[:, 128 * c : 128 * c + 128].astype(f32)
            first = first + jnp.sum(jnp.where(v < u, n, 0.0), axis=1, keepdims=True)
            last = last + jnp.sum(jnp.where(v <= u, n, 0.0), axis=1, keepdims=True)
        MID[128 * b : 128 * b + 128, 0:128] = jnp.broadcast_to(first, (128, 128))
        MID[128 * b : 128 * b + 128, 128:256] = jnp.broadcast_to(last, (128, 128))
    row = iota((KEYS, 128), 0)
    seg_q = (iota((KEYS, 128), 1) % GROUP) // SEG
    pos = row - MEMROWS
    mem_ok = (row < 8) & (seg_q <= row) & (row <= seg_q + 3)
    near_ok = (pos >= SEG * seg_q + 2) & (pos < SEG * seg_q + 52)
    rel = jnp.where(row < MEMROWS, row - 4, jnp.right_shift(pos, 4) - 2)
    KR[...] = jnp.where(
        jnp.where(row < MEMROWS, mem_ok.astype(jnp.int32), near_ok.astype(jnp.int32)) > 0,
        rel.astype(f32), -1e9,
    )

    def bounds(g, _):
        base = (me * NS + 4 * g).astype(f32)
        seg = base + ((iota((1, 128), 1) % GROUP) // SEG).astype(f32)
        st, en = MID[0:NU, 0:128], MID[0:NU, 128:256]
        lo = jnp.max(jnp.where(st <= seg, st, -1.0), axis=0, keepdims=True) - base
        hi = jnp.min(jnp.where(en > seg, en, 1e9), axis=0, keepdims=True) - base
        LOHI[g] = jnp.where(iota((8, 128), 0) == 0, lo, hi)
        return 0

    lax.fori_loop(0, NG, bounds, 0)
    rows, cols = iota((NG * 16, NS), 0), iota((NG * 16, NS), 1)
    seg = 4 * jnp.right_shift(rows, 4) - 4 + (rows & 15)
    SEL[...] = jnp.where(((rows & 15) < 8) & (seg == cols), 1.0, 0.0).astype(bf)
    SMALL[...] = jnp.zeros_like(SMALL)

    MW[...] = nn(SEL[...], nn(SUMM[...], wqkv[:, D:]).astype(bf)).astype(bf)

    def edges():
        to_right.wait()
        to_left.wait()
        xhat, _r = standardise(HX[...].astype(f32))
        nb = (xhat * gain1 + bias1).astype(bf)
        edge = nn(nb, wqkv[:, D:]).astype(bf)
        KV[0:FRONT, :] = edge[32:64]
        KV[T + FRONT : T + FRONT + 16, :] = edge[64:80]
        mem = nn(nn(mean16[:16, :64], nb[:64]).astype(bf), wqkv[:, D:])
        now = MW[0:16, :].astype(f32)
        MW[0:16, :] = jnp.where(iota((16, 1), 0) < 4, mem, now).astype(bf)

    loads[2].wait()
    loads[3].wait()
    gain2, bias2 = gf[...], bfn[...]

    def window(g, c):
        win = rows_of(g * GROUP, 112)
        mem = rows_of(g * MEMROWS, MEMROWS)
        return jnp.concatenate([MW[mem, c], KV[win, c]], axis=0)

    def attend(step, _):
        @pl.when(step == T // TT - 2)
        def _():
            edges()

        i = lax.rem(step + 1, T // TT)
        r = rows_of(i * TT, TT)
        gs = [i * GI + j for j in range(GI)]
        for j, g in enumerate(gs):
            for h in range(2):
                c = slice(256 * h, 256 * h + 256)
                q4 = spread_heads(Q[rows_of(g * GROUP, GROUP), c])
                OUT[KEYS * j : KEYS * j + KEYS, c] = nt(window(g, c), q4)
        for j, g in enumerate(gs):
            lo, hi = LOHI[g, 0:1, :], LOHI[g, 1:2, :]
            kr = KR[...]
            ok = (kr >= lo) & (kr < hi)
            for p in range(D // 128):
                cp = slice(128 * p, 128 * p + 128)
                s = jnp.where(ok, OUT[KEYS * j : KEYS * j + KEYS, cp], -1e30)
                e = jnp.exp(s - jnp.max(s, axis=0, keepdims=True))
                pr = e * (1.0 / jnp.sum(e, axis=0, keepdims=True))
                PR[rows_of(g * KEYS, KEYS), cp] = pr.astype(bf)
        tiles = []
        for g in gs:
            cols = []
            for p in range(D // 128):
                cp = slice(128 * p, 128 * p + 128)
                v2 = window(g, slice(D + 128 * p, D + 128 * p + 128))
                cols.append(own_columns(tn(PR[rows_of(g * KEYS, KEYS), cp], v2)))
            tiles.append(jnp.concatenate(cols, axis=1))
        att = jnp.concatenate(tiles, axis=0).astype(bf)
        ATTT[:, rows_of(i * TT, TT, 128)] = att.T
        DYT[:, rows_of(i * TT, TT, 128)] = DY[r, :].T
        mid = X[r, :].astype(f32) + nn(att, wo[...])
        MID[r, :] = mid
        xhat, _r = standardise(mid)
        n2 = (xhat * gain2 + bias2).astype(bf)
        N2[r, :] = n2
        N2T[:, rows_of(i * TT, TT, 128)] = n2.T
        return 0

    lax.fori_loop(0, T // TT, attend, 0)

    loads[4].wait()
    loads[5].wait()
    keep_mid = pltpu.make_async_copy(MID, mid_h, bsem.at[NC])
    keep_mid.start()

    def keep_act(c, i, r):
        return pltpu.make_async_copy(ACT.at[r], acts_h.at[c, r], asem.at[i])

    for c in range(NC):
        cs = slice(c * FFC, (c + 1) * FFC)

        def ffn(i, _, c=c, cs=cs):
            slots(i, T // TT)

            r = rows_of(i * TT, TT)
            h = nn(N2[r, :], wu[:, cs])
            da = nt(DY[r, :], wd[cs, :])
            phi = 0.5 + 0.5 * lax.erf(h * 0.7071067811865476)
            slope = phi + h * (jnp.exp(h * h * -0.5) * 0.3989422804014327)
            d = (da * slope).astype(bf)
            if c:
                keep_act(c - 1, i, r).wait()
            ACT[r, :] = (h * phi).astype(bf)
            keep_act(c, i, r).start()
            DH[r, :] = d
            d2 = nt(d, wu[:, cs])
            if c:
                D2[r, :] += d2
            else:
                D2[r, :] = d2
            return 0

        lax.fori_loop(0, T // TT, ffn, 0)
        U[c] = nn(DYT[...], ACT[...]).astype(bf)
        reduce_unit(c, ORDER[2 * c])
        slot()
        U[NC + c] = nn(N2T[...], DH[...]).astype(bf)
        reduce_unit(NC + c, ORDER[2 * c + 1])
        slot()

    def back_mid(i, _):
        slots(i, T // TT)

        r = rows_of(i * TT, TT)
        d2 = D2[r, :]
        xhat, rstd = standardise(MID[r, :])
        SMALL[2:3, :] += jnp.sum(d2 * xhat, axis=0, keepdims=True)
        SMALL[3:4, :] += jnp.sum(d2, axis=0, keepdims=True)
        dmid = DY[r, :].astype(f32) + norm_grad(d2, xhat, rstd, gain2)
        D2[r, :] = dmid
        db = dmid.astype(bf)
        keep_act(NC - 1, i, r).wait()
        ACT[r, :] = db
        DH[r, :] = nt(db, wo[...]).astype(bf)
        return 0

    lax.fori_loop(0, T // TT, back_mid, 0)
    U[2 * NC] = nn(ATTT[...], ACT[...]).astype(bf)
    reduce_unit(2 * NC, ORDER[2 * NC])

    homes = [DY.at[0:T], PR.at[0:T], PR.at[T : 2 * T], DH.at[0:T]]
    fetches = [
        pltpu.make_async_copy(acts_h.at[c], homes[c], bsem.at[c]) for c in range(NC)
    ]
    fetches.append(pltpu.make_async_copy(mid_h, MID, bsem.at[NC]))
    fetches[0].start()
    keep_mid.wait()

    for h in range(2):
        c = slice(256 * h, 256 * h + 256)
        cv = slice(D + 256 * h, D + 256 * h + 256)
        OUT[...] = jnp.zeros_like(OUT)
        give_left = remote(2 + 2 * h, SNL.at[h], HRL.at[h], left)
        give_right = remote(3 + 2 * h, SNR.at[h], HRR.at[h], right)

        def back_att(i, _, h=h, c=c, cv=cv, give_left=give_left, give_right=give_right):
            slots(i, NG // GI)

            gs = [lax.rem(i * GI + j + NG - 1, NG) for j in range(GI)]
            half = slice(0, 256)
            for j, g in enumerate(gs):
                o4 = spread_heads(DH[rows_of(g * GROUP, GROUP), c])
                MID[GI * KEYS + KEYS * j : GI * KEYS + KEYS * j + KEYS, half] = nt(window(g, cv), o4)
            for j, g in enumerate(gs):
                for p in range(2):
                    cp = slice(128 * p, 128 * p + 128)
                    cg = slice(256 * h + 128 * p, 256 * h + 128 * p + 128)
                    pf = PR[rows_of(g * KEYS, KEYS), cg].astype(f32)
                    t = pf * MID[GI * KEYS + KEYS * j : GI * KEYS + KEYS * j + KEYS, cp]
                    ds = t - pf * jnp.sum(t, axis=0, keepdims=True)
                    ACT[KEYS * j : KEYS * j + KEYS, cp] = ds.astype(bf)
            for j, g in enumerate(gs):
                k4 = window(g, c)
                for p in range(2):
                    cp = slice(128 * p, 128 * p + 128)
                    dq = own_columns(tn(ACT[KEYS * j : KEYS * j + KEYS, cp], k4[:, cp]))
                    ACT[GROUP * j : GROUP * j + GROUP, 256 + 128 * p : 384 + 128 * p] = (
                        dq * HEAD_DIM**-0.5
                    ).astype(bf)
            for j, g in enumerate(gs):
                qr = rows_of(g * GROUP, GROUP)
                MID[KEYS * j : KEYS * j + KEYS, 0:256] = nn(
                    ACT[KEYS * j : KEYS * j + KEYS, half], spread_heads(Q[qr, c])
                )
                MID[KEYS * j : KEYS * j + KEYS, 256:512] = nn(
                    PR[rows_of(g * KEYS, KEYS), c], spread_heads(DH[qr, c])
                )
            for j, g in enumerate(gs):
                win = rows_of(g * GROUP, 112)
                mem = rows_of(g * MEMROWS, MEMROWS)
                Q[rows_of(g * GROUP, GROUP), c] = ACT[GROUP * j : GROUP * j + GROUP, 256:512]
                MW[mem, c] = MID[KEYS * j : KEYS * j + MEMROWS, 0:256].astype(bf)
                MW[mem, cv] = MID[KEYS * j : KEYS * j + MEMROWS, 256:512].astype(bf)
                OUT[win, :] += MID[KEYS * j + MEMROWS : KEYS * j + KEYS, :]

            @pl.when(i == 0)
            def _():
                SNL[h, 0:FRONT, :] = OUT[0:FRONT, :].astype(bf)
                SNL[h, FRONT : FRONT + 16, 0:256] = MW[0:16, c]
                SNL[h, FRONT : FRONT + 16, 256:512] = MW[0:16, cv]
                SNR[h] = OUT[T + FRONT : T + FRONT + 16, :].astype(bf)
                give_left.start()
                give_right.start()

            return 0

        lax.fori_loop(0, NG // GI, back_att, 0)
        if h:
            for fetch in fetches[1:]:
                fetch.start()
        at = 768 * h
        N2T[:, at : at + 256] = nn(NT_[...], Q[:, c]).astype(bf)
        give_left.wait()
        give_right.wait()
        live_l = jnp.where(me < ntm - 1, 1.0, 0.0).astype(f32)
        live_r = jnp.where(me > 0, 1.0, 0.0).astype(f32)
        OUT[T : T + FRONT, :] += HRL[h, 0:FRONT, :].astype(f32) * live_l
        OUT[FRONT : FRONT + 16, :] += HRR[h].astype(f32) * live_r
        pick = jnp.where(
            (iota((NS, 16), 0) == iota((NS, 16), 1) + NS - 4) & (iota((NS, 16), 1) < 4), 1.0, 0.0
        ).astype(bf)
        dmw = jnp.concatenate([MW[:, c], MW[:, cv]], axis=1)
        dmk = tn(SEL[:, 0:NS], dmw) + nn(pick, HRL[h, FRONT : FRONT + 16, :]) * live_l
        N2[NS * h : NS * h + NS, :] = dmk.astype(bf)

        def to_low(i, _, c=c, cv=cv):
            r = rows_of(i * TT + FRONT, TT)
            KV[r, c] = OUT[r, 0:256].astype(bf)
            KV[r, cv] = OUT[r, 256:512].astype(bf)
            return 0

        lax.fori_loop(0, T // TT, to_low, 0)
        own = slice(FRONT, T + FRONT)
        N2T[:, at + 256 : at + 512] = (
            nn(NT_[...], KV[own, c]) + tn(SUMM[0:NS, :], N2[NS * h : NS * h + NS, 0:256])
        ).astype(bf)
        N2T[:, at + 512 : at + 768] = (
            nn(NT_[...], KV[own, cv]) + tn(SUMM[0:NS, :], N2[NS * h : NS * h + NS, 256:512])
        ).astype(bf)
        reduce_block(
            nu + h, ORDER[2 * NC + 1 + h],
            lambda r, c, at=at: N2T.at[r, pl.ds(at + c.start, c.size)],
            lambda r, c, h=h: UQR.at[h, r, c],
            768,
        )
        slot()

    dsum = jnp.zeros((NS, D), f32)
    for h in range(2):
        for k in range(2):
            lo = D * (1 + k) + 256 * h
            dsum += nt(N2[NS * h : NS * h + NS, 256 * k : 256 * k + 256], wqkv[:, lo : lo + 256])
    N2[2 * NS : 3 * NS, :] = (dsum * (1.0 / SEG)).astype(bf)
    widen = jnp.where(
        jnp.right_shift(iota((TT, NM), 0), 4) == iota((TT, NM), 1), 1.0, 0.0
    ).astype(bf)

    def back_in(i, _):
        slots(i, T // TT)

        r = rows_of(i * TT, TT)
        rk = rows_of(i * TT + FRONT, TT)
        dn = nt(Q[r, :], wqkv[:, :D]) + nt(KV[rk, :], wqkv[:, D:])
        dn = dn + nn(widen, N2[rows_of(i * NM + 2 * NS, NM), :])
        xhat, rstd = standardise(X[r, :].astype(f32))
        SMALL[0:1, :] += jnp.sum(dn * xhat, axis=0, keepdims=True)
        SMALL[1:2, :] += jnp.sum(dn, axis=0, keepdims=True)
        D2[r, :] += norm_grad(dn, xhat, rstd, gain1)
        give_back(i, r).start()
        return 0

    def give_back(i, r):
        return pltpu.make_async_copy(D2.at[r], gframes_h.at[r], asem.at[i])

    lax.fori_loop(0, T // TT, back_in, 0)

    small_stages, base, sem = [], 0, 0
    for stage in [[0]] + [[1 + b for b in stage] for stage in kinds["q"]]:
        some = [axes[a] for a in stage]
        rank = sum(bit * 2**j for j, (bit, _) in enumerate(some))
        peers = [
            flipped([a for j, a in enumerate(some) if (m >> j) & 1]) for m in range(1, 1 << len(some))
        ]
        small_stages.append((base + rank, base, 1 << len(some), peers, sem))
        base, sem = base + (1 << len(some)), sem + len(peers)

    def small_copies(k):
        mine, _, _, peers, sem = small_stages[k]
        return [
            pltpu.make_async_remote_copy(
                src_ref=SMR.at[mine], dst_ref=SMR.at[mine], send_sem=xssem.at[sem + q],
                recv_sem=xrsem.at[sem + q], device_id=peer, device_id_type=MESH,
            )
            for q, peer in enumerate(peers)
        ]

    def small_step(k):
        if 0 < k <= len(small_stages):
            for copy in small_copies(k - 1):
                copy.wait()
            _, base, count, _, _ = small_stages[k - 1]
            total = SMR[base]
            for q in range(1, count):
                total = total + SMR[base + q]
            SMALL[...] = total
        if k < len(small_stages):
            SMR[small_stages[k][0]] = SMALL[...]
            for copy in small_copies(k):
                copy.start()

    small_step(0)

    for fetch in fetches:
        fetch.wait()

    def put_out(i, r):
        return pltpu.make_async_copy(N2.at[r], out_h.at[r], bsem.at[i])

    def down(i, _):
        slots(i, T // TT)
        for k in range(1, T // TT):

            @pl.when(i == k)
            def _(k=k):
                small_step(k)

        r = rows_of(i * TT, TT)
        total = MID[r, :]
        for c, home in enumerate(homes):
            total = total + nn(home[r, :], wd[c * FFC : (c + 1) * FFC, :])
        N2[r, :] = total.astype(bf)
        put_out(i, r).start()
        return 0

    lax.fori_loop(0, T // TT, down, 0)
    for k in range(T // TT, len(small_stages) + 1):
        small_step(k)
    store_s = pltpu.make_async_copy(SMALL, small_h, osem.at[4])
    store_s.start()
    while active:
        slot(True)
    store_u = pltpu.make_async_copy(U, units_h, osem.at[2])
    store_q = pltpu.make_async_copy(N2T.at[:, 0 : 3 * D], uqkv_h, osem.at[3])
    store_u.start()
    store_q.start()
    for i in range(T // TT):
        r = pl.ds(i * TT, TT)
        give_back(i, r).wait()
        put_out(i, r).wait()
    for store in (store_u, store_q, store_s):
        store.wait()


def finish(gd, gu, go, gq, out, gframes, small, gd_o, gu_o, go_o, gq_o, out_o, gframes_o, *vectors):
    for k, vector in enumerate(vectors):
        vector[...] = small[k : k + 1, :]
    gd_o[...] = gd[0].astype(f32).T
    gu_o[...] = gu[0].astype(f32)
    go_o[...] = go[0].astype(f32)
    for h in range(2):
        for p in range(3):
            gq_o[:, 512 * p + 256 * h : 512 * p + 256 * h + 256] = gq[
                :, 768 * h + 256 * p : 768 * h + 256 * p + 256
            ].astype(f32)
    out_o[...] = out[...]
    gframes_o[...] = gframes[...]


def local(frames, lens, wqkv, wo, wu, wd, ga, ba, gf, bfn, dy):
    T, D = frames.shape[1:]
    FF = wu.shape[1]
    NU = lens.shape[1]
    NG, NS = T // GROUP, T // SEG
    NC = FF // FFC
    ntm = lax.axis_size("tm")
    levels = ntm.bit_length()
    nu = 2 * NC + 1
    V = pl.BlockSpec(memory_space=pltpu.VMEM)
    A = pl.BlockSpec(memory_space=pl.ANY)
    vm = lambda *s: pltpu.VMEM(s[:-1], s[-1])
    dma = lambda *s: pltpu.SemaphoreType.DMA(s)
    land, sems = 0, 0
    for kind in schemes(levels - 1).values():
        need = Reduction.landing([1] + [len(stage) for stage in kind], D)
        land, sems = max(land, need[0]), max(sems, need[1])
    scratch = [
        vm(T, D, bf), vm(T, D, bf), vm(D, 3 * D, bf), vm(D, D, bf), vm(D, FF, bf), vm(FF, D, bf),
        vm(T, D, bf), vm(T + FRONT + 16, 2 * D, bf), vm(NG * 16, 2 * D, bf),
        vm(D, T, bf), vm(NS, D, bf), vm(D, T, bf), vm(NG * KEYS, D, bf),
        vm(T, D, f32), vm(T, D, bf), vm(D, T, bf), vm(D, T, bf),
        vm(T + FRONT + 16, D, f32), vm(T, D, f32), vm(T, FFC, bf), vm(T, FFC, bf),
        vm(NG * 16, NS, bf), vm(KEYS, 128, f32), vm(NG, 8, 128, f32),
        vm(80, D, bf),
        vm(2, 48, D, bf), vm(2, 16, D, bf), vm(2, 48, D, bf), vm(2, 16, D, bf),
        vm(nu, D, D, bf), vm(nu, land, D, bf), vm(2, land, 768, bf),
        vm(8, D, f32), vm(2 * levels, 8, D, f32),
        dma(6), dma(5), dma(6), dma(6),
        dma(2 * nu + 4, sems), dma(2 * nu + 4, sems), dma(2 * levels), dma(2 * levels),
        pltpu.SemaphoreType.REGULAR((2 * nu + 4, levels)), dma(T // TT), dma(max(NC + 1, T // TT)),
    ]
    row = lambda v: v.reshape(1, D)
    out, gframes, units, uqkv, small, _, _ = pl.pallas_call(
        functools.partial(body, ntm, (T, D, FF, NU)),
        out_shape=[
            jax.ShapeDtypeStruct((T, D), bf),
            jax.ShapeDtypeStruct((T, D), f32),
            jax.ShapeDtypeStruct((nu, D, D), bf),
            jax.ShapeDtypeStruct((D, 3 * D), bf),
            jax.ShapeDtypeStruct((8, D), f32),
            jax.ShapeDtypeStruct((NC, T, FFC), bf),
            jax.ShapeDtypeStruct((T, D), f32),
        ],
        in_specs=[A] * 6 + [V] * 5,
        out_specs=[A] * 7,
        scratch_shapes=scratch,
        compiler_params=pltpu.CompilerParams(
            vmem_limit_bytes=64 * 2**20 - 2**18, collective_id=0, has_side_effects=True
        ),
    )(frames[0], dy[0], wqkv, wo, wu, wd, lens, row(ga), row(ba), row(gf), row(bfn))
    parts = FFC // 512
    steps = NC * parts
    part, tile = D // steps, T // steps
    spec = lambda shape, index: pl.BlockSpec(shape, index)
    down, up, gout, gqkv, out, gframes, *vectors = pl.pallas_call(
        finish,
        grid=(steps,),
        out_shape=[
            jax.ShapeDtypeStruct((FF, D), f32),
            jax.ShapeDtypeStruct((D, FF), f32),
            jax.ShapeDtypeStruct((D, D), f32),
            jax.ShapeDtypeStruct((D, 3 * D), f32),
            jax.ShapeDtypeStruct((T, D), bf),
            jax.ShapeDtypeStruct((T, D), f32),
        ]
        + [jax.ShapeDtypeStruct((1, D), f32)] * 4,
        in_specs=[
            spec((1, D, 512), lambda k: (k // parts, 0, k % parts)),
            spec((1, D, 512), lambda k: (NC + k // parts, 0, k % parts)),
            spec((1, part, D), lambda k: (2 * NC, k, 0)),
            spec((part, 3 * D), lambda k: (k, 0)),
            spec((tile, D), lambda k: (k, 0)),
            spec((tile, D), lambda k: (k, 0)),
            spec((8, D), lambda k: (0, 0)),
        ],
        out_specs=[
            spec((512, D), lambda k: (k, 0)),
            spec((D, 512), lambda k: (0, k)),
            spec((part, D), lambda k: (k, 0)),
            spec((part, 3 * D), lambda k: (k, 0)),
            spec((tile, D), lambda k: (k, 0)),
            spec((tile, D), lambda k: (k, 0)),
        ]
        + [spec((1, D), lambda k: (0, 0))] * 4,
        compiler_params=pltpu.CompilerParams(vmem_limit_bytes=62 * 2**20),
    )(units, units, units, uqkv, out, gframes, small)
    return (
        out[None], gframes[None], gqkv, gout, up, down,
        *[v.reshape(D) for v in vectors],
    )


def solution(mesh):
    big, rep = P("rows", "tm", None), P()
    return jax.shard_map(
        local,
        mesh=mesh,
        in_specs=(big, P("rows", None)) + (rep,) * 8 + (big,),
        out_specs=(big, big) + (rep,) * 8,
        check_vma=False,
    )
```

```python
import functools

import jax
import jax.numpy as jnp
from jax import lax
from jax.experimental import pallas as pl
from jax.experimental.pallas import tpu as pltpu
from jax.sharding import PartitionSpec as P

HEAD_DIM = 64
SEG = 16
GROUP = 64
KEYS = 128
MEMROWS = 16
FRONT = 32
EPS = 1e-05
FFC = 512
TT = 512
GI = TT // GROUP
bf = jnp.bfloat16
f32 = jnp.float32
MESH = pl.DeviceIdType.MESH
ORDER = ["01"] * 9 + ["qqq", "qqq"]
ENDS = [[2], [2]]
SPREAD = [1.5, 1.4, 1.2, 1.0, 1.5, 1.4, 1.2, 1.0, 1.0, 1.0, 1.0]
GAPS = {
    "0": [1, 4, 3, 3, 4, 3, 3, 4, 1],
    "p": [1, 5, 3, 3, 3, 5, 1],
    "q": [1, 4, 3, 3, 4, 1],
}


def nn(a, b):
    return jnp.dot(a, b, preferred_element_type=f32)


def nt(a, b):
    return lax.dot_general(a, b, (((1,), (1,)), ((), ())), preferred_element_type=f32)


def tn(a, b):
    return lax.dot_general(a, b, (((0,), (0,)), ((), ())), preferred_element_type=f32)


def iota(shape, dim):
    return lax.broadcasted_iota(jnp.int32, shape, dim)


def standardise(x):
    mu = jnp.mean(x, axis=-1, keepdims=True)
    xc = x - mu
    rstd = lax.rsqrt(jnp.mean(xc * xc, axis=-1, keepdims=True) + EPS)
    return xc * rstd, rstd


def norm_grad(d, xhat, rstd, gain):
    g = d * gain
    return rstd * (
        g
        - jnp.mean(g, axis=-1, keepdims=True)
        - xhat * jnp.mean(g * xhat, axis=-1, keepdims=True)
    )


def rows_of(start, size, step=16):
    return pl.ds(pl.multiple_of(start, step), size)


def spread_heads(x):
    lane = iota((1, 256), 1) // HEAD_DIM
    return jnp.concatenate(
        [jnp.where(lane == h, x, jnp.zeros_like(x)) for h in range(4)], axis=0
    )


def own_columns(a):
    return jnp.where(iota((1, 128), 1) < HEAD_DIM, a[:GROUP], a[GROUP:])


class Reduction:
    def __init__(self, stages, rows, own, got, sems, gaps, store):
        self.own, self.got, self.store = own, got, store
        self.ssem, self.rsem, self.freed = sems
        self.gaps = gaps
        self.pos, self.rest = 0, 0.0
        self.levels = []
        lo, size, at, sem = 0, rows, 0, 0
        for n, axes in enumerate(stages):
            k = len(axes)
            split = size % (16 << k) == 0 and (k > 1 or n < len(stages) - 1)
            part = size >> k if split else size
            rank = sum(bit * 2**j for j, (bit, _) in enumerate(axes))
            peers = []
            for m in range(1, 1 << k):
                flip = [(m >> j) & 1 for j in range(k)]
                other = sum(
                    (1 - bit if f else bit) * 2**j for j, (f, (bit, _)) in enumerate(zip(flip, axes))
                )
                dev = {}
                for f, (bit, (axis, here, step)) in zip(flip, axes):
                    if f:
                        dev[axis] = dev.get(axis, here) + (1 - 2 * bit) * step
                peers.append((dev, other))
            mine = lo + rank * part if split else lo
            self.levels.append((peers, lo, mine, part, at, sem, split))
            lo, size = mine, part
            at += part * len(peers)
            sem += 2 * len(peers)
        self.steps = [(i, True) for i in range(len(stages))]
        self.steps += [(i, False) for i in reversed(range(len(stages))) if self.levels[i][6]]

    @staticmethod
    def landing(stages, rows):
        size, at, sem = rows, 0, 0
        for n, k in enumerate(stages):
            split = size % (16 << k) == 0 and (k > 1 or n < len(stages) - 1)
            size = size >> k if split else size
            at += size * ((1 << k) - 1)
            sem += 2 * ((1 << k) - 1)
        return at, sem

    def copies(self, k):
        i, inward = self.steps[k]
        peers, lo, mine, part, at, sem, split = self.levels[i]
        made = []
        for q, (dev, other) in enumerate(peers):
            if inward:
                src = self.own(lo + other * part if split else lo, part)
                dst = self.got(at + q * part, part)
            else:
                src = dst = self.own(mine, part)
            z = sem + 2 * q + (0 if inward else 1)
            made.append(
                pltpu.make_async_remote_copy(
                    src_ref=src, dst_ref=dst, send_sem=self.ssem.at[z], recv_sem=self.rsem.at[z],
                    device_id=dev, device_id_type=MESH,
                )
            )
        return made

    def finish(self, k):
        for copy in self.copies(k):
            copy.wait()
        i, inward = self.steps[k]
        if inward:
            peers, _, mine, part, at, _, split = self.levels[i]
            if split:
                for dev, _other in peers:
                    pl.semaphore_signal(
                        self.freed.at[i], inc=1, device_id=dev, device_id_type=MESH
                    )
            view = self.own(mine, part)
            total = view[...]
            for q in range(len(peers)):
                total = total + self.got(at + q * part, part)[...]
            view[...] = total

    def advance(self):
        if self.pos:
            self.finish(self.pos - 1)
        if self.pos < len(self.steps):
            i, inward = self.steps[self.pos]
            if not inward:
                pl.semaphore_wait(self.freed.at[i], len(self.levels[i][0]))
            for copy in self.copies(self.pos):
                copy.start()
            self.rest += self.gaps[min(self.pos, len(self.gaps) - 1)]
        self.pos += 1
        return self.pos > len(self.steps)


def schemes(bits):
    low, high = list(range(min(2, bits))), list(range(2, bits))
    one = lambda order: [[b] for b in order]
    return {
        "0": one(low + high),
        "1": one(low[::-1] + high),
        "2": one(high + low),
        "3": one(high + low[::-1]),
        "p": [low] + one(high),
        "q": [low] + [high[i : i + 2] for i in range(0, len(high), 2)],
    }


def body(ntm, dims, *refs):
    T, D, FF, NU = dims
    NG = T // GROUP
    NS = T // SEG
    NC = FF // FFC
    nu = 2 * NC + 1
    (
        frames_h, dy_h, wqkv_h, wo_h, wu_h, wd_h, lens, ga, ba, gf, bfn,
        out_h, gframes_h, units_h, uqkv_h, small_h, acts_h, mid_h,
        X, DY, wqkv, wo, wu, wd,
        Q, KV, MW, NT_, SUMM, ATTT, PR, MID, N2, N2T, DYT, OUT, D2, ACT, DH,
        SEL, KR, LOHI, HX, HRL, HRR, SNL, SNR, U, UR, UQR, SMALL, SMR,
        lsem, osem, ssem, rsem, ussem, ursem, xssem, xrsem, freed, asem, bsem,
    ) = refs
    me, row_id = lax.axis_index("tm"), lax.axis_index("rows")
    right = lax.rem(me + 1, ntm)
    left = lax.rem(me + ntm - 1, ntm)

    loads = [
        pltpu.make_async_copy(src, dst, lsem.at[k])
        for k, (src, dst) in enumerate(
            [(frames_h, X), (wqkv_h, wqkv), (dy_h, DY), (wo_h, wo), (wu_h, wu), (wd_h, wd)]
        )
    ]
    for load in loads[:2]:
        load.start()

    bits = ntm.bit_length() - 1
    axes = [(row_id, ("rows", row_id, 1))]
    for b in range(bits):
        axes.append((lax.rem(lax.div(me, 2**b), 2), ("tm", me, 2**b)))

    def flipped(which):
        dev = {}
        for bit, (axis, here, step) in which:
            dev[axis] = dev.get(axis, here) + (1 - 2 * bit) * step
        return dev

    barrier = pltpu.get_barrier_semaphore()
    others = [{"tm": left}, {"tm": right}] + [flipped([a]) for a in axes]
    low = axes[1:3]
    others += [flipped(low)] if len(low) == 2 else []
    others += [flipped(axes[i : i + 2]) for i in range(3, bits, 2)]
    for other in others:
        pl.semaphore_signal(barrier, inc=1, device_id=other, device_id_type=MESH)

    def remote(k, src, dst, to):
        return pltpu.make_async_remote_copy(
            src_ref=src, dst_ref=dst, send_sem=ssem.at[k], recv_sem=rsem.at[k],
            device_id={"tm": to}, device_id_type=MESH,
        )

    kinds = schemes(bits)
    active, stored = [], []

    def reduction(k, kind, rows, own, got, store, spread):
        stages = [[axes[0]]] + [[axes[1 + b] for b in stage] for stage in kinds[kind]]
        gaps = [spread * gap for gap in GAPS.get(kind, GAPS["0"])]
        active.append(Reduction(stages, rows, own, got, (ussem.at[k], ursem.at[k], freed.at[k]), gaps, store))

    def slot(every=False):
        for red in list(active):
            red.rest -= 1
            if (red.rest <= 0.01 or every) and red.advance():
                active.remove(red)
                red.store.start()
                stored.append(red.store)

    def slots(i, count):
        for k in range(count):
            if active:

                @pl.when(i == k)
                def _():
                    slot()

    def reduce_unit(k, kind):
        for part, order in enumerate(kind):
            cols = pl.ds(part * (D // len(kind)), D // len(kind))
            reduction(
                2 * k + part, order, D,
                lambda lo, n, cols=cols: U.at[k, rows_of(lo, n), cols],
                lambda lo, n, cols=cols: UR.at[k, pl.ds(lo, n), cols],
                pltpu.make_async_copy(
                    U.at[k, :, cols], units_h.at[k, :, cols], osem.at[2 * k + part]
                ),
                SPREAD[k],
            )

    def reduce_part(h, p):
        if p not in ENDS[h]:
            return
        first = max([e + 1 for e in ENDS[h] if e < p], default=0)
        k, at, n256 = 2 * nu + 3 * h + p, 768 * h + 256 * first, 256 * (p + 1 - first)
        reduction(
            k, ORDER[2 * NC + 1 + h][p], D,
            lambda lo, n: N2T.at[rows_of(lo, n), at : at + n256],
            lambda lo, n: UQR.at[h, lo : lo + n, 256 * first : 256 * first + n256],
            pltpu.make_async_copy(
                N2T.at[:, at : at + n256], uqkv_h.at[:, at : at + n256], osem.at[k]
            ),
            SPREAD[2 * NC + 1 + h],
        )

    for load in loads[:2]:
        load.wait()
    for load in loads[2:]:
        load.start()
    gain1, bias1 = ga[...], ba[...]
    NM = TT // SEG
    mean16 = jnp.where(
        iota((NM, TT), 0) == jnp.right_shift(iota((NM, TT), 1), 4), 1.0 / SEG, 0.0
    ).astype(bf)

    def project(i, _):
        r = rows_of(i * TT, TT)
        xhat, _r = standardise(X[r, :].astype(f32))
        nb = (xhat * gain1 + bias1).astype(bf)
        NT_[:, rows_of(i * TT, TT, 128)] = nb.T
        SUMM[rows_of(i * NM, NM), :] = nn(mean16, nb).astype(bf)
        Q[r, :] = (nn(nb, wqkv[:, :D]) * HEAD_DIM**-0.5).astype(bf)
        KV[rows_of(i * TT + FRONT, TT), :] = nn(nb, wqkv[:, D:]).astype(bf)
        return 0

    lax.fori_loop(0, T // TT, project, 0)

    pl.semaphore_wait(barrier, len(others))
    to_right = remote(0, frames_h.at[T - 64 : T], HX.at[0:64], right)
    to_left = remote(1, frames_h.at[0:16], HX.at[64:80], left)
    to_right.start()
    to_left.start()

    for b in range(NU // 128):
        u = iota((128, 128), 0) + 128 * b
        first = jnp.zeros((128, 1), f32)
        last = jnp.zeros((128, 1), f32)
        for c in range(NU // 128):
            v = iota((128, 128), 1) + 128 * c
            n = lens[:, 128 * c : 128 * c + 128].astype(f32)
            first = first + jnp.sum(jnp.where(v < u, n, 0.0), axis=1, keepdims=True)
            last = last + jnp.sum(jnp.where(v <= u, n, 0.0), axis=1, keepdims=True)
        MID[128 * b : 128 * b + 128, 0:128] = jnp.broadcast_to(first, (128, 128))
        MID[128 * b : 128 * b + 128, 128:256] = jnp.broadcast_to(last, (128, 128))
    row = iota((KEYS, 128), 0)
    seg_q = (iota((KEYS, 128), 1) % GROUP) // SEG
    pos = row - MEMROWS
    mem_ok = (row < 8) & (seg_q <= row) & (row <= seg_q + 3)
    near_ok = (pos >= SEG * seg_q + 2) & (pos < SEG * seg_q + 52)
    rel = jnp.where(row < MEMROWS, row - 4, jnp.right_shift(pos, 4) - 2)
    KR[...] = jnp.where(
        jnp.where(row < MEMROWS, mem_ok.astype(jnp.int32), near_ok.astype(jnp.int32)) > 0,
        rel.astype(f32), -1e9,
    )

    def bounds(g, _):
        base = (me * NS + 4 * g).astype(f32)
        seg = base + ((iota((1, 128), 1) % GROUP) // SEG).astype(f32)
        st, en = MID[0:NU, 0:128], MID[0:NU, 128:256]
        lo = jnp.max(jnp.where(st <= seg, st, -1.0), axis=0, keepdims=True) - base
        hi = jnp.min(jnp.where(en > seg, en, 1e9), axis=0, keepdims=True) - base
        LOHI[g] = jnp.where(iota((8, 128), 0) == 0, lo, hi)
        return 0

    lax.fori_loop(0, NG, bounds, 0)
    rows, cols = iota((NG * 16, NS), 0), iota((NG * 16, NS), 1)
    seg = 4 * jnp.right_shift(rows, 4) - 4 + (rows & 15)
    SEL[...] = jnp.where(((rows & 15) < 8) & (seg == cols), 1.0, 0.0).astype(bf)
    SMALL[...] = jnp.zeros_like(SMALL)

    MW[...] = nn(SEL[...], nn(SUMM[...], wqkv[:, D:]).astype(bf)).astype(bf)

    def edges():
        to_right.wait()
        to_left.wait()
        xhat, _r = standardise(HX[...].astype(f32))
        nb = (xhat * gain1 + bias1).astype(bf)
        edge = nn(nb, wqkv[:, D:]).astype(bf)
        KV[0:FRONT, :] = edge[32:64]
        KV[T + FRONT : T + FRONT + 16, :] = edge[64:80]
        mem = nn(nn(mean16[:16, :64], nb[:64]).astype(bf), wqkv[:, D:])
        now = MW[0:16, :].astype(f32)
        MW[0:16, :] = jnp.where(iota((16, 1), 0) < 4, mem, now).astype(bf)

    loads[2].wait()
    loads[3].wait()
    gain2, bias2 = gf[...], bfn[...]

    def window(g, c):
        win = rows_of(g * GROUP, 112)
        mem = rows_of(g * MEMROWS, MEMROWS)
        return jnp.concatenate([MW[mem, c], KV[win, c]], axis=0)

    def attend(step, _):
        @pl.when(step == T // TT - 2)
        def _():
            edges()

        i = lax.rem(step + 1, T // TT)
        r = rows_of(i * TT, TT)
        gs = [i * GI + j for j in range(GI)]
        for j, g in enumerate(gs):
            for h in range(2):
                c = slice(256 * h, 256 * h + 256)
                q4 = spread_heads(Q[rows_of(g * GROUP, GROUP), c])
                OUT[KEYS * j : KEYS * j + KEYS, c] = nt(window(g, c), q4)
        for j, g in enumerate(gs):
            lo, hi = LOHI[g, 0:1, :], LOHI[g, 1:2, :]
            kr = KR[...]
            ok = (kr >= lo) & (kr < hi)
            for p in range(D // 128):
                cp = slice(128 * p, 128 * p + 128)
                s = jnp.where(ok, OUT[KEYS * j : KEYS * j + KEYS, cp], -1e30)
                e = jnp.exp(s - jnp.max(s, axis=0, keepdims=True))
                pr = e * (1.0 / jnp.sum(e, axis=0, keepdims=True))
                PR[rows_of(g * KEYS, KEYS), cp] = pr.astype(bf)
        tiles = []
        for g in gs:
            cols = []
            for p in range(D // 128):
                cp = slice(128 * p, 128 * p + 128)
                v2 = window(g, slice(D + 128 * p, D + 128 * p + 128))
                cols.append(own_columns(tn(PR[rows_of(g * KEYS, KEYS), cp], v2)))
            tiles.append(jnp.concatenate(cols, axis=1))
        att = jnp.concatenate(tiles, axis=0).astype(bf)
        ATTT[:, rows_of(i * TT, TT, 128)] = att.T
        DYT[:, rows_of(i * TT, TT, 128)] = DY[r, :].T
        mid = X[r, :].astype(f32) + nn(att, wo[...])
        MID[r, :] = mid
        xhat, _r = standardise(mid)
        n2 = (xhat * gain2 + bias2).astype(bf)
        N2[r, :] = n2
        N2T[:, rows_of(i * TT, TT, 128)] = n2.T
        return 0

    lax.fori_loop(0, T // TT, attend, 0)

    loads[4].wait()
    loads[5].wait()
    keep_mid = pltpu.make_async_copy(MID, mid_h, bsem.at[NC])
    keep_mid.start()

    def keep_act(c, i, r):
        return pltpu.make_async_copy(ACT.at[r], acts_h.at[c, r], asem.at[i])

    for c in range(NC):
        cs = slice(c * FFC, (c + 1) * FFC)

        def ffn(i, _, c=c, cs=cs):
            slots(i, T // TT)
            r = rows_of(i * TT, TT)
            if c:
                keep_act(c - 1, i, r).wait()
            h = nn(N2[r, :], wu[:, cs])
            da = nt(DY[r, :], wd[cs, :])
            phi = 0.5 + 0.5 * lax.erf(h * 0.7071067811865476)
            slope = phi + h * (jnp.exp(h * h * -0.5) * 0.3989422804014327)
            d = (da * slope).astype(bf)
            ACT[r, :] = (h * phi).astype(bf)
            DH[r, :] = d
            d2 = nt(d, wu[:, cs])
            if c:
                D2[r, :] += d2
            else:
                D2[r, :] = d2
            keep_act(c, i, r).start()
            return 0

        lax.fori_loop(0, T // TT, ffn, 0)
        U[c] = nn(DYT[...], ACT[...]).astype(bf)
        reduce_unit(c, ORDER[2 * c])
        slot()
        U[NC + c] = nn(N2T[...], DH[...]).astype(bf)
        reduce_unit(NC + c, ORDER[2 * c + 1])
        slot()

    def back_mid(i, _):
        slots(i, T // TT)

        r = rows_of(i * TT, TT)
        keep_act(NC - 1, i, r).wait()
        d2 = D2[r, :]
        xhat, rstd = standardise(MID[r, :])
        SMALL[2:3, :] += jnp.sum(d2 * xhat, axis=0, keepdims=True)
        SMALL[3:4, :] += jnp.sum(d2, axis=0, keepdims=True)
        dmid = DY[r, :].astype(f32) + norm_grad(d2, xhat, rstd, gain2)
        D2[r, :] = dmid
        db = dmid.astype(bf)
        ACT[r, :] = db
        DH[r, :] = nt(db, wo[...]).astype(bf)
        return 0

    lax.fori_loop(0, T // TT, back_mid, 0)
    U[2 * NC] = nn(ATTT[...], ACT[...]).astype(bf)
    reduce_unit(2 * NC, ORDER[2 * NC])

    homes = [DY.at[0:T], PR.at[0:T], PR.at[T : 2 * T], DH.at[0:T]]
    fetches = [
        pltpu.make_async_copy(acts_h.at[c], homes[c], bsem.at[c]) for c in range(NC)
    ]
    fetches.append(pltpu.make_async_copy(mid_h, MID, bsem.at[NC]))
    fetches[0].start()
    keep_mid.wait()

    for h in range(2):
        c = slice(256 * h, 256 * h + 256)
        cv = slice(D + 256 * h, D + 256 * h + 256)
        OUT[...] = jnp.zeros_like(OUT)
        give_left = remote(2 + 2 * h, SNL.at[h], HRL.at[h], left)
        give_right = remote(3 + 2 * h, SNR.at[h], HRR.at[h], right)

        def back_att(i, _, h=h, c=c, cv=cv, give_left=give_left, give_right=give_right):
            slots(i, NG // GI)

            gs = [lax.rem(i * GI + j + NG - 1, NG) for j in range(GI)]
            half = slice(0, 256)
            for j, g in enumerate(gs):
                o4 = spread_heads(DH[rows_of(g * GROUP, GROUP), c])
                MID[GI * KEYS + KEYS * j : GI * KEYS + KEYS * j + KEYS, half] = nt(window(g, cv), o4)
            for j, g in enumerate(gs):
                for p in range(2):
                    cp = slice(128 * p, 128 * p + 128)
                    cg = slice(256 * h + 128 * p, 256 * h + 128 * p + 128)
                    pf = PR[rows_of(g * KEYS, KEYS), cg].astype(f32)
                    t = pf * MID[GI * KEYS + KEYS * j : GI * KEYS + KEYS * j + KEYS, cp]
                    ds = t - pf * jnp.sum(t, axis=0, keepdims=True)
                    ACT[KEYS * j : KEYS * j + KEYS, cp] = ds.astype(bf)
            for j, g in enumerate(gs):
                k4 = window(g, c)
                for p in range(2):
                    cp = slice(128 * p, 128 * p + 128)
                    dq = own_columns(tn(ACT[KEYS * j : KEYS * j + KEYS, cp], k4[:, cp]))
                    ACT[GROUP * j : GROUP * j + GROUP, 256 + 128 * p : 384 + 128 * p] = (
                        dq * HEAD_DIM**-0.5
                    ).astype(bf)
            for j, g in enumerate(gs):
                qr = rows_of(g * GROUP, GROUP)
                MID[KEYS * j : KEYS * j + KEYS, 0:256] = nn(
                    ACT[KEYS * j : KEYS * j + KEYS, half], spread_heads(Q[qr, c])
                )
                MID[KEYS * j : KEYS * j + KEYS, 256:512] = nn(
                    PR[rows_of(g * KEYS, KEYS), c], spread_heads(DH[qr, c])
                )
            for j, g in enumerate(gs):
                win = rows_of(g * GROUP, 112)
                mem = rows_of(g * MEMROWS, MEMROWS)
                Q[rows_of(g * GROUP, GROUP), c] = ACT[GROUP * j : GROUP * j + GROUP, 256:512]
                MW[mem, c] = MID[KEYS * j : KEYS * j + MEMROWS, 0:256].astype(bf)
                MW[mem, cv] = MID[KEYS * j : KEYS * j + MEMROWS, 256:512].astype(bf)
                OUT[win, :] += MID[KEYS * j + MEMROWS : KEYS * j + KEYS, :]

            @pl.when(i == 0)
            def _():
                SNL[h, 0:FRONT, :] = OUT[0:FRONT, :].astype(bf)
                SNL[h, FRONT : FRONT + 16, 0:256] = MW[0:16, c]
                SNL[h, FRONT : FRONT + 16, 256:512] = MW[0:16, cv]
                SNR[h] = OUT[T + FRONT : T + FRONT + 16, :].astype(bf)
                give_left.start()
                give_right.start()

            return 0

        lax.fori_loop(0, NG // GI, back_att, 0)
        if h:
            for fetch in fetches[1:]:
                fetch.start()
        at = 768 * h
        N2T[:, at : at + 256] = nn(NT_[...], Q[:, c]).astype(bf)
        reduce_part(h, 0)
        slot()
        give_left.wait()
        give_right.wait()
        live_l = jnp.where(me < ntm - 1, 1.0, 0.0).astype(f32)
        live_r = jnp.where(me > 0, 1.0, 0.0).astype(f32)
        OUT[T : T + FRONT, :] += HRL[h, 0:FRONT, :].astype(f32) * live_l
        OUT[FRONT : FRONT + 16, :] += HRR[h].astype(f32) * live_r
        pick = jnp.where(
            (iota((NS, 16), 0) == iota((NS, 16), 1) + NS - 4) & (iota((NS, 16), 1) < 4), 1.0, 0.0
        ).astype(bf)
        dmw = jnp.concatenate([MW[:, c], MW[:, cv]], axis=1)
        dmk = tn(SEL[:, 0:NS], dmw) + nn(pick, HRL[h, FRONT : FRONT + 16, :]) * live_l
        N2[NS * h : NS * h + NS, :] = dmk.astype(bf)

        def to_low(i, _, c=c, cv=cv):
            r = rows_of(i * TT + FRONT, TT)
            KV[r, c] = OUT[r, 0:256].astype(bf)
            KV[r, cv] = OUT[r, 256:512].astype(bf)
            return 0

        lax.fori_loop(0, T // TT, to_low, 0)
        own = slice(FRONT, T + FRONT)
        N2T[:, at + 256 : at + 512] = (
            nn(NT_[...], KV[own, c]) + tn(SUMM[0:NS, :], N2[NS * h : NS * h + NS, 0:256])
        ).astype(bf)
        reduce_part(h, 1)
        slot()
        N2T[:, at + 512 : at + 768] = (
            nn(NT_[...], KV[own, cv]) + tn(SUMM[0:NS, :], N2[NS * h : NS * h + NS, 256:512])
        ).astype(bf)
        reduce_part(h, 2)
        slot()

    dsum = jnp.zeros((NS, D), f32)
    for h in range(2):
        for k in range(2):
            lo = D * (1 + k) + 256 * h
            dsum += nt(N2[NS * h : NS * h + NS, 256 * k : 256 * k + 256], wqkv[:, lo : lo + 256])
    N2[2 * NS : 3 * NS, :] = (dsum * (1.0 / SEG)).astype(bf)
    widen = jnp.where(
        jnp.right_shift(iota((TT, NM), 0), 4) == iota((TT, NM), 1), 1.0, 0.0
    ).astype(bf)

    def back_in(i, _):
        slots(i, T // TT)

        r = rows_of(i * TT, TT)
        rk = rows_of(i * TT + FRONT, TT)
        dn = nt(Q[r, :], wqkv[:, :D]) + nt(KV[rk, :], wqkv[:, D:])
        dn = dn + nn(widen, N2[rows_of(i * NM + 2 * NS, NM), :])
        xhat, rstd = standardise(X[r, :].astype(f32))
        SMALL[0:1, :] += jnp.sum(dn * xhat, axis=0, keepdims=True)
        SMALL[1:2, :] += jnp.sum(dn, axis=0, keepdims=True)
        D2[r, :] += norm_grad(dn, xhat, rstd, gain1)
        give_back(i, r).start()
        return 0

    def give_back(i, r):
        return pltpu.make_async_copy(D2.at[r], gframes_h.at[r], asem.at[i])

    lax.fori_loop(0, T // TT, back_in, 0)

    small_stages, base, sem = [], 0, 0
    for stage in [[0]] + [[1 + b for b in stage] for stage in kinds["q"]]:
        some = [axes[a] for a in stage]
        rank = sum(bit * 2**j for j, (bit, _) in enumerate(some))
        peers = [
            flipped([a for j, a in enumerate(some) if (m >> j) & 1]) for m in range(1, 1 << len(some))
        ]
        small_stages.append((base + rank, base, 1 << len(some), peers, sem))
        base, sem = base + (1 << len(some)), sem + len(peers)

    def small_copies(k):
        mine, _, _, peers, sem = small_stages[k]
        return [
            pltpu.make_async_remote_copy(
                src_ref=SMR.at[mine], dst_ref=SMR.at[mine], send_sem=xssem.at[sem + q],
                recv_sem=xrsem.at[sem + q], device_id=peer, device_id_type=MESH,
            )
            for q, peer in enumerate(peers)
        ]

    def small_step(k):
        if 0 < k <= len(small_stages):
            for copy in small_copies(k - 1):
                copy.wait()
            _, base, count, _, _ = small_stages[k - 1]
            total = SMR[base]
            for q in range(1, count):
                total = total + SMR[base + q]
            SMALL[...] = total
        if k < len(small_stages):
            SMR[small_stages[k][0]] = SMALL[...]
            for copy in small_copies(k):
                copy.start()

    small_step(0)

    for fetch in fetches:
        fetch.wait()

    def put_out(i, r):
        return pltpu.make_async_copy(N2.at[r], out_h.at[r], bsem.at[i])

    def down(i, _):
        slots(i, T // TT)
        for k in range(1, T // TT):

            @pl.when(i == k)
            def _(k=k):
                small_step(k)

        r = rows_of(i * TT, TT)
        total = MID[r, :]
        for c, home in enumerate(homes):
            total = total + nn(home[r, :], wd[c * FFC : (c + 1) * FFC, :])
        N2[r, :] = total.astype(bf)
        put_out(i, r).start()
        return 0

    lax.fori_loop(0, T // TT, down, 0)
    for k in range(T // TT, len(small_stages) + 1):
        small_step(k)
    store_s = pltpu.make_async_copy(SMALL, small_h, osem.at[2 * nu + 6])
    store_s.start()
    while active:
        slot(True)
    for i in range(T // TT):
        r = pl.ds(i * TT, TT)
        give_back(i, r).wait()
        put_out(i, r).wait()
    for store in stored + [store_s]:
        store.wait()


def finish(gd, gu, go, gq, out, gframes, small, gd_o, gu_o, go_o, gq_o, out_o, gframes_o, *vectors):
    for k, vector in enumerate(vectors):
        vector[...] = small[k : k + 1, :]
    gd_o[...] = gd[0].astype(f32).T
    gu_o[...] = gu[0].astype(f32)
    go_o[...] = go[0].astype(f32)
    for h in range(2):
        for p in range(3):
            gq_o[:, 512 * p + 256 * h : 512 * p + 256 * h + 256] = gq[
                :, 768 * h + 256 * p : 768 * h + 256 * p + 256
            ].astype(f32)
    out_o[...] = out[...]
    gframes_o[...] = gframes[...]


def local(frames, lens, wqkv, wo, wu, wd, ga, ba, gf, bfn, dy):
    T, D = frames.shape[1:]
    FF = wu.shape[1]
    NU = lens.shape[1]
    NG, NS = T // GROUP, T // SEG
    NC = FF // FFC
    ntm = lax.axis_size("tm")
    levels = ntm.bit_length()
    nu = 2 * NC + 1
    V = pl.BlockSpec(memory_space=pltpu.VMEM)
    A = pl.BlockSpec(memory_space=pl.ANY)
    vm = lambda *s: pltpu.VMEM(s[:-1], s[-1])
    dma = lambda *s: pltpu.SemaphoreType.DMA(s)
    land, sems = 0, 0
    for kind in schemes(levels - 1).values():
        need = Reduction.landing([1] + [len(stage) for stage in kind], D)
        land, sems = max(land, need[0]), max(sems, need[1])
    scratch = [
        vm(T, D, bf), vm(T, D, bf), vm(D, 3 * D, bf), vm(D, D, bf), vm(D, FF, bf), vm(FF, D, bf),
        vm(T, D, bf), vm(T + FRONT + 16, 2 * D, bf), vm(NG * 16, 2 * D, bf),
        vm(D, T, bf), vm(NS, D, bf), vm(D, T, bf), vm(NG * KEYS, D, bf),
        vm(T, D, f32), vm(T, D, bf), vm(D, T, bf), vm(D, T, bf),
        vm(T + FRONT + 16, D, f32), vm(T, D, f32), vm(T, FFC, bf), vm(T, FFC, bf),
        vm(NG * 16, NS, bf), vm(KEYS, 128, f32), vm(NG, 8, 128, f32),
        vm(80, D, bf),
        vm(2, 48, D, bf), vm(2, 16, D, bf), vm(2, 48, D, bf), vm(2, 16, D, bf),
        vm(nu, D, D, bf), vm(nu, land, D, bf), vm(2, land, 768, bf),
        vm(8, D, f32), vm(2 * levels, 8, D, f32),
        dma(6), dma(2 * nu + 7), dma(6), dma(6),
        dma(2 * nu + 6, sems), dma(2 * nu + 6, sems), dma(2 * levels), dma(2 * levels),
        pltpu.SemaphoreType.REGULAR((2 * nu + 6, levels)), dma(T // TT), dma(max(NC + 1, T // TT)),
    ]
    row = lambda v: v.reshape(1, D)
    out, gframes, units, uqkv, small, _, _ = pl.pallas_call(
        functools.partial(body, ntm, (T, D, FF, NU)),
        out_shape=[
            jax.ShapeDtypeStruct((T, D), bf),
            jax.ShapeDtypeStruct((T, D), f32),
            jax.ShapeDtypeStruct((nu, D, D), bf),
            jax.ShapeDtypeStruct((D, 3 * D), bf),
            jax.ShapeDtypeStruct((8, D), f32),
            jax.ShapeDtypeStruct((NC, T, FFC), bf),
            jax.ShapeDtypeStruct((T, D), f32),
        ],
        in_specs=[A] * 6 + [V] * 5,
        out_specs=[A] * 7,
        scratch_shapes=scratch,
        compiler_params=pltpu.CompilerParams(
            vmem_limit_bytes=64 * 2**20 - 2**18, collective_id=0, has_side_effects=True
        ),
    )(frames[0], dy[0], wqkv, wo, wu, wd, lens, row(ga), row(ba), row(gf), row(bfn))
    steps = NC
    part, tile = D // steps, T // steps
    spec = lambda shape, index: pl.BlockSpec(shape, index)
    down, up, gout, gqkv, out, gframes, *vectors = pl.pallas_call(
        finish,
        grid=(steps,),
        out_shape=[
            jax.ShapeDtypeStruct((FF, D), f32),
            jax.ShapeDtypeStruct((D, FF), f32),
            jax.ShapeDtypeStruct((D, D), f32),
            jax.ShapeDtypeStruct((D, 3 * D), f32),
            jax.ShapeDtypeStruct((T, D), bf),
            jax.ShapeDtypeStruct((T, D), f32),
        ]
        + [jax.ShapeDtypeStruct((1, D), f32)] * 4,
        in_specs=[
            spec((1, D, D), lambda k: (k, 0, 0)),
            spec((1, D, D), lambda k: (NC + k, 0, 0)),
            spec((1, part, D), lambda k: (2 * NC, k, 0)),
            spec((part, 3 * D), lambda k: (k, 0)),
            spec((tile, D), lambda k: (k, 0)),
            spec((tile, D), lambda k: (k, 0)),
            spec((8, D), lambda k: (0, 0)),
        ],
        out_specs=[
            spec((FFC, D), lambda k: (k, 0)),
            spec((D, FFC), lambda k: (0, k)),
            spec((part, D), lambda k: (k, 0)),
            spec((part, 3 * D), lambda k: (k, 0)),
            spec((tile, D), lambda k: (k, 0)),
            spec((tile, D), lambda k: (k, 0)),
        ]
        + [spec((1, D), lambda k: (0, 0))] * 4,
        compiler_params=pltpu.CompilerParams(vmem_limit_bytes=62 * 2**20),
    )(units, units, units, uqkv, out, gframes, small)
    return (
        out[None], gframes[None], gqkv, gout, up, down,
        *[v.reshape(D) for v in vectors],
    )


def solution(mesh):
    big, rep = P("rows", "tm", None), P()
    return jax.shard_map(
        local,
        mesh=mesh,
        in_specs=(big, P("rows", None)) + (rep,) * 8 + (big,),
        out_specs=(big, big) + (rep,) * 8,
        check_vma=False,
    )
```

```python
import functools

import jax
import jax.numpy as jnp
from jax import lax
from jax.experimental import pallas as pl
from jax.experimental.pallas import tpu as pltpu
from jax.sharding import PartitionSpec as P

HEAD_DIM = 64
SEG = 16
GROUP = 64
KEYS = 128
MEMROWS = 16
FRONT = 32
EPS = 1e-05
FFC = 512
TT = 512
GI = TT // GROUP
bf = jnp.bfloat16
f32 = jnp.float32
MESH = pl.DeviceIdType.MESH
ORDER = ["01", "02", "01", "01", "01", "12", "01", "01", "01", "qqq", "qqq"]
ENDS = [[2], [2]]
SPREAD = [1.3, 1.3, 1.2, 1.0, 1.3, 1.3, 1.2, 1.0, 1.0, 1.0, 1.0]
GAPS = {
    "0": [1, 4, 3, 3, 4, 3, 3, 4, 1],
    "p": [1, 5, 3, 3, 3, 5, 1],
    "q": [1, 4, 3, 3, 4, 1],
}


def nn(a, b):
    return jnp.dot(a, b, preferred_element_type=f32)


def nt(a, b):
    return lax.dot_general(a, b, (((1,), (1,)), ((), ())), preferred_element_type=f32)


def tn(a, b):
    return lax.dot_general(a, b, (((0,), (0,)), ((), ())), preferred_element_type=f32)


def iota(shape, dim):
    return lax.broadcasted_iota(jnp.int32, shape, dim)


def standardise(x):
    mu = jnp.mean(x, axis=-1, keepdims=True)
    xc = x - mu
    rstd = lax.rsqrt(jnp.mean(xc * xc, axis=-1, keepdims=True) + EPS)
    return xc * rstd, rstd


def norm_grad(d, xhat, rstd, gain):
    g = d * gain
    return rstd * (
        g
        - jnp.mean(g, axis=-1, keepdims=True)
        - xhat * jnp.mean(g * xhat, axis=-1, keepdims=True)
    )


def rows_of(start, size, step=16):
    return pl.ds(pl.multiple_of(start, step), size)


def spread_heads(x):
    lane = iota((1, 256), 1) // HEAD_DIM
    return jnp.concatenate(
        [jnp.where(lane == h, x, jnp.zeros_like(x)) for h in range(4)], axis=0
    )


def own_columns(a):
    return jnp.where(iota((1, 128), 1) < HEAD_DIM, a[:GROUP], a[GROUP:])


class Reduction:
    def __init__(self, stages, rows, own, got, sems, gaps, store):
        self.own, self.got, self.store = own, got, store
        self.ssem, self.rsem, self.freed = sems
        self.gaps = gaps
        self.pos, self.rest = 0, 0.0
        self.levels = []
        lo, size, at, sem = 0, rows, 0, 0
        for n, axes in enumerate(stages):
            k = len(axes)
            split = size % (16 << k) == 0 and (k > 1 or n < len(stages) - 1)
            part = size >> k if split else size
            rank = sum(bit * 2**j for j, (bit, _) in enumerate(axes))
            peers = []
            for m in range(1, 1 << k):
                flip = [(m >> j) & 1 for j in range(k)]
                other = sum(
                    (1 - bit if f else bit) * 2**j for j, (f, (bit, _)) in enumerate(zip(flip, axes))
                )
                dev = {}
                for f, (bit, (axis, here, step)) in zip(flip, axes):
                    if f:
                        dev[axis] = dev.get(axis, here) + (1 - 2 * bit) * step
                peers.append((dev, other))
            mine = lo + rank * part if split else lo
            self.levels.append((peers, lo, mine, part, at, sem, split))
            lo, size = mine, part
            at += part * len(peers)
            sem += 2 * len(peers)
        self.steps = [(i, True) for i in range(len(stages))]
        self.steps += [(i, False) for i in reversed(range(len(stages))) if self.levels[i][6]]

    @staticmethod
    def landing(stages, rows):
        size, at, sem = rows, 0, 0
        for n, k in enumerate(stages):
            split = size % (16 << k) == 0 and (k > 1 or n < len(stages) - 1)
            size = size >> k if split else size
            at += size * ((1 << k) - 1)
            sem += 2 * ((1 << k) - 1)
        return at, sem

    def copies(self, k):
        i, inward = self.steps[k]
        peers, lo, mine, part, at, sem, split = self.levels[i]
        made = []
        for q, (dev, other) in enumerate(peers):
            if inward:
                src = self.own(lo + other * part if split else lo, part)
                dst = self.got(at + q * part, part)
            else:
                src = dst = self.own(mine, part)
            z = sem + 2 * q + (0 if inward else 1)
            made.append(
                pltpu.make_async_remote_copy(
                    src_ref=src, dst_ref=dst, send_sem=self.ssem.at[z], recv_sem=self.rsem.at[z],
                    device_id=dev, device_id_type=MESH,
                )
            )
        return made

    def finish(self, k):
        for copy in self.copies(k):
            copy.wait()
        i, inward = self.steps[k]
        if inward:
            peers, _, mine, part, at, _, split = self.levels[i]
            if split:
                for dev, _other in peers:
                    pl.semaphore_signal(
                        self.freed.at[i], inc=1, device_id=dev, device_id_type=MESH
                    )
            view = self.own(mine, part)
            total = view[...]
            for q in range(len(peers)):
                total = total + self.got(at + q * part, part)[...]
            view[...] = total

    def advance(self):
        if self.pos:
            self.finish(self.pos - 1)
        if self.pos < len(self.steps):
            i, inward = self.steps[self.pos]
            if not inward:
                pl.semaphore_wait(self.freed.at[i], len(self.levels[i][0]))
            for copy in self.copies(self.pos):
                copy.start()
            self.rest += self.gaps[min(self.pos, len(self.gaps) - 1)]
        self.pos += 1
        return self.pos > len(self.steps)


def schemes(bits):
    low, high = list(range(min(2, bits))), list(range(2, bits))
    one = lambda order: [[b] for b in order]
    return {
        "0": one(low + high),
        "1": one(low[::-1] + high),
        "2": one(high + low),
        "3": one(high + low[::-1]),
        "p": [low] + one(high),
        "q": [low] + [high[i : i + 2] for i in range(0, len(high), 2)],
    }


def body(ntm, dims, *refs):
    T, D, FF, NU = dims
    NG = T // GROUP
    NS = T // SEG
    NC = FF // FFC
    nu = 2 * NC + 1
    (
        frames_h, dy_h, wqkv_h, wo_h, wu_h, wd_h, lens, ga, ba, gf, bfn,
        out_h, gframes_h, units_h, uqkv_h, small_h, acts_h, mid_h,
        X, DY, wqkv, wo, wu, wd,
        Q, KV, MW, NT_, SUMM, ATTT, PR, MID, N2, N2T, DYT, OUT, D2, ACT, DH,
        SEL, KR, LOHI, HX, HRL, HRR, SNL, SNR, U, UR, UQR, SMALL, SMR,
        lsem, osem, ssem, rsem, ussem, ursem, xssem, xrsem, freed, asem, bsem,
    ) = refs
    me, row_id = lax.axis_index("tm"), lax.axis_index("rows")
    right = lax.rem(me + 1, ntm)
    left = lax.rem(me + ntm - 1, ntm)

    loads = [
        pltpu.make_async_copy(src, dst, lsem.at[k])
        for k, (src, dst) in enumerate(
            [(frames_h, X), (wqkv_h, wqkv), (dy_h, DY), (wo_h, wo), (wu_h, wu), (wd_h, wd)]
        )
    ]
    for load in loads[:2]:
        load.start()

    bits = ntm.bit_length() - 1
    axes = [(row_id, ("rows", row_id, 1))]
    for b in range(bits):
        axes.append((lax.rem(lax.div(me, 2**b), 2), ("tm", me, 2**b)))

    def flipped(which):
        dev = {}
        for bit, (axis, here, step) in which:
            dev[axis] = dev.get(axis, here) + (1 - 2 * bit) * step
        return dev

    barrier = pltpu.get_barrier_semaphore()
    others = [{"tm": left}, {"tm": right}] + [flipped([a]) for a in axes]
    low = axes[1:3]
    others += [flipped(low)] if len(low) == 2 else []
    others += [flipped(axes[i : i + 2]) for i in range(3, bits, 2)]
    for other in others:
        pl.semaphore_signal(barrier, inc=1, device_id=other, device_id_type=MESH)

    def remote(k, src, dst, to):
        return pltpu.make_async_remote_copy(
            src_ref=src, dst_ref=dst, send_sem=ssem.at[k], recv_sem=rsem.at[k],
            device_id={"tm": to}, device_id_type=MESH,
        )

    kinds = schemes(bits)
    active, stored = [], []

    def reduction(k, kind, rows, own, got, store, spread):
        stages = [[axes[0]]] + [[axes[1 + b] for b in stage] for stage in kinds[kind]]
        gaps = [spread * gap for gap in GAPS.get(kind, GAPS["0"])]
        active.append(Reduction(stages, rows, own, got, (ussem.at[k], ursem.at[k], freed.at[k]), gaps, store))

    def slot(every=False):
        for red in list(active):
            red.rest -= 1
            if (red.rest <= 0.01 or every) and red.advance():
                active.remove(red)
                red.store.start()
                stored.append(red.store)

    def slots(i, count):
        for k in range(count):
            if active:

                @pl.when(i == k)
                def _():
                    slot()

    def reduce_unit(k, kind):
        for part, order in enumerate(kind):
            cols = pl.ds(part * (D // len(kind)), D // len(kind))
            reduction(
                2 * k + part, order, D,
                lambda lo, n, cols=cols: U.at[k, rows_of(lo, n), cols],
                lambda lo, n, cols=cols: UR.at[k, pl.ds(lo, n), cols],
                pltpu.make_async_copy(
                    U.at[k, :, cols], units_h.at[k, :, cols], osem.at[2 * k + part]
                ),
                SPREAD[k],
            )

    def reduce_part(h, p):
        if p not in ENDS[h]:
            return
        first = max([e + 1 for e in ENDS[h] if e < p], default=0)
        k, at, n256 = 2 * nu + 3 * h + p, 768 * h + 256 * first, 256 * (p + 1 - first)
        reduction(
            k, ORDER[2 * NC + 1 + h][p], D,
            lambda lo, n: N2T.at[rows_of(lo, n), at : at + n256],
            lambda lo, n: UQR.at[h, lo : lo + n, 256 * first : 256 * first + n256],
            pltpu.make_async_copy(
                N2T.at[:, at : at + n256], uqkv_h.at[:, at : at + n256], osem.at[k]
            ),
            SPREAD[2 * NC + 1 + h],
        )

    for load in loads[:2]:
        load.wait()
    for load in loads[2:]:
        load.start()
    gain1, bias1 = ga[...], ba[...]
    NM = TT // SEG
    mean16 = jnp.where(
        iota((NM, TT), 0) == jnp.right_shift(iota((NM, TT), 1), 4), 1.0 / SEG, 0.0
    ).astype(bf)

    def project(i, _):
        r = rows_of(i * TT, TT)
        xhat, _r = standardise(X[r, :].astype(f32))
        nb = (xhat * gain1 + bias1).astype(bf)
        NT_[:, rows_of(i * TT, TT, 128)] = nb.T
        SUMM[rows_of(i * NM, NM), :] = nn(mean16, nb).astype(bf)
        Q[r, :] = (nn(nb, wqkv[:, :D]) * HEAD_DIM**-0.5).astype(bf)
        KV[rows_of(i * TT + FRONT, TT), :] = nn(nb, wqkv[:, D:]).astype(bf)
        return 0

    lax.fori_loop(0, T // TT, project, 0)

    pl.semaphore_wait(barrier, len(others))
    to_right = remote(0, frames_h.at[T - 64 : T], HX.at[0:64], right)
    to_left = remote(1, frames_h.at[0:16], HX.at[64:80], left)
    to_right.start()
    to_left.start()

    for b in range(NU // 128):
        u = iota((128, 128), 0) + 128 * b
        first = jnp.zeros((128, 1), f32)
        last = jnp.zeros((128, 1), f32)
        for c in range(NU // 128):
            v = iota((128, 128), 1) + 128 * c
            n = lens[:, 128 * c : 128 * c + 128].astype(f32)
            first = first + jnp.sum(jnp.where(v < u, n, 0.0), axis=1, keepdims=True)
            last = last + jnp.sum(jnp.where(v <= u, n, 0.0), axis=1, keepdims=True)
        MID[128 * b : 128 * b + 128, 0:128] = jnp.broadcast_to(first, (128, 128))
        MID[128 * b : 128 * b + 128, 128:256] = jnp.broadcast_to(last, (128, 128))
    row = iota((KEYS, 128), 0)
    seg_q = (iota((KEYS, 128), 1) % GROUP) // SEG
    pos = row - MEMROWS
    mem_ok = (row < 8) & (seg_q <= row) & (row <= seg_q + 3)
    near_ok = (pos >= SEG * seg_q + 2) & (pos < SEG * seg_q + 52)
    rel = jnp.where(row < MEMROWS, row - 4, jnp.right_shift(pos, 4) - 2)
    KR[...] = jnp.where(
        jnp.where(row < MEMROWS, mem_ok.astype(jnp.int32), near_ok.astype(jnp.int32)) > 0,
        rel.astype(f32), -1e9,
    )

    def bounds(g, _):
        base = (me * NS + 4 * g).astype(f32)
        seg = base + ((iota((1, 128), 1) % GROUP) // SEG).astype(f32)
        st, en = MID[0:NU, 0:128], MID[0:NU, 128:256]
        lo = jnp.max(jnp.where(st <= seg, st, -1.0), axis=0, keepdims=True) - base
        hi = jnp.min(jnp.where(en > seg, en, 1e9), axis=0, keepdims=True) - base
        LOHI[g] = jnp.where(iota((8, 128), 0) == 0, lo, hi)
        return 0

    lax.fori_loop(0, NG, bounds, 0)
    rows, cols = iota((NG * 16, NS), 0), iota((NG * 16, NS), 1)
    seg = 4 * jnp.right_shift(rows, 4) - 4 + (rows & 15)
    SEL[...] = jnp.where(((rows & 15) < 8) & (seg == cols), 1.0, 0.0).astype(bf)
    SMALL[...] = jnp.zeros_like(SMALL)

    MW[...] = nn(SEL[...], nn(SUMM[...], wqkv[:, D:]).astype(bf)).astype(bf)

    def edges():
        to_right.wait()
        to_left.wait()
        xhat, _r = standardise(HX[...].astype(f32))
        nb = (xhat * gain1 + bias1).astype(bf)
        edge = nn(nb, wqkv[:, D:]).astype(bf)
        KV[0:FRONT, :] = edge[32:64]
        KV[T + FRONT : T + FRONT + 16, :] = edge[64:80]
        mem = nn(nn(mean16[:16, :64], nb[:64]).astype(bf), wqkv[:, D:])
        now = MW[0:16, :].astype(f32)
        MW[0:16, :] = jnp.where(iota((16, 1), 0) < 4, mem, now).astype(bf)

    loads[2].wait()
    loads[3].wait()
    gain2, bias2 = gf[...], bfn[...]

    def window(g, c):
        win = rows_of(g * GROUP, 112)
        mem = rows_of(g * MEMROWS, MEMROWS)
        return jnp.concatenate([MW[mem, c], KV[win, c]], axis=0)

    def attend(step, _):
        @pl.when(step == T // TT - 2)
        def _():
            edges()

        i = lax.rem(step + 1, T // TT)
        r = rows_of(i * TT, TT)
        gs = [i * GI + j for j in range(GI)]
        for j, g in enumerate(gs):
            for h in range(2):
                c = slice(256 * h, 256 * h + 256)
                q4 = spread_heads(Q[rows_of(g * GROUP, GROUP), c])
                OUT[KEYS * j : KEYS * j + KEYS, c] = nt(window(g, c), q4)
        for j, g in enumerate(gs):
            lo, hi = LOHI[g, 0:1, :], LOHI[g, 1:2, :]
            kr = KR[...]
            ok = (kr >= lo) & (kr < hi)
            for p in range(D // 128):
                cp = slice(128 * p, 128 * p + 128)
                s = jnp.where(ok, OUT[KEYS * j : KEYS * j + KEYS, cp], -1e30)
                e = jnp.exp(s - jnp.max(s, axis=0, keepdims=True))
                pr = e * (1.0 / jnp.sum(e, axis=0, keepdims=True))
                PR[rows_of(g * KEYS, KEYS), cp] = pr.astype(bf)
        tiles = []
        for g in gs:
            cols = []
            for p in range(D // 128):
                cp = slice(128 * p, 128 * p + 128)
                v2 = window(g, slice(D + 128 * p, D + 128 * p + 128))
                cols.append(own_columns(tn(PR[rows_of(g * KEYS, KEYS), cp], v2)))
            tiles.append(jnp.concatenate(cols, axis=1))
        att = jnp.concatenate(tiles, axis=0).astype(bf)
        ATTT[:, rows_of(i * TT, TT, 128)] = att.T
        DYT[:, rows_of(i * TT, TT, 128)] = DY[r, :].T
        mid = X[r, :].astype(f32) + nn(att, wo[...])
        MID[r, :] = mid
        xhat, _r = standardise(mid)
        n2 = (xhat * gain2 + bias2).astype(bf)
        N2[r, :] = n2
        N2T[:, rows_of(i * TT, TT, 128)] = n2.T
        return 0

    lax.fori_loop(0, T // TT, attend, 0)

    loads[4].wait()
    loads[5].wait()
    keep_mid = pltpu.make_async_copy(MID, mid_h, bsem.at[NC])
    keep_mid.start()

    def keep_act(c, i, r):
        return pltpu.make_async_copy(ACT.at[r], acts_h.at[c, r], asem.at[i])

    for c in range(NC):
        cs = slice(c * FFC, (c + 1) * FFC)

        def ffn(i, _, c=c, cs=cs):
            slots(i, T // TT)
            r = rows_of(i * TT, TT)
            if c:
                keep_act(c - 1, i, r).wait()
            h = nn(N2[r, :], wu[:, cs])
            da = nt(DY[r, :], wd[cs, :])
            phi = 0.5 + 0.5 * lax.erf(h * 0.7071067811865476)
            slope = phi + h * (jnp.exp(h * h * -0.5) * 0.3989422804014327)
            d = (da * slope).astype(bf)
            ACT[r, :] = (h * phi).astype(bf)
            DH[r, :] = d
            d2 = nt(d, wu[:, cs])
            if c:
                D2[r, :] += d2
            else:
                D2[r, :] = d2
            keep_act(c, i, r).start()
            return 0

        lax.fori_loop(0, T // TT, ffn, 0)
        U[c] = nn(DYT[...], ACT[...]).astype(bf)
        reduce_unit(c, ORDER[2 * c])
        slot()
        U[NC + c] = nn(N2T[...], DH[...]).astype(bf)
        reduce_unit(NC + c, ORDER[2 * c + 1])
        slot()

    def back_mid(i, _):
        slots(i, T // TT)

        r = rows_of(i * TT, TT)
        keep_act(NC - 1, i, r).wait()
        d2 = D2[r, :]
        xhat, rstd = standardise(MID[r, :])
        SMALL[2:3, :] += jnp.sum(d2 * xhat, axis=0, keepdims=True)
        SMALL[3:4, :] += jnp.sum(d2, axis=0, keepdims=True)
        dmid = DY[r, :].astype(f32) + norm_grad(d2, xhat, rstd, gain2)
        D2[r, :] = dmid
        db = dmid.astype(bf)
        ACT[r, :] = db
        DH[r, :] = nt(db, wo[...]).astype(bf)
        return 0

    lax.fori_loop(0, T // TT, back_mid, 0)
    U[2 * NC] = nn(ATTT[...], ACT[...]).astype(bf)
    reduce_unit(2 * NC, ORDER[2 * NC])

    homes = [DY.at[0:T], PR.at[0:T], PR.at[T : 2 * T], DH.at[0:T]]
    fetches = [
        pltpu.make_async_copy(acts_h.at[c], homes[c], bsem.at[c]) for c in range(NC)
    ]
    fetches.append(pltpu.make_async_copy(mid_h, MID, bsem.at[NC]))
    fetches[0].start()
    keep_mid.wait()

    for h in range(2):
        c = slice(256 * h, 256 * h + 256)
        cv = slice(D + 256 * h, D + 256 * h + 256)
        OUT[...] = jnp.zeros_like(OUT)
        give_left = remote(2 + 2 * h, SNL.at[h], HRL.at[h], left)
        give_right = remote(3 + 2 * h, SNR.at[h], HRR.at[h], right)

        def back_att(i, _, h=h, c=c, cv=cv, give_left=give_left, give_right=give_right):
            slots(i, NG // GI)

            gs = [lax.rem(i * GI + j + NG - 1, NG) for j in range(GI)]
            half = slice(0, 256)
            for j, g in enumerate(gs):
                o4 = spread_heads(DH[rows_of(g * GROUP, GROUP), c])
                MID[GI * KEYS + KEYS * j : GI * KEYS + KEYS * j + KEYS, half] = nt(window(g, cv), o4)
            for j, g in enumerate(gs):
                for p in range(2):
                    cp = slice(128 * p, 128 * p + 128)
                    cg = slice(256 * h + 128 * p, 256 * h + 128 * p + 128)
                    pf = PR[rows_of(g * KEYS, KEYS), cg].astype(f32)
                    t = pf * MID[GI * KEYS + KEYS * j : GI * KEYS + KEYS * j + KEYS, cp]
                    ds = t - pf * jnp.sum(t, axis=0, keepdims=True)
                    ACT[KEYS * j : KEYS * j + KEYS, cp] = ds.astype(bf)
            for j, g in enumerate(gs):
                k4 = window(g, c)
                for p in range(2):
                    cp = slice(128 * p, 128 * p + 128)
                    dq = own_columns(tn(ACT[KEYS * j : KEYS * j + KEYS, cp], k4[:, cp]))
                    ACT[GROUP * j : GROUP * j + GROUP, 256 + 128 * p : 384 + 128 * p] = (
                        dq * HEAD_DIM**-0.5
                    ).astype(bf)
            for j, g in enumerate(gs):
                qr = rows_of(g * GROUP, GROUP)
                MID[KEYS * j : KEYS * j + KEYS, 0:256] = nn(
                    ACT[KEYS * j : KEYS * j + KEYS, half], spread_heads(Q[qr, c])
                )
                MID[KEYS * j : KEYS * j + KEYS, 256:512] = nn(
                    PR[rows_of(g * KEYS, KEYS), c], spread_heads(DH[qr, c])
                )
            for j, g in enumerate(gs):
                win = rows_of(g * GROUP, 112)
                mem = rows_of(g * MEMROWS, MEMROWS)
                Q[rows_of(g * GROUP, GROUP), c] = ACT[GROUP * j : GROUP * j + GROUP, 256:512]
                MW[mem, c] = MID[KEYS * j : KEYS * j + MEMROWS, 0:256].astype(bf)
                MW[mem, cv] = MID[KEYS * j : KEYS * j + MEMROWS, 256:512].astype(bf)
                OUT[win, :] += MID[KEYS * j + MEMROWS : KEYS * j + KEYS, :]

            @pl.when(i == 0)
            def _():
                SNL[h, 0:FRONT, :] = OUT[0:FRONT, :].astype(bf)
                SNL[h, FRONT : FRONT + 16, 0:256] = MW[0:16, c]
                SNL[h, FRONT : FRONT + 16, 256:512] = MW[0:16, cv]
                SNR[h] = OUT[T + FRONT : T + FRONT + 16, :].astype(bf)
                give_left.start()
                give_right.start()

            return 0

        lax.fori_loop(0, NG // GI, back_att, 0)
        if h:
            for fetch in fetches[1:]:
                fetch.start()
        at = 768 * h
        N2T[:, at : at + 256] = nn(NT_[...], Q[:, c]).astype(bf)
        reduce_part(h, 0)
        slot()
        give_left.wait()
        give_right.wait()
        live_l = jnp.where(me < ntm - 1, 1.0, 0.0).astype(f32)
        live_r = jnp.where(me > 0, 1.0, 0.0).astype(f32)
        OUT[T : T + FRONT, :] += HRL[h, 0:FRONT, :].astype(f32) * live_l
        OUT[FRONT : FRONT + 16, :] += HRR[h].astype(f32) * live_r
        pick = jnp.where(
            (iota((NS, 16), 0) == iota((NS, 16), 1) + NS - 4) & (iota((NS, 16), 1) < 4), 1.0, 0.0
        ).astype(bf)
        dmw = jnp.concatenate([MW[:, c], MW[:, cv]], axis=1)
        dmk = tn(SEL[:, 0:NS], dmw) + nn(pick, HRL[h, FRONT : FRONT + 16, :]) * live_l
        N2[NS * h : NS * h + NS, :] = dmk.astype(bf)

        def to_low(i, _, c=c, cv=cv):
            r = rows_of(i * TT + FRONT, TT)
            KV[r, c] = OUT[r, 0:256].astype(bf)
            KV[r, cv] = OUT[r, 256:512].astype(bf)
            return 0

        lax.fori_loop(0, T // TT, to_low, 0)
        own = slice(FRONT, T + FRONT)
        N2T[:, at + 256 : at + 512] = (
            nn(NT_[...], KV[own, c]) + tn(SUMM[0:NS, :], N2[NS * h : NS * h + NS, 0:256])
        ).astype(bf)
        reduce_part(h, 1)
        slot()
        N2T[:, at + 512 : at + 768] = (
            nn(NT_[...], KV[own, cv]) + tn(SUMM[0:NS, :], N2[NS * h : NS * h + NS, 256:512])
        ).astype(bf)
        reduce_part(h, 2)
        slot()

    dsum = jnp.zeros((NS, D), f32)
    for h in range(2):
        for k in range(2):
            lo = D * (1 + k) + 256 * h
            dsum += nt(N2[NS * h : NS * h + NS, 256 * k : 256 * k + 256], wqkv[:, lo : lo + 256])
    N2[2 * NS : 3 * NS, :] = (dsum * (1.0 / SEG)).astype(bf)
    widen = jnp.where(
        jnp.right_shift(iota((TT, NM), 0), 4) == iota((TT, NM), 1), 1.0, 0.0
    ).astype(bf)

    def back_in(i, _):
        slots(i, T // TT)

        r = rows_of(i * TT, TT)
        rk = rows_of(i * TT + FRONT, TT)
        dn = nt(Q[r, :], wqkv[:, :D]) + nt(KV[rk, :], wqkv[:, D:])
        dn = dn + nn(widen, N2[rows_of(i * NM + 2 * NS, NM), :])
        xhat, rstd = standardise(X[r, :].astype(f32))
        SMALL[0:1, :] += jnp.sum(dn * xhat, axis=0, keepdims=True)
        SMALL[1:2, :] += jnp.sum(dn, axis=0, keepdims=True)
        D2[r, :] += norm_grad(dn, xhat, rstd, gain1)
        give_back(i, r).start()
        return 0

    def give_back(i, r):
        return pltpu.make_async_copy(D2.at[r], gframes_h.at[r], asem.at[i])

    lax.fori_loop(0, T // TT, back_in, 0)

    small_stages, base, sem = [], 0, 0
    for stage in [[0]] + [[1 + b for b in stage] for stage in kinds["q"]]:
        some = [axes[a] for a in stage]
        rank = sum(bit * 2**j for j, (bit, _) in enumerate(some))
        peers = [
            flipped([a for j, a in enumerate(some) if (m >> j) & 1]) for m in range(1, 1 << len(some))
        ]
        small_stages.append((base + rank, base, 1 << len(some), peers, sem))
        base, sem = base + (1 << len(some)), sem + len(peers)

    def small_copies(k):
        mine, _, _, peers, sem = small_stages[k]
        return [
            pltpu.make_async_remote_copy(
                src_ref=SMR.at[mine], dst_ref=SMR.at[mine], send_sem=xssem.at[sem + q],
                recv_sem=xrsem.at[sem + q], device_id=peer, device_id_type=MESH,
            )
            for q, peer in enumerate(peers)
        ]

    def small_step(k):
        if 0 < k <= len(small_stages):
            for copy in small_copies(k - 1):
                copy.wait()
            _, base, count, _, _ = small_stages[k - 1]
            total = SMR[base]
            for q in range(1, count):
                total = total + SMR[base + q]
            SMALL[...] = total
        if k < len(small_stages):
            SMR[small_stages[k][0]] = SMALL[...]
            for copy in small_copies(k):
                copy.start()

    small_step(0)

    for fetch in fetches:
        fetch.wait()

    def put_out(i, r):
        return pltpu.make_async_copy(N2.at[r], out_h.at[r], bsem.at[i])

    def down(i, _):
        slots(i, T // TT)
        for k in range(1, T // TT):

            @pl.when(i == k)
            def _(k=k):
                small_step(k)

        r = rows_of(i * TT, TT)
        total = MID[r, :]
        for c, home in enumerate(homes):
            total = total + nn(home[r, :], wd[c * FFC : (c + 1) * FFC, :])
        N2[r, :] = total.astype(bf)
        put_out(i, r).start()
        return 0

    lax.fori_loop(0, T // TT, down, 0)
    for k in range(T // TT, len(small_stages) + 1):
        small_step(k)
    store_s = pltpu.make_async_copy(SMALL, small_h, osem.at[2 * nu + 6])
    store_s.start()
    while active:
        slot(True)
    for i in range(T // TT):
        r = pl.ds(i * TT, TT)
        give_back(i, r).wait()
        put_out(i, r).wait()
    for store in stored + [store_s]:
        store.wait()


def finish(gd, gu, go, gq, out, gframes, small, gd_o, gu_o, go_o, gq_o, out_o, gframes_o, *vectors):
    for k, vector in enumerate(vectors):
        vector[...] = small[k : k + 1, :]
    gd_o[...] = gd[0].astype(f32).T
    gu_o[...] = gu[0].astype(f32)
    go_o[...] = go[0].astype(f32)
    for h in range(2):
        for p in range(3):
            gq_o[:, 512 * p + 256 * h : 512 * p + 256 * h + 256] = gq[
                :, 768 * h + 256 * p : 768 * h + 256 * p + 256
            ].astype(f32)
    out_o[...] = out[...]
    gframes_o[...] = gframes[...]


def local(frames, lens, wqkv, wo, wu, wd, ga, ba, gf, bfn, dy):
    T, D = frames.shape[1:]
    FF = wu.shape[1]
    NU = lens.shape[1]
    NG, NS = T // GROUP, T // SEG
    NC = FF // FFC
    ntm = lax.axis_size("tm")
    levels = ntm.bit_length()
    nu = 2 * NC + 1
    V = pl.BlockSpec(memory_space=pltpu.VMEM)
    A = pl.BlockSpec(memory_space=pl.ANY)
    vm = lambda *s: pltpu.VMEM(s[:-1], s[-1])
    dma = lambda *s: pltpu.SemaphoreType.DMA(s)
    land, sems = 0, 0
    for kind in schemes(levels - 1).values():
        need = Reduction.landing([1] + [len(stage) for stage in kind], D)
        land, sems = max(land, need[0]), max(sems, need[1])
    scratch = [
        vm(T, D, bf), vm(T, D, bf), vm(D, 3 * D, bf), vm(D, D, bf), vm(D, FF, bf), vm(FF, D, bf),
        vm(T, D, bf), vm(T + FRONT + 16, 2 * D, bf), vm(NG * 16, 2 * D, bf),
        vm(D, T, bf), vm(NS, D, bf), vm(D, T, bf), vm(NG * KEYS, D, bf),
        vm(T, D, f32), vm(T, D, bf), vm(D, T, bf), vm(D, T, bf),
        vm(T + FRONT + 16, D, f32), vm(T, D, f32), vm(T, FFC, bf), vm(T, FFC, bf),
        vm(NG * 16, NS, bf), vm(KEYS, 128, f32), vm(NG, 8, 128, f32),
        vm(80, D, bf),
        vm(2, 48, D, bf), vm(2, 16, D, bf), vm(2, 48, D, bf), vm(2, 16, D, bf),
        vm(nu, D, D, bf), vm(nu, land, D, bf), vm(2, land, 768, bf),
        vm(8, D, f32), vm(2 * levels, 8, D, f32),
        dma(6), dma(2 * nu + 7), dma(6), dma(6),
        dma(2 * nu + 6, sems), dma(2 * nu + 6, sems), dma(2 * levels), dma(2 * levels),
        pltpu.SemaphoreType.REGULAR((2 * nu + 6, levels)), dma(T // TT), dma(max(NC + 1, T // TT)),
    ]
    row = lambda v: v.reshape(1, D)
    out, gframes, units, uqkv, small, _, _ = pl.pallas_call(
        functools.partial(body, ntm, (T, D, FF, NU)),
        out_shape=[
            jax.ShapeDtypeStruct((T, D), bf),
            jax.ShapeDtypeStruct((T, D), f32),
            jax.ShapeDtypeStruct((nu, D, D), bf),
            jax.ShapeDtypeStruct((D, 3 * D), bf),
            jax.ShapeDtypeStruct((8, D), f32),
            jax.ShapeDtypeStruct((NC, T, FFC), bf),
            jax.ShapeDtypeStruct((T, D), f32),
        ],
        in_specs=[A] * 6 + [V] * 5,
        out_specs=[A] * 7,
        scratch_shapes=scratch,
        compiler_params=pltpu.CompilerParams(
            vmem_limit_bytes=64 * 2**20 - 2**18, collective_id=0, has_side_effects=True
        ),
    )(frames[0], dy[0], wqkv, wo, wu, wd, lens, row(ga), row(ba), row(gf), row(bfn))
    steps = NC
    part, tile = D // steps, T // steps
    spec = lambda shape, index: pl.BlockSpec(shape, index)
    down, up, gout, gqkv, out, gframes, *vectors = pl.pallas_call(
        finish,
        grid=(steps,),
        out_shape=[
            jax.ShapeDtypeStruct((FF, D), f32),
            jax.ShapeDtypeStruct((D, FF), f32),
            jax.ShapeDtypeStruct((D, D), f32),
            jax.ShapeDtypeStruct((D, 3 * D), f32),
            jax.ShapeDtypeStruct((T, D), bf),
            jax.ShapeDtypeStruct((T, D), f32),
        ]
        + [jax.ShapeDtypeStruct((1, D), f32)] * 4,
        in_specs=[
            spec((1, D, D), lambda k: (k, 0, 0)),
            spec((1, D, D), lambda k: (NC + k, 0, 0)),
            spec((1, part, D), lambda k: (2 * NC, k, 0)),
            spec((part, 3 * D), lambda k: (k, 0)),
            spec((tile, D), lambda k: (k, 0)),
            spec((tile, D), lambda k: (k, 0)),
            spec((8, D), lambda k: (0, 0)),
        ],
        out_specs=[
            spec((FFC, D), lambda k: (k, 0)),
            spec((D, FFC), lambda k: (0, k)),
            spec((part, D), lambda k: (k, 0)),
            spec((part, 3 * D), lambda k: (k, 0)),
            spec((tile, D), lambda k: (k, 0)),
            spec((tile, D), lambda k: (k, 0)),
        ]
        + [spec((1, D), lambda k: (0, 0))] * 4,
        compiler_params=pltpu.CompilerParams(vmem_limit_bytes=62 * 2**20),
    )(units, units, units, uqkv, out, gframes, small)
    return (
        out[None], gframes[None], gqkv, gout, up, down,
        *[v.reshape(D) for v in vectors],
    )


def solution(mesh):
    big, rep = P("rows", "tm", None), P()
    return jax.shard_map(
        local,
        mesh=mesh,
        in_specs=(big, P("rows", None)) + (rep,) * 8 + (big,),
        out_specs=(big, big) + (rep,) * 8,
        check_vma=False,
    )
```

```python
import functools

import jax
import jax.numpy as jnp
from jax import lax
from jax.experimental import pallas as pl
from jax.experimental.pallas import tpu as pltpu
from jax.sharding import PartitionSpec as P

HEAD_DIM = 64
SEG = 16
GROUP = 64
KEYS = 128
MEMROWS = 16
FRONT = 32
EPS = 1e-05
FFC = 512
TT = 512
GI = TT // GROUP
bf = jnp.bfloat16
f32 = jnp.float32
MESH = pl.DeviceIdType.MESH
ORDER = ["01", "02", "01", "01", "01", "12", "01", "01", "01", "qqq", "qqq"]
ENDS = [[2], [2]]
SPREAD = [1.3, 1.3, 1.2, 1.0, 1.3, 1.3, 1.2, 1.0, 1.0, 1.0, 1.0]
GAPS = {
    "0": [1, 4, 3, 3, 4, 3, 3, 4, 1],
    "p": [1, 5, 3, 3, 3, 5, 1],
    "q": [1, 4, 3, 3, 4, 1],
}


def nn(a, b):
    return jnp.dot(a, b, preferred_element_type=f32)


def nt(a, b):
    return lax.dot_general(a, b, (((1,), (1,)), ((), ())), preferred_element_type=f32)


def tn(a, b):
    return lax.dot_general(a, b, (((0,), (0,)), ((), ())), preferred_element_type=f32)


def iota(shape, dim):
    return lax.broadcasted_iota(jnp.int32, shape, dim)


def standardise(x):
    mu = jnp.mean(x, axis=-1, keepdims=True)
    xc = x - mu
    rstd = lax.rsqrt(jnp.mean(xc * xc, axis=-1, keepdims=True) + EPS)
    return xc * rstd, rstd


def norm_grad(d, xhat, rstd, gain):
    g = d * gain
    return rstd * (
        g
        - jnp.mean(g, axis=-1, keepdims=True)
        - xhat * jnp.mean(g * xhat, axis=-1, keepdims=True)
    )


def rows_of(start, size, step=16):
    return pl.ds(pl.multiple_of(start, step), size)


def spread_heads(x):
    lane = iota((1, 256), 1) // HEAD_DIM
    return jnp.concatenate(
        [jnp.where(lane == h, x, jnp.zeros_like(x)) for h in range(4)], axis=0
    )


def own_columns(a):
    return jnp.where(iota((1, 128), 1) < HEAD_DIM, a[:GROUP], a[GROUP:])


class Reduction:
    def __init__(self, stages, rows, own, got, sems, gaps, store):
        self.own, self.got, self.store = own, got, store
        self.ssem, self.rsem, self.freed = sems
        self.gaps = gaps
        self.pos, self.rest = 0, 0.0
        self.levels = []
        lo, size, at, sem = 0, rows, 0, 0
        for n, axes in enumerate(stages):
            k = len(axes)
            split = size % (16 << k) == 0 and (k > 1 or n < len(stages) - 1)
            part = size >> k if split else size
            rank = sum(bit * 2**j for j, (bit, _) in enumerate(axes))
            peers = []
            for m in range(1, 1 << k):
                flip = [(m >> j) & 1 for j in range(k)]
                other = sum(
                    (1 - bit if f else bit) * 2**j for j, (f, (bit, _)) in enumerate(zip(flip, axes))
                )
                dev = {}
                for f, (bit, (axis, here, step)) in zip(flip, axes):
                    if f:
                        dev[axis] = dev.get(axis, here) + (1 - 2 * bit) * step
                peers.append((dev, other))
            mine = lo + rank * part if split else lo
            self.levels.append((peers, lo, mine, part, at, sem, split))
            lo, size = mine, part
            at += part * len(peers)
            sem += 2 * len(peers)
        self.steps = [(i, True) for i in range(len(stages))]
        self.steps += [(i, False) for i in reversed(range(len(stages))) if self.levels[i][6]]

    @staticmethod
    def landing(stages, rows):
        size, at, sem = rows, 0, 0
        for n, k in enumerate(stages):
            split = size % (16 << k) == 0 and (k > 1 or n < len(stages) - 1)
            size = size >> k if split else size
            at += size * ((1 << k) - 1)
            sem += 2 * ((1 << k) - 1)
        return at, sem

    def copies(self, k):
        i, inward = self.steps[k]
        peers, lo, mine, part, at, sem, split = self.levels[i]
        made = []
        for q, (dev, other) in enumerate(peers):
            if inward:
                src = self.own(lo + other * part if split else lo, part)
                dst = self.got(at + q * part, part)
            else:
                src = dst = self.own(mine, part)
            z = sem + 2 * q + (0 if inward else 1)
            made.append(
                pltpu.make_async_remote_copy(
                    src_ref=src, dst_ref=dst, send_sem=self.ssem.at[z], recv_sem=self.rsem.at[z],
                    device_id=dev, device_id_type=MESH,
                )
            )
        return made

    def finish(self, k):
        for copy in self.copies(k):
            copy.wait()
        i, inward = self.steps[k]
        if inward:
            peers, _, mine, part, at, _, split = self.levels[i]
            if split:
                for dev, _other in peers:
                    pl.semaphore_signal(
                        self.freed.at[i], inc=1, device_id=dev, device_id_type=MESH
                    )
            view = self.own(mine, part)
            total = view[...]
            for q in range(len(peers)):
                total = total + self.got(at + q * part, part)[...]
            view[...] = total

    def advance(self):
        if self.pos:
            self.finish(self.pos - 1)
        if self.pos < len(self.steps):
            i, inward = self.steps[self.pos]
            if not inward:
                pl.semaphore_wait(self.freed.at[i], len(self.levels[i][0]))
            for copy in self.copies(self.pos):
                copy.start()
            self.rest += self.gaps[min(self.pos, len(self.gaps) - 1)]
        self.pos += 1
        return self.pos > len(self.steps)


def schemes(bits):
    low, high = list(range(min(2, bits))), list(range(2, bits))
    one = lambda order: [[b] for b in order]
    return {
        "0": one(low + high),
        "1": one(low[::-1] + high),
        "2": one(high + low),
        "3": one(high + low[::-1]),
        "p": [low] + one(high),
        "q": [low] + [high[i : i + 2] for i in range(0, len(high), 2)],
    }


def body(ntm, dims, *refs):
    T, D, FF, NU = dims
    NG = T // GROUP
    NS = T // SEG
    NC = FF // FFC
    nu = 2 * NC + 1
    (
        frames_h, dy_h, wqkv_h, wo_h, wu_h, wd_h, lens, ga, ba, gf, bfn,
        out_h, gframes_h, units_h, uqkv_h, small_h, acts_h, mid_h,
        X, DY, wqkv, wo, wu, wd,
        Q, KV, MW, NT_, SUMM, ATTT, PR, MID, N2, N2T, DYT, OUT, D2, ACT, DH,
        SEL, KR, LOHI, HX, HRL, HRR, SNL, SNR, U, UR, UQR, SMALL, SMR,
        lsem, osem, ssem, rsem, ussem, ursem, xssem, xrsem, freed, asem, bsem,
    ) = refs
    me, row_id = lax.axis_index("tm"), lax.axis_index("rows")
    right = lax.rem(me + 1, ntm)
    left = lax.rem(me + ntm - 1, ntm)

    loads = [
        pltpu.make_async_copy(src, dst, lsem.at[k])
        for k, (src, dst) in enumerate(
            [(frames_h, X), (wqkv_h, wqkv), (dy_h, DY), (wo_h, wo), (wu_h, wu), (wd_h, wd)]
        )
    ]
    for load in loads[:2]:
        load.start()

    bits = ntm.bit_length() - 1
    axes = [(row_id, ("rows", row_id, 1))]
    for b in range(bits):
        axes.append((lax.rem(lax.div(me, 2**b), 2), ("tm", me, 2**b)))

    def flipped(which):
        dev = {}
        for bit, (axis, here, step) in which:
            dev[axis] = dev.get(axis, here) + (1 - 2 * bit) * step
        return dev

    barrier = pltpu.get_barrier_semaphore()
    others = [{"tm": left}, {"tm": right}] + [flipped([a]) for a in axes]
    low = axes[1:3]
    others += [flipped(low)] if len(low) == 2 else []
    others += [flipped(axes[i : i + 2]) for i in range(3, bits, 2)]
    for other in others:
        pl.semaphore_signal(barrier, inc=1, device_id=other, device_id_type=MESH)

    def remote(k, src, dst, to):
        return pltpu.make_async_remote_copy(
            src_ref=src, dst_ref=dst, send_sem=ssem.at[k], recv_sem=rsem.at[k],
            device_id={"tm": to}, device_id_type=MESH,
        )

    kinds = schemes(bits)
    active, stored = [], []

    def reduction(k, kind, rows, own, got, store, spread):
        stages = [[axes[0]]] + [[axes[1 + b] for b in stage] for stage in kinds[kind]]
        gaps = [spread * gap for gap in GAPS.get(kind, GAPS["0"])]
        active.append(Reduction(stages, rows, own, got, (ussem.at[k], ursem.at[k], freed.at[k]), gaps, store))

    def slot(every=False):
        for red in list(active):
            red.rest -= 1
            if (red.rest <= 0.01 or every) and red.advance():
                active.remove(red)
                red.store.start()
                stored.append(red.store)

    def slots(i, count):
        for k in range(count):
            if active:

                @pl.when(i == k)
                def _():
                    slot()

    def reduce_unit(k, kind):
        for part, order in enumerate(kind):
            cols = pl.ds(part * (D // len(kind)), D // len(kind))
            reduction(
                2 * k + part, order, D,
                lambda lo, n, cols=cols: U.at[k, rows_of(lo, n), cols],
                lambda lo, n, cols=cols: UR.at[k, pl.ds(lo, n), cols],
                pltpu.make_async_copy(
                    U.at[k, :, cols], units_h.at[k, :, cols], osem.at[2 * k + part]
                ),
                SPREAD[k],
            )

    def reduce_part(h, p):
        if p not in ENDS[h]:
            return
        first = max([e + 1 for e in ENDS[h] if e < p], default=0)
        k, at, n256 = 2 * nu + 3 * h + p, 768 * h + 256 * first, 256 * (p + 1 - first)
        reduction(
            k, ORDER[2 * NC + 1 + h][p], D,
            lambda lo, n: N2T.at[rows_of(lo, n), at : at + n256],
            lambda lo, n: UQR.at[h, lo : lo + n, 256 * first : 256 * first + n256],
            pltpu.make_async_copy(
                N2T.at[:, at : at + n256], uqkv_h.at[:, at : at + n256], osem.at[k]
            ),
            SPREAD[2 * NC + 1 + h],
        )

    for load in loads[:2]:
        load.wait()
    for load in loads[2:]:
        load.start()
    gain1, bias1 = ga[...], ba[...]
    NM = TT // SEG
    mean16 = jnp.where(
        iota((NM, TT), 0) == jnp.right_shift(iota((NM, TT), 1), 4), 1.0 / SEG, 0.0
    ).astype(bf)

    def project(i, _):
        r = rows_of(i * TT, TT)
        xhat, _r = standardise(X[r, :].astype(f32))
        nb = (xhat * gain1 + bias1).astype(bf)
        NT_[:, rows_of(i * TT, TT, 128)] = nb.T
        SUMM[rows_of(i * NM, NM), :] = nn(mean16, nb).astype(bf)
        Q[r, :] = (nn(nb, wqkv[:, :D]) * HEAD_DIM**-0.5).astype(bf)
        KV[rows_of(i * TT + FRONT, TT), :] = nn(nb, wqkv[:, D:]).astype(bf)
        return 0

    lax.fori_loop(0, T // TT, project, 0)

    pl.semaphore_wait(barrier, len(others))
    to_right = remote(0, frames_h.at[T - 64 : T], HX.at[0:64], right)
    to_left = remote(1, frames_h.at[0:16], HX.at[64:80], left)
    to_right.start()
    to_left.start()

    for b in range(NU // 128):
        u = iota((128, 128), 0) + 128 * b
        first = jnp.zeros((128, 1), f32)
        last = jnp.zeros((128, 1), f32)
        for c in range(NU // 128):
            v = iota((128, 128), 1) + 128 * c
            n = lens[:, 128 * c : 128 * c + 128].astype(f32)
            first = first + jnp.sum(jnp.where(v < u, n, 0.0), axis=1, keepdims=True)
            last = last + jnp.sum(jnp.where(v <= u, n, 0.0), axis=1, keepdims=True)
        MID[128 * b : 128 * b + 128, 0:128] = jnp.broadcast_to(first, (128, 128))
        MID[128 * b : 128 * b + 128, 128:256] = jnp.broadcast_to(last, (128, 128))
    row = iota((KEYS, 128), 0)
    seg_q = (iota((KEYS, 128), 1) % GROUP) // SEG
    pos = row - MEMROWS
    mem_ok = (row < 8) & (seg_q <= row) & (row <= seg_q + 3)
    near_ok = (pos >= SEG * seg_q + 2) & (pos < SEG * seg_q + 52)
    rel = jnp.where(row < MEMROWS, row - 4, jnp.right_shift(pos, 4) - 2)
    KR[...] = jnp.where(
        jnp.where(row < MEMROWS, mem_ok.astype(jnp.int32), near_ok.astype(jnp.int32)) > 0,
        rel.astype(f32), -1e9,
    )

    def bounds(g, _):
        base = (me * NS + 4 * g).astype(f32)
        seg = base + ((iota((1, 128), 1) % GROUP) // SEG).astype(f32)
        st, en = MID[0:NU, 0:128], MID[0:NU, 128:256]
        lo = jnp.max(jnp.where(st <= seg, st, -1.0), axis=0, keepdims=True) - base
        hi = jnp.min(jnp.where(en > seg, en, 1e9), axis=0, keepdims=True) - base
        LOHI[g] = jnp.where(iota((8, 128), 0) == 0, lo, hi)
        return 0

    lax.fori_loop(0, NG, bounds, 0)
    rows, cols = iota((NG * 16, NS), 0), iota((NG * 16, NS), 1)
    seg = 4 * jnp.right_shift(rows, 4) - 4 + (rows & 15)
    SEL[...] = jnp.where(((rows & 15) < 8) & (seg == cols), 1.0, 0.0).astype(bf)
    SMALL[...] = jnp.zeros_like(SMALL)

    MW[...] = nn(SEL[...], nn(SUMM[...], wqkv[:, D:]).astype(bf)).astype(bf)

    def edges():
        to_right.wait()
        to_left.wait()
        xhat, _r = standardise(HX[...].astype(f32))
        nb = (xhat * gain1 + bias1).astype(bf)
        edge = nn(nb, wqkv[:, D:]).astype(bf)
        KV[0:FRONT, :] = edge[32:64]
        KV[T + FRONT : T + FRONT + 16, :] = edge[64:80]
        mem = nn(nn(mean16[:16, :64], nb[:64]).astype(bf), wqkv[:, D:])
        now = MW[0:16, :].astype(f32)
        MW[0:16, :] = jnp.where(iota((16, 1), 0) < 4, mem, now).astype(bf)

    loads[2].wait()
    loads[3].wait()
    gain2, bias2 = gf[...], bfn[...]

    def window(g, c):
        win = rows_of(g * GROUP, 112)
        mem = rows_of(g * MEMROWS, MEMROWS)
        return jnp.concatenate([MW[mem, c], KV[win, c]], axis=0)

    def attend(step, _):
        @pl.when(step == T // TT - 2)
        def _():
            edges()

        i = lax.rem(step + 1, T // TT)
        r = rows_of(i * TT, TT)
        gs = [i * GI + j for j in range(GI)]
        for j, g in enumerate(gs):
            for h in range(2):
                c = slice(256 * h, 256 * h + 256)
                q4 = spread_heads(Q[rows_of(g * GROUP, GROUP), c])
                OUT[KEYS * j : KEYS * j + KEYS, c] = nt(window(g, c), q4)
        for j, g in enumerate(gs):
            lo, hi = LOHI[g, 0:1, :], LOHI[g, 1:2, :]
            kr = KR[...]
            ok = (kr >= lo) & (kr < hi)
            for p in range(D // 128):
                cp = slice(128 * p, 128 * p + 128)
                s = jnp.where(ok, OUT[KEYS * j : KEYS * j + KEYS, cp], -1e30)
                e = jnp.exp(s - jnp.max(s, axis=0, keepdims=True))
                pr = e * (1.0 / jnp.sum(e, axis=0, keepdims=True))
                PR[rows_of(g * KEYS, KEYS), cp] = pr.astype(bf)
        tiles = []
        for g in gs:
            cols = []
            for p in range(D // 128):
                cp = slice(128 * p, 128 * p + 128)
                v2 = window(g, slice(D + 128 * p, D + 128 * p + 128))
                cols.append(own_columns(tn(PR[rows_of(g * KEYS, KEYS), cp], v2)))
            tiles.append(jnp.concatenate(cols, axis=1))
        att = jnp.concatenate(tiles, axis=0).astype(bf)
        ATTT[:, rows_of(i * TT, TT, 128)] = att.T
        DYT[:, rows_of(i * TT, TT, 128)] = DY[r, :].T
        mid = X[r, :].astype(f32) + nn(att, wo[...])
        MID[r, :] = mid
        xhat, _r = standardise(mid)
        n2 = (xhat * gain2 + bias2).astype(bf)
        N2[r, :] = n2
        N2T[:, rows_of(i * TT, TT, 128)] = n2.T
        return 0

    lax.fori_loop(0, T // TT, attend, 0)

    loads[4].wait()
    loads[5].wait()
    keep_mid = pltpu.make_async_copy(MID, mid_h, bsem.at[NC])
    keep_mid.start()

    def keep_act(c, i, r):
        return pltpu.make_async_copy(ACT.at[r], acts_h.at[c, r], asem.at[i])

    for c in range(NC):
        cs = slice(c * FFC, (c + 1) * FFC)

        def ffn(i, _, c=c, cs=cs):
            slots(i, T // TT)
            r = rows_of(i * TT, TT)
            if c:
                keep_act(c - 1, i, r).wait()
            h = nn(N2[r, :], wu[:, cs])
            da = nt(DY[r, :], wd[cs, :])
            phi = 0.5 + 0.5 * lax.erf(h * 0.7071067811865476)
            slope = phi + h * (jnp.exp(h * h * -0.5) * 0.3989422804014327)
            d = (da * slope).astype(bf)
            ACT[r, :] = (h * phi).astype(bf)
            DH[r, :] = d
            d2 = nt(d, wu[:, cs])
            if c:
                D2[r, :] += d2
            else:
                D2[r, :] = d2
            keep_act(c, i, r).start()
            return 0

        lax.fori_loop(0, T // TT, ffn, 0)
        U[c] = nn(DYT[...], ACT[...]).astype(bf)
        reduce_unit(c, ORDER[2 * c])
        slot()
        U[NC + c] = nn(N2T[...], DH[...]).astype(bf)
        reduce_unit(NC + c, ORDER[2 * c + 1])
        slot()

    def back_mid(i, _):
        slots(i, T // TT)

        r = rows_of(i * TT, TT)
        keep_act(NC - 1, i, r).wait()
        d2 = D2[r, :]
        xhat, rstd = standardise(MID[r, :])
        SMALL[2:3, :] += jnp.sum(d2 * xhat, axis=0, keepdims=True)
        SMALL[3:4, :] += jnp.sum(d2, axis=0, keepdims=True)
        dmid = DY[r, :].astype(f32) + norm_grad(d2, xhat, rstd, gain2)
        D2[r, :] = dmid
        db = dmid.astype(bf)
        ACT[r, :] = db
        DH[r, :] = nt(db, wo[...]).astype(bf)
        return 0

    lax.fori_loop(0, T // TT, back_mid, 0)
    U[2 * NC] = nn(ATTT[...], ACT[...]).astype(bf)
    reduce_unit(2 * NC, ORDER[2 * NC])

    homes = [DY.at[0:T], PR.at[0:T], PR.at[T : 2 * T], DH.at[0:T]]
    fetches = [
        pltpu.make_async_copy(acts_h.at[c], homes[c], bsem.at[c]) for c in range(NC)
    ]
    fetches.append(pltpu.make_async_copy(mid_h, MID, bsem.at[NC]))
    fetches[0].start()
    keep_mid.wait()

    for h in range(2):
        c = slice(256 * h, 256 * h + 256)
        cv = slice(D + 256 * h, D + 256 * h + 256)
        OUT[...] = jnp.zeros_like(OUT)
        give_left = remote(2 + 2 * h, SNL.at[h], HRL.at[h], left)
        give_right = remote(3 + 2 * h, SNR.at[h], HRR.at[h], right)

        def back_att(i, _, h=h, c=c, cv=cv, give_left=give_left, give_right=give_right):
            slots(i, NG // GI)

            gs = [lax.rem(i * GI + j + NG - 1, NG) for j in range(GI)]
            half = slice(0, 256)
            for j, g in enumerate(gs):
                o4 = spread_heads(DH[rows_of(g * GROUP, GROUP), c])
                MID[GI * KEYS + KEYS * j : GI * KEYS + KEYS * j + KEYS, half] = nt(window(g, cv), o4)
            for j, g in enumerate(gs):
                for p in range(2):
                    cp = slice(128 * p, 128 * p + 128)
                    cg = slice(256 * h + 128 * p, 256 * h + 128 * p + 128)
                    pf = PR[rows_of(g * KEYS, KEYS), cg].astype(f32)
                    t = pf * MID[GI * KEYS + KEYS * j : GI * KEYS + KEYS * j + KEYS, cp]
                    ds = t - pf * jnp.sum(t, axis=0, keepdims=True)
                    ACT[KEYS * j : KEYS * j + KEYS, cp] = ds.astype(bf)
            for j, g in enumerate(gs):
                k4 = window(g, c)
                for p in range(2):
                    cp = slice(128 * p, 128 * p + 128)
                    dq = own_columns(tn(ACT[KEYS * j : KEYS * j + KEYS, cp], k4[:, cp]))
                    ACT[GROUP * j : GROUP * j + GROUP, 256 + 128 * p : 384 + 128 * p] = (
                        dq * HEAD_DIM**-0.5
                    ).astype(bf)
            for j, g in enumerate(gs):
                qr = rows_of(g * GROUP, GROUP)
                MID[KEYS * j : KEYS * j + KEYS, 0:256] = nn(
                    ACT[KEYS * j : KEYS * j + KEYS, half], spread_heads(Q[qr, c])
                )
                MID[KEYS * j : KEYS * j + KEYS, 256:512] = nn(
                    PR[rows_of(g * KEYS, KEYS), c], spread_heads(DH[qr, c])
                )
            for j, g in enumerate(gs):
                win = rows_of(g * GROUP, 112)
                mem = rows_of(g * MEMROWS, MEMROWS)
                Q[rows_of(g * GROUP, GROUP), c] = ACT[GROUP * j : GROUP * j + GROUP, 256:512]
                MW[mem, c] = MID[KEYS * j : KEYS * j + MEMROWS, 0:256].astype(bf)
                MW[mem, cv] = MID[KEYS * j : KEYS * j + MEMROWS, 256:512].astype(bf)
                OUT[win, :] += MID[KEYS * j + MEMROWS : KEYS * j + KEYS, :]

            @pl.when(i == 0)
            def _():
                SNL[h, 0:FRONT, :] = OUT[0:FRONT, :].astype(bf)
                SNL[h, FRONT : FRONT + 16, 0:256] = MW[0:16, c]
                SNL[h, FRONT : FRONT + 16, 256:512] = MW[0:16, cv]
                SNR[h] = OUT[T + FRONT : T + FRONT + 16, :].astype(bf)
                give_left.start()
                give_right.start()

            return 0

        lax.fori_loop(0, NG // GI, back_att, 0)
        if h:
            for fetch in fetches[1:]:
                fetch.start()
        at = 768 * h
        N2T[:, at : at + 256] = nn(NT_[...], Q[:, c]).astype(bf)
        reduce_part(h, 0)
        slot()
        give_left.wait()
        give_right.wait()
        live_l = jnp.where(me < ntm - 1, 1.0, 0.0).astype(f32)
        live_r = jnp.where(me > 0, 1.0, 0.0).astype(f32)
        OUT[T : T + FRONT, :] += HRL[h, 0:FRONT, :].astype(f32) * live_l
        OUT[FRONT : FRONT + 16, :] += HRR[h].astype(f32) * live_r
        pick = jnp.where(
            (iota((NS, 16), 0) == iota((NS, 16), 1) + NS - 4) & (iota((NS, 16), 1) < 4), 1.0, 0.0
        ).astype(bf)
        dmw = jnp.concatenate([MW[:, c], MW[:, cv]], axis=1)
        dmk = tn(SEL[:, 0:NS], dmw) + nn(pick, HRL[h, FRONT : FRONT + 16, :]) * live_l
        N2[NS * h : NS * h + NS, :] = dmk.astype(bf)

        def to_low(i, _, c=c, cv=cv):
            r = rows_of(i * TT + FRONT, TT)
            KV[r, c] = OUT[r, 0:256].astype(bf)
            KV[r, cv] = OUT[r, 256:512].astype(bf)
            return 0

        lax.fori_loop(0, T // TT, to_low, 0)
        own = slice(FRONT, T + FRONT)
        N2T[:, at + 256 : at + 512] = (
            nn(NT_[...], KV[own, c]) + tn(SUMM[0:NS, :], N2[NS * h : NS * h + NS, 0:256])
        ).astype(bf)
        reduce_part(h, 1)
        slot()
        N2T[:, at + 512 : at + 768] = (
            nn(NT_[...], KV[own, cv]) + tn(SUMM[0:NS, :], N2[NS * h : NS * h + NS, 256:512])
        ).astype(bf)
        reduce_part(h, 2)
        slot()

    dsum = jnp.zeros((NS, D), f32)
    for h in range(2):
        for k in range(2):
            lo = D * (1 + k) + 256 * h
            dsum += nt(N2[NS * h : NS * h + NS, 256 * k : 256 * k + 256], wqkv[:, lo : lo + 256])
    N2[2 * NS : 3 * NS, :] = (dsum * (1.0 / SEG)).astype(bf)
    widen = jnp.where(
        jnp.right_shift(iota((TT, NM), 0), 4) == iota((TT, NM), 1), 1.0, 0.0
    ).astype(bf)

    def back_in(i, _):
        slots(i, T // TT)

        r = rows_of(i * TT, TT)
        rk = rows_of(i * TT + FRONT, TT)
        dn = nt(Q[r, :], wqkv[:, :D]) + nt(KV[rk, :], wqkv[:, D:])
        dn = dn + nn(widen, N2[rows_of(i * NM + 2 * NS, NM), :])
        xhat, rstd = standardise(X[r, :].astype(f32))
        SMALL[0:1, :] += jnp.sum(dn * xhat, axis=0, keepdims=True)
        SMALL[1:2, :] += jnp.sum(dn, axis=0, keepdims=True)
        Q[r, :] = (D2[r, :] + norm_grad(dn, xhat, rstd, gain1)).astype(bf)
        give_back(i, r).start()
        return 0

    def give_back(i, r):
        return pltpu.make_async_copy(Q.at[r], gframes_h.at[r], asem.at[i])

    lax.fori_loop(0, T // TT, back_in, 0)

    small_stages, base, sem = [], 0, 0
    for stage in [[0]] + [[1 + b for b in stage] for stage in kinds["q"]]:
        some = [axes[a] for a in stage]
        rank = sum(bit * 2**j for j, (bit, _) in enumerate(some))
        peers = [
            flipped([a for j, a in enumerate(some) if (m >> j) & 1]) for m in range(1, 1 << len(some))
        ]
        small_stages.append((base + rank, base, 1 << len(some), peers, sem))
        base, sem = base + (1 << len(some)), sem + len(peers)

    def small_copies(k):
        mine, _, _, peers, sem = small_stages[k]
        return [
            pltpu.make_async_remote_copy(
                src_ref=SMR.at[mine], dst_ref=SMR.at[mine], send_sem=xssem.at[sem + q],
                recv_sem=xrsem.at[sem + q], device_id=peer, device_id_type=MESH,
            )
            for q, peer in enumerate(peers)
        ]

    def small_step(k):
        if 0 < k <= len(small_stages):
            for copy in small_copies(k - 1):
                copy.wait()
            _, base, count, _, _ = small_stages[k - 1]
            total = SMR[base]
            for q in range(1, count):
                total = total + SMR[base + q]
            SMALL[...] = total
        if k < len(small_stages):
            SMR[small_stages[k][0]] = SMALL[...]
            for copy in small_copies(k):
                copy.start()

    small_step(0)

    for fetch in fetches:
        fetch.wait()

    def put_out(i, r):
        return pltpu.make_async_copy(N2.at[r], out_h.at[r], bsem.at[i])

    def down(i, _):
        slots(i, T // TT)
        for k in range(1, T // TT):

            @pl.when(i == k)
            def _(k=k):
                small_step(k)

        r = rows_of(i * TT, TT)
        total = MID[r, :]
        for c, home in enumerate(homes):
            total = total + nn(home[r, :], wd[c * FFC : (c + 1) * FFC, :])
        N2[r, :] = total.astype(bf)
        put_out(i, r).start()
        return 0

    lax.fori_loop(0, T // TT, down, 0)
    for k in range(T // TT, len(small_stages) + 1):
        small_step(k)
    store_s = pltpu.make_async_copy(SMALL, small_h, osem.at[2 * nu + 6])
    store_s.start()
    while active:
        slot(True)
    for i in range(T // TT):
        r = pl.ds(i * TT, TT)
        give_back(i, r).wait()
        put_out(i, r).wait()
    for store in stored + [store_s]:
        store.wait()


def finish(gd, gu, go, gq, out, gframes, small, gd_o, gu_o, go_o, gq_o, out_o, gframes_o, *vectors):
    for k, vector in enumerate(vectors):
        vector[...] = small[k : k + 1, :]
    gd_o[...] = gd[0].astype(f32).T
    gu_o[...] = gu[0].astype(f32)
    go_o[...] = go[0].astype(f32)
    for h in range(2):
        for p in range(3):
            gq_o[:, 512 * p + 256 * h : 512 * p + 256 * h + 256] = gq[
                :, 768 * h + 256 * p : 768 * h + 256 * p + 256
            ].astype(f32)
    out_o[...] = out[...]
    gframes_o[...] = gframes[...].astype(f32)


def local(frames, lens, wqkv, wo, wu, wd, ga, ba, gf, bfn, dy):
    T, D = frames.shape[1:]
    FF = wu.shape[1]
    NU = lens.shape[1]
    NG, NS = T // GROUP, T // SEG
    NC = FF // FFC
    ntm = lax.axis_size("tm")
    levels = ntm.bit_length()
    nu = 2 * NC + 1
    V = pl.BlockSpec(memory_space=pltpu.VMEM)
    A = pl.BlockSpec(memory_space=pl.ANY)
    vm = lambda *s: pltpu.VMEM(s[:-1], s[-1])
    dma = lambda *s: pltpu.SemaphoreType.DMA(s)
    land, sems = 0, 0
    for kind in schemes(levels - 1).values():
        need = Reduction.landing([1] + [len(stage) for stage in kind], D)
        land, sems = max(land, need[0]), max(sems, need[1])
    scratch = [
        vm(T, D, bf), vm(T, D, bf), vm(D, 3 * D, bf), vm(D, D, bf), vm(D, FF, bf), vm(FF, D, bf),
        vm(T, D, bf), vm(T + FRONT + 16, 2 * D, bf), vm(NG * 16, 2 * D, bf),
        vm(D, T, bf), vm(NS, D, bf), vm(D, T, bf), vm(NG * KEYS, D, bf),
        vm(T, D, f32), vm(T, D, bf), vm(D, T, bf), vm(D, T, bf),
        vm(T + FRONT + 16, D, f32), vm(T, D, f32), vm(T, FFC, bf), vm(T, FFC, bf),
        vm(NG * 16, NS, bf), vm(KEYS, 128, f32), vm(NG, 8, 128, f32),
        vm(80, D, bf),
        vm(2, 48, D, bf), vm(2, 16, D, bf), vm(2, 48, D, bf), vm(2, 16, D, bf),
        vm(nu, D, D, bf), vm(nu, land, D, bf), vm(2, land, 768, bf),
        vm(8, D, f32), vm(2 * levels, 8, D, f32),
        dma(6), dma(2 * nu + 7), dma(6), dma(6),
        dma(2 * nu + 6, sems), dma(2 * nu + 6, sems), dma(2 * levels), dma(2 * levels),
        pltpu.SemaphoreType.REGULAR((2 * nu + 6, levels)), dma(T // TT), dma(max(NC + 1, T // TT)),
    ]
    row = lambda v: v.reshape(1, D)
    out, gframes, units, uqkv, small, _, _ = pl.pallas_call(
        functools.partial(body, ntm, (T, D, FF, NU)),
        out_shape=[
            jax.ShapeDtypeStruct((T, D), bf),
            jax.ShapeDtypeStruct((T, D), bf),
            jax.ShapeDtypeStruct((nu, D, D), bf),
            jax.ShapeDtypeStruct((D, 3 * D), bf),
            jax.ShapeDtypeStruct((8, D), f32),
            jax.ShapeDtypeStruct((NC, T, FFC), bf),
            jax.ShapeDtypeStruct((T, D), f32),
        ],
        in_specs=[A] * 6 + [V] * 5,
        out_specs=[A] * 7,
        scratch_shapes=scratch,
        compiler_params=pltpu.CompilerParams(
            vmem_limit_bytes=64 * 2**20 - 2**18, collective_id=0, has_side_effects=True
        ),
    )(frames[0], dy[0], wqkv, wo, wu, wd, lens, row(ga), row(ba), row(gf), row(bfn))
    steps = NC
    part, tile = D // steps, T // steps
    spec = lambda shape, index: pl.BlockSpec(shape, index)
    down, up, gout, gqkv, out, gframes, *vectors = pl.pallas_call(
        finish,
        grid=(steps,),
        out_shape=[
            jax.ShapeDtypeStruct((FF, D), f32),
            jax.ShapeDtypeStruct((D, FF), f32),
            jax.ShapeDtypeStruct((D, D), f32),
            jax.ShapeDtypeStruct((D, 3 * D), f32),
            jax.ShapeDtypeStruct((T, D), bf),
            jax.ShapeDtypeStruct((T, D), f32),
        ]
        + [jax.ShapeDtypeStruct((1, D), f32)] * 4,
        in_specs=[
            spec((1, D, D), lambda k: (k, 0, 0)),
            spec((1, D, D), lambda k: (NC + k, 0, 0)),
            spec((1, part, D), lambda k: (2 * NC, k, 0)),
            spec((part, 3 * D), lambda k: (k, 0)),
            spec((tile, D), lambda k: (k, 0)),
            spec((tile, D), lambda k: (k, 0)),
            spec((8, D), lambda k: (0, 0)),
        ],
        out_specs=[
            spec((FFC, D), lambda k: (k, 0)),
            spec((D, FFC), lambda k: (0, k)),
            spec((part, D), lambda k: (k, 0)),
            spec((part, 3 * D), lambda k: (k, 0)),
            spec((tile, D), lambda k: (k, 0)),
            spec((tile, D), lambda k: (k, 0)),
        ]
        + [spec((1, D), lambda k: (0, 0))] * 4,
        compiler_params=pltpu.CompilerParams(vmem_limit_bytes=62 * 2**20),
    )(units, units, units, uqkv, out, gframes, small)
    return (
        out[None], gframes[None], gqkv, gout, up, down,
        *[v.reshape(D) for v in vectors],
    )


def solution(mesh):
    big, rep = P("rows", "tm", None), P()
    return jax.shard_map(
        local,
        mesh=mesh,
        in_specs=(big, P("rows", None)) + (rep,) * 8 + (big,),
        out_specs=(big, big) + (rep,) * 8,
        check_vma=False,
    )
```
